256 devices in a mesh: seq: 128 (over z, x, y), head: 2 (over core).
Axes of the slice: x: 4, y: 4, z: 8, core: 2. Of those that a mesh axis runs over, the one named last changes fastest.
Arguments:
- queries: bfloat16 [16384, 4096], P('seq', 'head'), may hold values from -8 to 8
- keys: bfloat16 [16384, 4096], P('seq', 'head'), may hold values from -8 to 8
- values: bfloat16 [16384, 4096], P('seq', 'head'), may hold values from -6 to 6
- out_grad: bfloat16 [16384, 4096], P('seq', 'head'), may hold values from -6 to 6
- cluster_ids: int32 [16384, 32], P('seq', 'head'), may hold values from 0 to 127, as said below
Outputs:
- attended: bfloat16 [16384, 4096], P('seq', 'head')
- grad_queries: bfloat16 [16384, 4096], P('seq', 'head')
- grad_keys: bfloat16 [16384, 4096], P('seq', 'head')
- grad_values: bfloat16 [16384, 4096], P('seq', 'head')
The draws below stay inside these ranges and needn't reach their ends.
Inputs may be any that keep to these rules, and one draw needn't show every extreme that they name: `cluster_ids`: for each head the ids form 8 ranges of 16 consecutive ids, each used by exactly 2048 tokens; the tokens of one index of seq in one range number at most 24, reached in every head, and the counts of every index of seq over a head's ranges are the same numbers in some order.
All inputs are finite; a program needn't handle non-finite values.
Results may differ from the reference program's by a relative error of at most 0.012.
The reference program's roundings to bfloat16 on the way (of `weights_low` and `grad_scores`) count: a program that leaves them out, or rounds other values in their place, can miss the bound.
Values may be sent and summed in bfloat16 or wider, within the bound.
No kernel may reach another device: no remote copies, remote signals or barrier semaphores. Data moves between devices by JAX's collectives and lax.ppermute only.
A program may use at most 64 MiB of HBM per device.

```python
import math
import jax
import jax.numpy as jnp
from jax import lax

HEADS = 32
HEAD_DIM = 128
TOK_DEV = 128
SPAN = 256
CLUSTER_GROUP = 16
TOKENS = 16384
OWNERS = 8


def draw_query_like(key):
    values_out = jnp.clip(jax.random.normal(key, (TOKENS, HEADS, HEAD_DIM), jnp.float32), -4.0, 4.0)
    return values_out.reshape(TOKENS, HEADS * HEAD_DIM).astype(jnp.bfloat16)


def draw_queries(key, part):
    key = jax.random.fold_in(key, 11)
    return draw_query_like(key)


def draw_keys(key, part):
    key = jax.random.fold_in(key, 12)
    return draw_query_like(key)


def draw_cluster_ids(key, part):
    key = jax.random.fold_in(key, 5)
    key_split = jax.random.split(key, 5)
    groups = TOKENS // TOK_DEV
    per_owner = TOK_DEV // OWNERS
    if OWNERS > 1:
        half_share = per_owner // 2
        spread = jax.random.randint(key_split[0], (HEADS, OWNERS // 2), 0, half_share + 1)
        spread = spread.at[:, 0].set(half_share)
        shares = jnp.concatenate([per_owner + spread, per_owner - spread], axis=1)
        shares = jax.vmap(lambda head_key, row_shares: jax.random.permutation(head_key, row_shares))(jax.random.split(key_split[1], HEADS), shares)
        offsets = jax.vmap(lambda head_key: jax.random.permutation(head_key, groups) % OWNERS)(jax.random.split(key_split[2], HEADS))
        pick_index = (jnp.arange(OWNERS)[None, None, :] + offsets[:, :, None]) % OWNERS
        counts = jnp.take_along_axis(jnp.broadcast_to(shares[:, None, :], (HEADS, groups, OWNERS)), pick_index, axis=2)
    else:
        counts = jnp.full((HEADS, groups, 1), TOK_DEV, jnp.int32)
    ends = jnp.cumsum(counts, axis=-1)
    places = jnp.arange(TOK_DEV)
    labels = jnp.sum((places[None, None, :, None] >= ends[:, :, None, :]).astype(jnp.int32), axis=-1)
    flat_labels = labels.reshape(HEADS * groups, TOK_DEV)
    shuffles = jax.vmap(lambda row_key: jax.random.permutation(row_key, TOK_DEV))(jax.random.split(key_split[3], HEADS * groups))
    flat_labels = jnp.take_along_axis(flat_labels, shuffles, axis=1)
    labels = flat_labels.reshape(HEADS, groups, TOK_DEV)
    within = jax.random.randint(key_split[4], (HEADS, groups, TOK_DEV), 0, CLUSTER_GROUP)
    cluster = labels * CLUSTER_GROUP + within
    return cluster.transpose(1, 2, 0).reshape(TOKENS, HEADS).astype(jnp.int32)


def level_of(own_key, extent, shards, low, high):
    def one(dim, shards_of):
        draws = jax.random.uniform(jax.random.fold_in(jax.random.fold_in(own_key, 6), dim), (shards_of,), jnp.float32, low / len(shards), high / len(shards))
        return jnp.repeat(jnp.exp(draws), extent[dim] // shards_of).reshape((-1,) + (1,) * (len(extent) - dim - 1))

    gain = one(*shards[0])
    for cut in shards[1:]:
        gain = gain * one(*cut)
    return gain


def centred(rng, extent, scale, most, shards=(), kind=jnp.bfloat16):
    entries = jax.random.normal(rng, extent, jnp.float32) * scale
    if len(shards) > 0:
        entries = level_of(rng, extent, shards, -0.22, 0.18) * entries
    return jnp.clip(entries, min=-most, max=most).astype(kind)


def setup_inputs(seed: int = 0) -> dict:
    splits = jax.random.split(jax.random.key(seed), 6)
    queries = draw_queries(jax.random.fold_in(splits[5], 71), 0)
    keys = draw_keys(jax.random.fold_in(splits[5], 71), 0)
    values = centred(splits[2], (TOKENS, HEADS * HEAD_DIM), 1.0, 6.0, ((0, 128), (1, 2)))
    out_grad = centred(splits[3], (TOKENS, HEADS * HEAD_DIM), 1.0, 6.0, ((0, 128), (1, 2)))
    cluster_ids = draw_cluster_ids(jax.random.fold_in(splits[5], 71), 0)
    return dict(queries=queries, keys=keys, values=values, out_grad=out_grad, cluster_ids=cluster_ids)


def attend(sorted_q, key_pairs, value_pairs, grad_sorted, keep_mask):
    scaling = 1.0 / math.sqrt(HEAD_DIM)
    highest = lax.Precision.HIGHEST
    scores = jnp.einsum('cqd,ckd->cqk', sorted_q.astype(jnp.float32), key_pairs.astype(jnp.float32), precision=highest) * scaling
    scores = jnp.where(keep_mask, scores, -1e+30)
    row_peak = lax.optimization_barrier(jnp.max(scores, axis=-1, keepdims=True))
    raw_weights = jnp.exp(scores - row_peak)
    weights = raw_weights / lax.optimization_barrier(jnp.sum(raw_weights, axis=-1, keepdims=True))
    weights_low = weights.astype(jnp.bfloat16)
    attended = jnp.einsum('cqk,ckd->cqd', weights_low.astype(jnp.float32), value_pairs.astype(jnp.float32), precision=highest).astype(jnp.bfloat16)
    grad_weights = jnp.einsum('cqd,ckd->cqk', grad_sorted.astype(jnp.float32), value_pairs.astype(jnp.float32), precision=highest)
    inner_sum = lax.optimization_barrier(jnp.sum(weights * grad_weights, axis=-1, keepdims=True))
    grad_scores = (weights * (grad_weights - inner_sum) * scaling).astype(jnp.bfloat16)
    grad_query = jnp.einsum('cqk,ckd->cqd', grad_scores.astype(jnp.float32), key_pairs.astype(jnp.float32), precision=highest).astype(jnp.bfloat16)
    grad_kpairs = jnp.einsum('cqk,cqd->ckd', grad_scores.astype(jnp.float32), sorted_q.astype(jnp.float32), precision=highest)
    grad_vpairs = jnp.einsum('cqk,cqd->ckd', weights_low.astype(jnp.float32), grad_sorted.astype(jnp.float32), precision=highest)
    return (attended, grad_query, grad_kpairs, grad_vpairs)

def fold_pairs(grad_pairs):
    zero_rows = jnp.zeros((1, SPAN, HEAD_DIM), jnp.float32)
    later_part = jnp.concatenate([grad_pairs[1:, :SPAN], zero_rows], axis=0)
    return (grad_pairs[:, SPAN:] + later_part).astype(jnp.bfloat16)

def one_head(head_item):
    query_head, key_head, value_head, grad_head, id_head = head_item
    order = jnp.argsort(id_head, stable=True).astype(jnp.int32)
    span_count = TOKENS // SPAN

    def take_rows(array):
        return array[order].reshape(span_count, SPAN, HEAD_DIM)
    sorted_q = take_rows(query_head)
    sorted_k = take_rows(key_head)
    sorted_v = take_rows(value_head)
    grad_sorted = take_rows(grad_head)
    zero_span = jnp.zeros((1, SPAN, HEAD_DIM), jnp.bfloat16)
    key_pairs = jnp.concatenate([jnp.concatenate([zero_span, sorted_k[:-1]], axis=0), sorted_k], axis=1)
    value_pairs = jnp.concatenate([jnp.concatenate([zero_span, sorted_v[:-1]], axis=0), sorted_v], axis=1)
    keep_prev = jnp.arange(span_count) > 0
    keep_mask = jnp.concatenate([jnp.broadcast_to(keep_prev[:, None, None], (span_count, 1, SPAN)), jnp.ones((span_count, 1, SPAN), bool)], axis=2)
    attended, grad_query, grad_kpairs, grad_vpairs = attend(sorted_q, key_pairs, value_pairs, grad_sorted, keep_mask)

    def put_back(array):
        return jnp.zeros((TOKENS, HEAD_DIM), jnp.bfloat16).at[order].set(array.reshape(TOKENS, HEAD_DIM))
    return (put_back(attended), put_back(grad_query), put_back(fold_pairs(grad_kpairs)), put_back(fold_pairs(grad_vpairs)))

def reference(queries, keys, values, out_grad, cluster_ids):

    def split_heads(array):
        return array.reshape(TOKENS, HEADS, HEAD_DIM).transpose(1, 0, 2)
    results = lax.map(one_head, (split_heads(queries), split_heads(keys), split_heads(values), split_heads(out_grad), cluster_ids.T))

    def join_heads(array):
        return array.transpose(1, 0, 2).reshape(TOKENS, HEADS * HEAD_DIM)
    return (join_heads(results[0]), join_heads(results[1]), join_heads(results[2]), join_heads(results[3]))
```

```python
import functools
import math

import jax
import jax.numpy as jnp
from jax import lax
from jax.experimental import pallas as pl
from jax.experimental.pallas import tpu as pltpu
from jax.sharding import PartitionSpec as P

WIDTH = 128
SPAN = 256
CLUSTER_GROUP = 16
RANGES = 8
TOK = 128
MOST = 24
ZN = 8
PLANE = 16
HPZ = 2
CAP = ZN * MOST
ROWS = ZN * TOK
PACKED = RANGES * CAP
SLOTS = PLANE * CAP
BLOCK = 2048
SPANS = BLOCK // SPAN
SCALING = 1.0 / math.sqrt(WIDTH)
BF = jnp.bfloat16
F32 = jnp.float32
I32 = jnp.int32

PLANES = [[z * PLANE + i for i in range(PLANE)] for z in range(ZN)]


def z_pairs(step):
    return [
        (z * PLANE + i, ((z + step) % ZN) * PLANE + i)
        for z in range(ZN)
        for i in range(PLANE)
    ]


def vmem():
    return pl.BlockSpec(memory_space=pltpu.VMEM)


def smem():
    return pl.BlockSpec(memory_space=pltpu.SMEM)


def call(kernel, ins, outs, scratch=(), flops=0, smem_first=False, limit=40):
    specs = [vmem() for _ in ins]
    if smem_first:
        specs[0] = smem()
    size = sum(math.prod(o.shape) * o.dtype.itemsize for o in outs)
    size += sum(math.prod(a.shape) * a.dtype.itemsize for a in ins)
    return pl.pallas_call(
        kernel,
        out_shape=tuple(outs),
        in_specs=specs,
        out_specs=tuple(vmem() for _ in outs),
        scratch_shapes=list(scratch),
        cost_estimate=pl.CostEstimate(flops=flops, bytes_accessed=size, transcendentals=0),
        compiler_params=pltpu.CompilerParams(vmem_limit_bytes=limit * 1024 * 1024),
    )(*ins)


def out(shape, dtype):
    return jax.ShapeDtypeStruct(shape, dtype)


def iota(shape, dim):
    return lax.broadcasted_iota(I32, shape, dim)


def row_to_col(row):
    eye = iota((128, 128), 0) == iota((128, 128), 1)
    parts = []
    for i in range(row.shape[1] // 128):
        piece = row[:, i * 128 : (i + 1) * 128]
        parts.append(jnp.sum(jnp.where(eye, piece, 0.0), axis=1, keepdims=True))
    return jnp.concatenate(parts, axis=0)


def dot(a, b, dims=((1,), (0,))):
    return lax.dot_general(a, b, (dims, ((), ())), preferred_element_type=F32)


def meta_kernel(place_ref, *refs):
    id_refs, (dst_ref, key_ref) = refs[:ZN], refs[ZN:]
    z = place_ref[0]
    plane = place_ref[1]
    tri = (iota((ROWS, ROWS), 0) < iota((ROWS, ROWS), 1)).astype(F32).astype(BF)
    lane = iota((1, ROWS), 1)
    source = (z - lane // TOK) & (ZN - 1)
    token = lane & (TOK - 1)
    for hh in range(HPZ):
        ids = jnp.concatenate([r[hh : hh + 1, :] for r in id_refs], axis=1)
        group = ids // CLUSTER_GROUP
        hot = iota((RANGES, ROWS), 0) == group
        before = dot(hot.astype(F32).astype(BF), tri)
        slot = jnp.sum(jnp.where(hot, before, 0.0), axis=0, keepdims=True)
        dst = group * CAP + slot.astype(I32)
        dst_ref[hh : hh + 1, :] = dst
        facts = jnp.concatenate(
            [ids - group * CLUSTER_GROUP + 1, source, token, jnp.zeros((13, ROWS), I32)], axis=0
        ).astype(F32).astype(BF)
        for b in range(RANGES):
            pick = (dst == iota((CAP, ROWS), 0) + b * CAP).astype(F32).astype(BF)
            got = dot(facts, pick, ((1,), (1,))).astype(I32)
            key_ref[hh * RANGES + b, 0:1, :] = got[0:1] - 1
            key_ref[hh * RANGES + b, 1:2, :] = (
                got[1:2] * (PLANE * TOK) + plane * TOK + got[2:3]
            )


def rank_kernel(key_ref, rank_ref):
    cluster = key_ref[0:1, :]
    token = key_ref[1:2, :]
    key = jnp.where(cluster < 0, 1 << 20, cluster * (ZN * PLANE * TOK) + token).astype(F32)
    acc = jnp.zeros((8, SLOTS), F32)
    for j in range(SLOTS // 128):
        col = row_to_col(key[:, j * 128 : (j + 1) * 128])
        less = (col < key).astype(F32)
        acc = acc + jnp.sum(less.reshape(16, 8, SLOTS), axis=0)
    rank_ref[...] = jnp.sum(acc, axis=0, keepdims=True).astype(I32)


def pack_kernel(n, dst_ref, *refs):
    blocks, (send_ref, x_ref) = refs[:ZN], refs[ZN:]
    for hh in range(HPZ):
        cols = slice(hh * WIDTH, (hh + 1) * WIDTH)
        for d in range(ZN):
            for t in range(n):
                x_ref[d * TOK : (d + 1) * TOK, t * WIDTH : (t + 1) * WIDTH] = blocks[d][t, :, cols]
        dst = dst_ref[hh : hh + 1, :]
        x = x_ref[...]
        for b in range(RANGES):
            pick = (dst == iota((CAP, ROWS), 0) + b * CAP).astype(F32).astype(BF)
            got = dot(pick, x).astype(BF)
            for t in range(n):
                send_ref[hh * RANGES + b, t] = got[:, t * WIDTH : (t + 1) * WIDTH]


def place_kernel(n, rank_ref, recv_ref, sorted_ref, x_ref):
    for s in range(PLANE):
        for t in range(n):
            x_ref[s * CAP : (s + 1) * CAP, t * WIDTH : (t + 1) * WIDTH] = recv_ref[s, t]
    rank = rank_ref[...]
    x = x_ref[...]
    for c in range(SPANS):
        pick = (rank == iota((SPAN, SLOTS), 0) + c * SPAN).astype(F32).astype(BF)
        got = dot(pick, x).astype(BF)
        for t in range(n):
            sorted_ref[t, c] = got[:, t * WIDTH : (t + 1) * WIDTH]


def span_math(q, g, k0, k1, v0, v1, keep):
    s0 = dot(q, k0, ((1,), (1,)))
    s1 = dot(q, k1, ((1,), (1,)))
    if keep is not None:
        s0 = jnp.where(keep, s0, -1e30)
    peak = jnp.maximum(
        jnp.max(s0, axis=1, keepdims=True), jnp.max(s1, axis=1, keepdims=True)
    )
    factor = SCALING * math.log2(math.e)
    p0 = jnp.exp2((s0 - peak) * factor)
    p1 = jnp.exp2((s1 - peak) * factor)
    inverse = 1.0 / (
        jnp.sum(p0, axis=1, keepdims=True) + jnp.sum(p1, axis=1, keepdims=True)
    )
    w0 = p0 * inverse
    w1 = p1 * inverse
    l0 = w0.astype(BF)
    l1 = w1.astype(BF)
    attended = (dot(l0, v0) + dot(l1, v1)).astype(BF)
    e0 = dot(g, v0, ((1,), (1,)))
    e1 = dot(g, v1, ((1,), (1,)))
    inner = jnp.sum(w0 * e0, axis=1, keepdims=True) + jnp.sum(w1 * e1, axis=1, keepdims=True)
    h0 = (w0 * (e0 - inner) * SCALING).astype(BF)
    h1 = (w1 * (e1 - inner) * SCALING).astype(BF)
    dq = (dot(h0, k0) + dot(h1, k1)).astype(BF)
    tn = ((0,), (0,))
    return attended, dq, dot(h0, q, tn), dot(h1, q, tn), dot(l0, g, tn), dot(l1, g, tn)


def main_kernel(qk_ref, vg_ref, att_ref, dq_ref, dk_ref, dv_ref):
    dk_ref[0] = jnp.zeros((SPAN, WIDTH), F32)
    dv_ref[0] = jnp.zeros((SPAN, WIDTH), F32)

    def one(c, carry):
        att, dq, dk0, dk1, dv0, dv1 = span_math(
            qk_ref[0, c], vg_ref[1, c], qk_ref[1, c - 1], qk_ref[1, c],
            vg_ref[0, c - 1], vg_ref[0, c], None,
        )
        att_ref[c] = att
        dq_ref[c] = dq
        dk_ref[c - 1] += dk0
        dk_ref[c] = dk1
        dv_ref[c - 1] += dv0
        dv_ref[c] = dv1
        return carry

    lax.fori_loop(1, SPANS, one, 0)


def edge_kernel(place_ref, qk_ref, vg_ref, hk_ref, hv_ref, att_ref, dq_ref, dk_ref, dv_ref, halo_ref):
    keep = jnp.broadcast_to(place_ref[2], (SPAN, SPAN)) > 0
    att, dq, dk0, dk1, dv0, dv1 = span_math(
        qk_ref[0], vg_ref[1], hk_ref[...], qk_ref[1], hv_ref[...], vg_ref[0], keep
    )
    att_ref[...] = att
    dq_ref[...] = dq
    dk_ref[...] = dk1
    dv_ref[...] = dv1
    halo_ref[0] = dk0.astype(BF)
    halo_ref[1] = dv0.astype(BF)


def pick_out(rank_ref, o_ref, send_ref, col_ref):
    col_ref[...] = row_to_col(rank_ref[...].astype(F32)).astype(I32)
    o = o_ref[...]
    for s in range(PLANE):
        col = col_ref[s * CAP : (s + 1) * CAP, :]
        pick = (col == iota((CAP, BLOCK), 1)).astype(F32).astype(BF)
        got = dot(pick, o).astype(BF)
        for t in range(2):
            send_ref[s, t] = got[:, t * WIDTH : (t + 1) * WIDTH]


def pick_first_kernel(rank_ref, att_ref, dq_ref, att0_ref, dq0_ref, send_ref, o_ref, col_ref):
    o_ref[0:SPAN, 0:WIDTH] = att0_ref[...]
    o_ref[0:SPAN, WIDTH:] = dq0_ref[...]
    for c in range(1, SPANS):
        rows = slice(c * SPAN, (c + 1) * SPAN)
        o_ref[rows, 0:WIDTH] = att_ref[c]
        o_ref[rows, WIDTH:] = dq_ref[c]
    pick_out(rank_ref, o_ref, send_ref, col_ref)


def pick_second_kernel(
    rank_ref, dk_ref, dv_ref, dk0_ref, dv0_ref, halo_ref, send_ref, o_ref, col_ref
):
    for i, (d_ref, d0_ref) in enumerate(((dk_ref, dk0_ref), (dv_ref, dv0_ref))):
        cols = slice(i * WIDTH, (i + 1) * WIDTH)
        for c in range(SPANS):
            piece = d_ref[c]
            if c == 0:
                piece = piece + d0_ref[...]
            if c == SPANS - 1:
                piece = piece + halo_ref[i].astype(F32)
            o_ref[c * SPAN : (c + 1) * SPAN, cols] = piece.astype(BF)
    pick_out(rank_ref, o_ref, send_ref, col_ref)


def unpack_kernel(n, dst_ref, recv_ref, *refs):
    blocks, x_ref = refs[:ZN], refs[ZN]
    for hh in range(HPZ):
        cols = slice(hh * WIDTH, (hh + 1) * WIDTH)
        for b in range(RANGES):
            for t in range(n):
                x_ref[b * CAP : (b + 1) * CAP, t * WIDTH : (t + 1) * WIDTH] = recv_ref[
                    hh * RANGES + b, t
                ]
        x = x_ref[...]
        dst = dst_ref[hh : hh + 1, :].astype(F32)
        for d in range(ZN):
            col = row_to_col(dst[:, d * TOK : (d + 1) * TOK]).astype(I32)
            pick = (col == iota((TOK, PACKED), 1)).astype(F32).astype(BF)
            got = dot(pick, x).astype(BF)
            for t in range(n):
                blocks[d][t, :, cols] = got[:, t * WIDTH : (t + 1) * WIDTH]


def join_kernel(n, place_ref, *refs):
    blocks, outs = refs[:ZN], refs[ZN:]
    z = place_ref[0]
    for d in range(ZN):
        cols = pl.ds(pl.multiple_of(((z + d) & (ZN - 1)) * (HPZ * WIDTH), HPZ * WIDTH), HPZ * WIDTH)
        for t in range(n):
            outs[t][:, cols] = blocks[d][t]


def to_z(arrays, z):
    blocks = []
    for d in range(ZN):
        start = ((z + d) % ZN) * (HPZ * WIDTH)
        blocks.append(
            jnp.stack([lax.dynamic_slice_in_dim(a, start, HPZ * WIDTH, 1) for a in arrays])
        )
    return [blocks[0]] + [
        lax.ppermute(blocks[d], "seq", z_pairs(d)) for d in range(1, ZN)
    ]


def plane_exchange(array):
    return lax.all_to_all(
        array, "seq", split_axis=0, concat_axis=0, axis_index_groups=PLANES, tiled=True
    )


def shift_owner(value, by):
    pairs = []
    for base in range(0, ZN * PLANE, RANGES):
        pairs += [(base + i, base + i + by) for i in range(RANGES) if 0 <= i + by < RANGES]
    return lax.ppermute(value, "seq", pairs)


def body(queries, keys, values, out_grad, cluster_ids):
    index = lax.axis_index("seq")
    z = index // PLANE
    plane = index % PLANE
    place = jnp.stack([z, plane, (index % RANGES != 0).astype(I32)]).astype(I32)
    id_rows = cluster_ids.T
    id_blocks = []
    for d in range(ZN):
        piece = lax.dynamic_slice_in_dim(id_rows, ((z + d) % ZN) * HPZ, HPZ, 0)
        id_blocks.append(piece if d == 0 else lax.ppermute(piece, "seq", z_pairs(d)))
    first = to_z([queries, keys], z)
    second = to_z([values, out_grad], z)
    dst, key_send = call(
        meta_kernel,
        [place] + id_blocks,
        [out((HPZ, ROWS), I32), out((PLANE, 2, CAP), I32)],
        smem_first=True,
        flops=10**8,
    )
    key_got = plane_exchange(key_send).transpose(1, 0, 2).reshape(2, SLOTS)
    (rank,) = call(rank_kernel, [key_got], [out((1, SLOTS), I32)], flops=10**7)

    def to_owner(blocks):
        (send,) = call(
            functools.partial(pack_kernel, 2),
            [dst] + blocks,
            [out((PLANE, 2, CAP, WIDTH), BF)],
            [pltpu.VMEM((ROWS, 2 * WIDTH), BF)],
            flops=HPZ * 2 * PACKED * ROWS * 2 * WIDTH,
        )
        got = plane_exchange(send)
        (placed,) = call(
            functools.partial(place_kernel, 2),
            [rank, got],
            [out((2, SPANS, SPAN, WIDTH), BF)],
            [pltpu.VMEM((SLOTS, 2 * WIDTH), BF)],
            flops=2 * BLOCK * SLOTS * 2 * WIDTH,
        )
        return placed

    qk = to_owner(first)
    halo_k = shift_owner(qk[1, SPANS - 1], 1)
    vg = to_owner(second)
    halo_v = shift_owner(vg[0, SPANS - 1], 1)
    att, dq, dk, dv = call(
        main_kernel,
        [qk, vg],
        [out((SPANS, SPAN, WIDTH), BF)] * 2 + [out((SPANS, SPAN, WIDTH), F32)] * 2,
        flops=14 * SPANS * SPAN * 2 * SPAN * WIDTH,
    )
    att0, dq0, dk0, dv0, halo_out = call(
        edge_kernel,
        [place, qk[:, 0], vg[:, 0], halo_k, halo_v],
        [out((SPAN, WIDTH), BF)] * 2
        + [out((SPAN, WIDTH), F32)] * 2
        + [out((2, SPAN, WIDTH), BF)],
        smem_first=True,
        flops=14 * SPAN * 2 * SPAN * WIDTH,
    )
    halo_in = shift_owner(halo_out, -1)
    scratch = [pltpu.VMEM((BLOCK, 2 * WIDTH), BF), pltpu.VMEM((SLOTS, 1), I32)]

    def to_tokens(send):
        got = plane_exchange(send)
        blocks = call(
            functools.partial(unpack_kernel, 2),
            [dst, got],
            [out((2, TOK, HPZ * WIDTH), BF)] * ZN,
            [pltpu.VMEM((PACKED, 2 * WIDTH), BF)],
            flops=HPZ * 2 * PACKED * ROWS * 2 * WIDTH,
        )
        back = [blocks[0]] + [
            lax.ppermute(blocks[d], "seq", z_pairs(-d)) for d in range(1, ZN)
        ]
        return call(
            functools.partial(join_kernel, 2),
            [place] + back,
            [out((TOK, ZN * HPZ * WIDTH), BF)] * 2,
            smem_first=True,
        )

    send_shape = [out((PLANE, 2, CAP, WIDTH), BF)]
    (send_a,) = call(
        pick_first_kernel, [rank, att, dq, att0, dq0], send_shape, scratch,
        flops=2 * BLOCK * SLOTS * 2 * WIDTH,
    )
    (send_b,) = call(
        pick_second_kernel, [rank, dk, dv, dk0, dv0, halo_in], send_shape, scratch,
        flops=2 * BLOCK * SLOTS * 2 * WIDTH,
    )
    attended, grad_queries = to_tokens(send_a)
    grad_keys, grad_values = to_tokens(send_b)
    return attended, grad_queries, grad_keys, grad_values


def solution(mesh):
    spec = P("seq", "head")
    return jax.shard_map(
        body,
        mesh=mesh,
        in_specs=(spec,) * 5,
        out_specs=(spec,) * 4,
        check_vma=False,
    )
```

```python
import functools
import math

import jax
import jax.numpy as jnp
from jax import lax
from jax.experimental import pallas as pl
from jax.experimental.pallas import tpu as pltpu
from jax.sharding import PartitionSpec as P

WIDTH = 128
SPAN = 256
CLUSTER_GROUP = 16
RANGES = 8
TOK = 128
MOST = 24
ZN = 8
PLANE = 16
HPZ = 2
ALL = 4 * WIDTH
PAIR = HPZ * WIDTH
STRIDE = 32
BLOCK = 2048
SPANS = BLOCK // SPAN
TILE = 16
NONE = 4095
SCALING = 1.0 / math.sqrt(WIDTH)
BF = jnp.bfloat16
F32 = jnp.float32
I32 = jnp.int32

CHUNKS = ((0, 1, 7, 4), (2, 6, 3, 5))
PLANES = [[z * PLANE + i for i in range(PLANE)] for z in range(ZN)]
LINES = [[z * PLANE + i for z in range(ZN)] for i in range(PLANE)]


def z_pairs(step):
    return [
        (z * PLANE + i, ((z + step) % ZN) * PLANE + i)
        for z in range(ZN)
        for i in range(PLANE)
    ]


def whole():
    return pl.BlockSpec(memory_space=pltpu.VMEM)


def call(kernel, ins, outs, scratch=(), flops=0, specs=None, grid=()):
    size = sum(math.prod(o.shape) * o.dtype.itemsize for o in outs)
    size += sum(math.prod(a.shape) * a.dtype.itemsize for a in ins)
    specs = specs or {}
    return pl.pallas_call(
        kernel,
        out_shape=tuple(outs),
        grid=grid,
        in_specs=[specs.get(i) or whole() for i in range(len(ins))],
        out_specs=tuple(whole() for _ in outs),
        scratch_shapes=list(scratch),
        cost_estimate=pl.CostEstimate(flops=flops, bytes_accessed=size, transcendentals=0),
        compiler_params=pltpu.CompilerParams(vmem_limit_bytes=48 * 1024 * 1024),
    )(*ins)


SMEM = {0: pl.BlockSpec(memory_space=pltpu.SMEM)}


def out(shape, dtype):
    return jax.ShapeDtypeStruct(shape, dtype)


def iota(shape, dim):
    return lax.broadcasted_iota(I32, shape, dim)


def one_hot(mask):
    return mask.astype(F32).astype(BF)


def row_to_col(row):
    eye = iota((128, 128), 0) == iota((128, 128), 1)
    parts = []
    for i in range(row.shape[1] // 128):
        piece = row[:, i * 128 : (i + 1) * 128]
        parts.append(jnp.sum(jnp.where(eye, piece, 0.0), axis=1, keepdims=True))
    return jnp.concatenate(parts, axis=0)


def dot(a, b, dims=((1,), (0,))):
    return lax.dot_general(a, b, (dims, ((), ())), preferred_element_type=F32)


NT = ((1,), (1,))
TN = ((0,), (0,))


def prep_kernel(place_ref, *refs):
    arrays, blocks = refs[:4], refs[4:]
    z = place_ref[0]
    for d in range(ZN):
        cols = pl.ds(pl.multiple_of(((z + d) & (ZN - 1)) * PAIR, PAIR), PAIR)
        for t in range(4):
            blocks[d][t * TOK : (t + 1) * TOK, :] = arrays[t][:, cols]


def meta_kernel(ids_ref, code_ref, tile_ref):
    tri = one_hot(iota((TOK, TOK), 0) < iota((TOK, TOK), 1))
    for hh in range(HPZ):
        ids = ids_ref[:, hh, :]
        group = lax.shift_right_logical(ids, 4)
        local = (ids & (CLUSTER_GROUP - 1)) + 1
        slot = jnp.zeros((ZN, TOK), F32)
        for b in range(RANGES):
            hot = (group == b).astype(F32)
            slot = slot + hot * dot(hot.astype(BF), tri)
        code = group * STRIDE + slot.astype(I32)
        code_ref[hh] = code
        rows = []
        for i in range(ZN):
            pick = one_hot(iota((RANGES * STRIDE, TOK), 0) == code[i : i + 1, :])
            value = jnp.broadcast_to(local[i : i + 1, :], (TILE, TOK)).astype(F32).astype(BF)
            rows.append(dot(value, pick, NT)[0:1, :])
        rows.append(jnp.zeros((TILE - ZN, RANGES * STRIDE), F32))
        tile_ref[hh, :, 0 : RANGES * STRIDE] = jnp.concatenate(rows, axis=0).astype(BF)
        tile_ref[hh, :, RANGES * STRIDE :] = jnp.zeros((TILE, ALL - RANGES * STRIDE), BF)


def pack_kernel(chunk, with_tile, place_ref, code_ref, *refs):
    n = len(chunk)
    blocks, rest = refs[:n], refs[n:]
    tile_ref = rest[0] if with_tile else None
    send_ref, x_ref = rest[-2:]
    z = place_ref[0]
    rows = n * MOST
    for hh in range(HPZ):
        codes = []
        for i, d in enumerate(chunk):
            for t in range(4):
                x_ref[i * TOK : (i + 1) * TOK, t * WIDTH : (t + 1) * WIDTH] = blocks[i][
                    t * TOK : (t + 1) * TOK, hh * WIDTH : (hh + 1) * WIDTH
                ]
            codes.append(code_ref[hh, pl.ds((z - d) & (ZN - 1), 1), :] + i * MOST * RANGES * STRIDE)
        code = jnp.concatenate(codes, axis=1)
        group = lax.shift_right_logical(code, 5) & (RANGES - 1)
        position = (code & (STRIDE - 1)) + lax.shift_right_logical(code, 8)
        x = x_ref[...]
        for b in range(RANGES):
            target = jnp.where(group == b, position, -1)
            pick = one_hot(target == iota((rows, n * TOK), 0))
            send_ref[hh * RANGES + b, 0:rows, :] = dot(pick, x).astype(BF)
            if with_tile:
                send_ref[hh * RANGES + b, rows : rows + TILE, :] = tile_ref[hh]


def rank_kernel(place_ref, tile_ref, *refs):
    ranks, (high_ref, low_ref) = refs[: len(CHUNKS)], refs[len(CHUNKS) :]
    z = place_ref[0]
    mine = place_ref[2]
    tiles = tile_ref[...].reshape(PLANE * TILE, RANGES * STRIDE)
    lanes = iota((RANGES * STRIDE, 128), 1)
    cut = one_hot((iota((RANGES * STRIDE, 128), 0) == lanes + mine * STRIDE) & (lanes < MOST))
    row = iota((ZN * PLANE, PLANE * TILE), 0)
    col = iota((ZN * PLANE, PLANE * TILE), 1)
    order = one_hot(((col & (TILE - 1)) == lax.shift_right_logical(row, 4)) & (
        lax.shift_right_logical(col, 4) == (row & (PLANE - 1))
    ))
    cluster = dot(order, dot(tiles, cut).astype(BF))
    tri = one_hot(iota((128, 128), 0) < iota((128, 128), 1))
    low_tri = one_hot(iota((128, 128), 0) > iota((128, 128), 1))
    ones = jnp.ones((128, 128), BF)
    base = jnp.zeros((1, 128), F32)
    rank = jnp.zeros((128, 128), F32)
    for c in range(CLUSTER_GROUP):
        hot = (cluster == float(c + 1)).astype(F32)
        low = hot.astype(BF)
        count = dot(low, ones)
        rank = rank + hot * (base + dot(low_tri, count.astype(BF)) + dot(low, tri))
        base = base + jnp.sum(count, axis=0, keepdims=True)
    rank = jnp.where(cluster > 0.5, rank, float(NONE)).astype(I32)
    high_ref[...] = lax.shift_right_logical(rank, 8).astype(F32)
    low_ref[...] = (rank & 255).astype(F32)
    for chunk, rank_ref in zip(CHUNKS, ranks):
        rows = len(chunk) * MOST
        high = jnp.zeros((PLANE, rows), F32)
        low = jnp.zeros((PLANE, rows), F32)
        for i, d in enumerate(chunk):
            at = pl.ds(pl.multiple_of(((z - d) & (ZN - 1)) * PLANE, PLANE), PLANE)
            slot = iota((128, rows), 0)
            spread = one_hot((iota((128, rows), 1) == slot + i * MOST) & (slot < MOST))
            high = high + dot(high_ref[at, :].astype(BF), spread)
            low = low + dot(low_ref[at, :].astype(BF), spread)
        rank_ref[...] = (high * 256.0 + low).astype(I32)


def place_kernel(rows, last, rank_ref, recv_ref, *refs):
    x_ref = refs[-1]
    x_ref[...] = recv_ref[:, 0:rows, :].reshape(PLANE * rows, ALL)
    rank = rank_ref[...]
    x = x_ref[...]
    sorted_ref = refs[1] if last else refs[0]
    step = 2
    for c in range(0, SPANS, step):
        pick = one_hot(rank == iota((step * SPAN, PLANE * rows), 0) + c * SPAN)
        got = dot(pick, x).astype(BF).reshape(step, SPAN, ALL)
        if last:
            got = got + refs[0][c : c + step]
        sorted_ref[c : c + step] = got
    if last:
        refs[2][...] = sorted_ref[SPANS - 1, :, WIDTH : 3 * WIDTH]
        refs[3][...] = sorted_ref[0]


def span_math(q, g, k0, k1, v0, v1, keep):
    s0 = dot(q, k0, NT)
    s1 = dot(q, k1, NT)
    if keep is not None:
        s0 = jnp.where(keep, s0, -1e30)
    peak = jnp.maximum(
        jnp.max(s0, axis=1, keepdims=True), jnp.max(s1, axis=1, keepdims=True)
    )
    factor = SCALING * math.log2(math.e)
    p0 = jnp.exp2((s0 - peak) * factor)
    p1 = jnp.exp2((s1 - peak) * factor)
    inverse = 1.0 / (
        jnp.sum(p0, axis=1, keepdims=True) + jnp.sum(p1, axis=1, keepdims=True)
    )
    w0 = p0 * inverse
    w1 = p1 * inverse
    l0 = w0.astype(BF)
    l1 = w1.astype(BF)
    attended = (dot(l0, v0) + dot(l1, v1)).astype(BF)
    e0 = dot(g, v0, NT)
    e1 = dot(g, v1, NT)
    inner = jnp.sum(w0 * e0, axis=1, keepdims=True) + jnp.sum(w1 * e1, axis=1, keepdims=True)
    h0 = (w0 * (e0 - inner) * SCALING).astype(BF)
    h1 = (w1 * (e1 - inner) * SCALING).astype(BF)
    dq = (dot(h0, k0) + dot(h1, k1)).astype(BF)
    return attended, dq, dot(h0, q, TN), dot(h1, q, TN), dot(l0, g, TN), dot(l1, g, TN)


Q, K, V, G = (slice(t * WIDTH, (t + 1) * WIDTH) for t in range(4))


def main_kernel(in_ref, o_ref, part_ref, d_ref):
    d_ref[0] = jnp.zeros((SPAN, PAIR), F32)

    def one(c, carry):
        att, dq, dk0, dk1, dv0, dv1 = span_math(
            in_ref[c, :, Q], in_ref[c, :, G], in_ref[c - 1, :, K], in_ref[c, :, K],
            in_ref[c - 1, :, V], in_ref[c, :, V], None,
        )
        o_ref[c, :, Q] = att
        o_ref[c, :, K] = dq
        d_ref[c - 1, :, Q] += dk0
        d_ref[c - 1, :, K] += dv0
        d_ref[c, :, Q] = dk1
        d_ref[c, :, K] = dv1
        o_ref[c - 1, :, 2 * WIDTH :] = d_ref[c - 1].astype(BF)
        return carry

    lax.fori_loop(1, SPANS, one, 0)
    part_ref[0] = d_ref[0]
    part_ref[1] = d_ref[SPANS - 1]
    o_ref[0, :, 0 : 2 * WIDTH] = jnp.zeros((SPAN, 2 * WIDTH), BF)
    o_ref[SPANS - 1, :, 2 * WIDTH :] = jnp.zeros((SPAN, 2 * WIDTH), BF)


def pick_out(rank_ref, o, send_ref):
    col = row_to_col(rank_ref[...].astype(F32)).astype(I32)
    rows = send_ref.shape[1]
    step = 8
    for s in range(0, PLANE, step):
        part = col[s * rows : (s + step) * rows, :]
        pick = one_hot(part == iota((step * rows, BLOCK), 1))
        send_ref[s : s + step] = dot(pick, o).astype(BF).reshape(step, rows, ALL)


def edge_kernel(
    place_ref, rank_ref, in_ref, last_ref, tail_ref, head_ref, main_ref, part_ref, o_ref, send_ref
):
    o_ref[SPAN : BLOCK, :] = main_ref[1:].reshape(BLOCK - SPAN, ALL)
    keep = jnp.broadcast_to(place_ref[2], (SPAN, SPAN)) > 0
    att, dq, _, dk1, _, dv1 = span_math(
        in_ref[0, :, Q], in_ref[0, :, G], tail_ref[:, Q], in_ref[0, :, K],
        tail_ref[:, K], in_ref[0, :, V], keep,
    )
    o_ref[0:SPAN, Q] = att
    o_ref[0:SPAN, K] = dq
    o_ref[0:SPAN, V] = (part_ref[0, :, Q] + dk1).astype(BF)
    o_ref[0:SPAN, G] = (part_ref[0, :, K] + dv1).astype(BF)
    _, _, dk0, _, dv0, _ = span_math(
        head_ref[:, Q], head_ref[:, G], last_ref[0, :, K], head_ref[:, K],
        last_ref[0, :, V], head_ref[:, V], None,
    )
    o_ref[BLOCK - SPAN :, V] = (part_ref[1, :, Q] + dk0).astype(BF)
    o_ref[BLOCK - SPAN :, G] = (part_ref[1, :, K] + dv0).astype(BF)
    pick_out(rank_ref, o_ref[...], send_ref)


def pick_kernel(rank_ref, o_ref, send_ref):
    pick_out(rank_ref, o_ref[...], send_ref)


def unpack_kernel(chunk, place_ref, code_ref, recv_ref, *blocks):
    z = place_ref[0]
    n = len(chunk)
    rows = n * MOST
    for hh in range(HPZ):
        cols = []
        for i, d in enumerate(chunk):
            code = code_ref[hh, pl.ds((z - d) & (ZN - 1), 1), :]
            target = lax.shift_right_logical(code, 5) * rows + (code & (STRIDE - 1)) + i * MOST
            cols.append(row_to_col(target.astype(F32)).astype(I32))
        col = jnp.concatenate(cols, axis=0)
        pick = one_hot(col == iota((n * TOK, RANGES * rows), 1))
        x = recv_ref[hh * RANGES : (hh + 1) * RANGES].reshape(RANGES * rows, ALL)
        got = dot(pick, x).astype(BF)
        for i in range(n):
            for t in range(4):
                blocks[i][t * TOK : (t + 1) * TOK, hh * WIDTH : (hh + 1) * WIDTH] = got[
                    i * TOK : (i + 1) * TOK, t * WIDTH : (t + 1) * WIDTH
                ]


def join_kernel(place_ref, *refs):
    blocks, outs = refs[:ZN], refs[ZN:]
    z = place_ref[0]
    for d in range(ZN):
        cols = pl.ds(pl.multiple_of(((z + d) & (ZN - 1)) * PAIR, PAIR), PAIR)
        for t in range(4):
            outs[t][:, cols] = blocks[d][t * TOK : (t + 1) * TOK, :]


def exchange(array, groups):
    return lax.all_to_all(
        array, "seq", split_axis=0, concat_axis=0, axis_index_groups=groups, tiled=True
    )


def shift_owner(value, by):
    pairs = []
    for base in range(0, ZN * PLANE, RANGES):
        pairs += [(base + i, base + i + by) for i in range(RANGES) if 0 <= i + by < RANGES]
    return lax.ppermute(value, "seq", pairs)


def body(queries, keys, values, out_grad, cluster_ids):
    index = lax.axis_index("seq")
    place = jnp.stack([index // PLANE, index % PLANE, index % RANGES]).astype(I32)
    blocks = call(
        prep_kernel,
        [place, queries, keys, values, out_grad],
        [out((4 * TOK, PAIR), BF)] * ZN,
        specs=SMEM,
    )
    moved = {0: blocks[0]}
    for chunk in CHUNKS:
        for d in chunk:
            if d:
                moved[d] = lax.ppermute(blocks[d], "seq", z_pairs(d))
    ids = exchange(cluster_ids.T, LINES).reshape(ZN, HPZ, TOK)
    code, tile = call(
        meta_kernel,
        [ids],
        [out((HPZ, ZN, TOK), I32), out((HPZ, TILE, ALL), BF)],
        flops=10**8,
    )
    ranks = None
    placed = None
    for i, chunk in enumerate(CHUNKS):
        n = len(chunk)
        rows = n * MOST
        first = i == 0
        extra = TILE if first else 0
        (send,) = call(
            functools.partial(pack_kernel, chunk, first),
            [place, code] + [moved[d] for d in chunk] + ([tile] if first else []),
            [out((PLANE, rows + extra, ALL), BF)],
            [pltpu.VMEM((n * TOK, ALL), BF)],
            flops=2 * PLANE * rows * n * TOK * ALL,
            specs=SMEM,
        )
        got = exchange(send, PLANES)
        if first:
            ranks = call(
                rank_kernel,
                [place, got],
                [out((PLANE, len(c) * MOST), I32) for c in CHUNKS],
                [pltpu.VMEM((ZN * PLANE, 128), F32)] * 2,
                flops=10**8,
                specs={
                    0: SMEM[0],
                    1: pl.BlockSpec((PLANE, TILE, RANGES * STRIDE), lambda i: (0, rows // TILE, 0)),
                },
                grid=(1,),
            )
            ranks = [r.reshape(1, -1) for r in ranks]
        last = i == len(CHUNKS) - 1
        outs = [out((SPANS, SPAN, ALL), BF)]
        if last:
            outs += [out((SPAN, PAIR), BF), out((SPAN, ALL), BF)]
        placed = call(
            functools.partial(place_kernel, rows, last),
            [ranks[i], got] + ([placed[0]] if last else []),
            outs,
            [pltpu.VMEM((PLANE * rows, ALL), BF)],
            flops=2 * BLOCK * PLANE * rows * ALL,
        )
    rows_in, tail, head = placed
    tail = shift_owner(tail, 1)
    head = shift_owner(head, -1)
    main, part = call(
        main_kernel,
        [rows_in],
        [out((SPANS, SPAN, ALL), BF), out((2, SPAN, PAIR), F32)],
        [pltpu.VMEM((SPANS, SPAN, PAIR), F32)],
        flops=14 * SPANS * SPAN * 2 * SPAN * WIDTH,
    )
    span_spec = lambda c: pl.BlockSpec((1, SPAN, ALL), lambda i: (c, 0, 0))
    o = None
    back = {}
    for chunk, rank in reversed(list(zip(CHUNKS, ranks))):
        rows = len(chunk) * MOST
        send_shape = out((PLANE, rows, ALL), BF)
        flops = 2 * BLOCK * PLANE * rows * ALL
        if o is None:
            o, send = call(
                edge_kernel,
                [place, rank, rows_in, rows_in, tail, head, main, part],
                [out((BLOCK, ALL), BF), send_shape],
                flops=flops,
                specs={0: SMEM[0], 2: span_spec(0), 3: span_spec(SPANS - 1)},
                grid=(1,),
            )
        else:
            (send,) = call(pick_kernel, [rank, o], [send_shape], flops=flops)
        got = exchange(send, PLANES)
        pieces = call(
            functools.partial(unpack_kernel, chunk),
            [place, code, got],
            [out((4 * TOK, PAIR), BF)] * len(chunk),
            flops=4 * RANGES * rows * len(chunk) * TOK * ALL,
            specs=SMEM,
        )
        for d, piece in zip(chunk, pieces):
            back[d] = lax.ppermute(piece, "seq", z_pairs(-d)) if d else piece
    return call(
        join_kernel,
        [place] + [back[d] for d in range(ZN)],
        [out((TOK, ZN * PAIR), BF)] * 4,
        specs=SMEM,
    )


def solution(mesh):
    spec = P("seq", "head")
    return jax.shard_map(
        body,
        mesh=mesh,
        in_specs=(spec,) * 5,
        out_specs=(spec,) * 4,
        check_vma=False,
    )
```

```python
import functools
import math

import jax
import jax.numpy as jnp
from jax import lax
from jax.experimental import pallas as pl
from jax.experimental.pallas import tpu as pltpu
from jax.sharding import PartitionSpec as P

WIDTH = 128
SPAN = 256
CLUSTER_GROUP = 16
RANGES = 8
TOK = 128
MOST = 24
ZN = 8
PLANE = 16
HPZ = 2
ALL = 4 * WIDTH
PAIR = HPZ * WIDTH
STRIDE = 32
SLOTS = PLANE * ZN * MOST
BLOCK = 2048
SPANS = BLOCK // SPAN
TILE = 16
PICKS = 2
NONE = 4095
SCALING = 1.0 / math.sqrt(WIDTH)
BF = jnp.bfloat16
F32 = jnp.float32
I32 = jnp.int32

CHUNKS = ((0, 1, 7, 4), (2, 6, 3, 5))
PACK_HINT = (10**6, 10**11)
PLANES = [[z * PLANE + i for i in range(PLANE)] for z in range(ZN)]


def z_pairs(step):
    return [
        (z * PLANE + i, ((z + step) % ZN) * PLANE + i)
        for z in range(ZN)
        for i in range(PLANE)
    ]


def whole():
    return pl.BlockSpec(memory_space=pltpu.VMEM)


def call(kernel, ins, outs, scratch=(), flops=0, specs=None, out_specs=None, limit=28):
    size = sum(math.prod(o.shape) * o.dtype.itemsize for o in outs)
    size += sum(math.prod(a.shape) * a.dtype.itemsize for a in ins)
    specs = specs or {}
    return pl.pallas_call(
        kernel,
        out_shape=tuple(
            pltpu.HBM(o.shape, o.dtype) if i in (out_specs or {}) else o
            for i, o in enumerate(outs)
        ),
        in_specs=[specs.get(i) or whole() for i in range(len(ins))],
        out_specs=tuple((out_specs or {}).get(i) or whole() for i in range(len(outs))),
        scratch_shapes=list(scratch),
        cost_estimate=pl.CostEstimate(flops=flops, bytes_accessed=size, transcendentals=0),
        compiler_params=pltpu.CompilerParams(vmem_limit_bytes=limit * 1024 * 1024),
    )(*ins)


SMEM = {0: pl.BlockSpec(memory_space=pltpu.SMEM)}


def out(shape, dtype):
    return jax.ShapeDtypeStruct(shape, dtype)


def iota(shape, dim):
    return lax.broadcasted_iota(I32, shape, dim)


def one_hot(mask):
    return mask.astype(F32).astype(BF)


def row_to_col(row):
    eye = iota((128, 128), 0) == iota((128, 128), 1)
    parts = []
    for i in range(row.shape[1] // 128):
        piece = row[:, i * 128 : (i + 1) * 128]
        parts.append(jnp.sum(jnp.where(eye, piece, 0.0), axis=1, keepdims=True))
    return jnp.concatenate(parts, axis=0)


def dot(a, b, dims=((1,), (0,))):
    return lax.dot_general(a, b, (dims, ((), ())), preferred_element_type=F32)


NT = ((1,), (1,))
TN = ((0,), (0,))


def prep_kernel(place_ref, ids_ref, *refs):
    arrays, blocks, sems = refs[:4], refs[4 : 4 + ZN], refs[4 + ZN]
    z = place_ref[0]
    copies = []
    for d in range(ZN):
        cols = pl.ds(pl.multiple_of(((z + d) & (ZN - 1)) * PAIR, PAIR), PAIR)
        for t in range(4):
            copies.append(
                pltpu.make_async_copy(
                    arrays[t].at[:, cols],
                    blocks[d].at[t * TOK : (t + 1) * TOK, :],
                    sems.at[d * 4 + t],
                )
            )
    for copy in copies:
        copy.start()
    for d in range(ZN):
        at = ((z + d) & (ZN - 1)) * HPZ
        rows = [ids_ref[pl.ds(at + hh, 1), :] for hh in range(HPZ)]
        tile = jnp.concatenate(rows + [jnp.zeros((TILE - HPZ, TOK), I32)], axis=0)
        blocks[d][4 * TOK :, 0:TOK] = tile.astype(F32).astype(BF)
        blocks[d][4 * TOK :, TOK:] = jnp.zeros((TILE, PAIR - TOK), BF)
    for copy in copies:
        copy.wait()


def leave(stage_ref, out_ref, sems, i, n):
    size = PLANE // n
    part = slice(i * size, (i + 1) * size)
    return pltpu.make_async_copy(stage_ref.at[part], out_ref.at[part], sems.at[i])


def pack_kernel(chunk, *refs):
    n = len(chunk)
    blocks, (out_ref, code_ref, x_ref, send_ref, sems) = refs[:n], refs[-5:]
    rows = n * MOST
    ids = [blocks[i][4 * TOK :, 0:TOK].astype(F32) for i in range(n)]
    ids = jnp.concatenate(
        [ids[i][hh : hh + 1] for hh in range(HPZ) for i in range(n)], axis=0
    ).astype(I32)
    group = lax.shift_right_logical(ids, 4)
    local = ((ids & (CLUSTER_GROUP - 1)) + 1).astype(F32).astype(BF)
    tri = one_hot(iota((TOK, TOK), 0) < iota((TOK, TOK), 1))
    slot = jnp.zeros(ids.shape, F32)
    for b in range(RANGES):
        hot = (group == b).astype(F32)
        slot = slot + hot * dot(hot.astype(BF), tri)
    code = group * STRIDE + slot.astype(I32)
    code_ref[...] = code
    for hh in range(HPZ):
        for i in range(n):
            for t in range(4):
                x_ref[i * TOK : (i + 1) * TOK, t * WIDTH : (t + 1) * WIDTH] = blocks[i][
                    t * TOK : (t + 1) * TOK, hh * WIDTH : (hh + 1) * WIDTH
                ]
        mine = range(hh * n, (hh + 1) * n)
        position = jnp.concatenate(
            [(code[i : i + 1] & (STRIDE - 1)) + (i - hh * n) * MOST for i in mine], axis=1
        )
        owner = jnp.concatenate([group[i : i + 1] for i in mine], axis=1)
        value = jnp.concatenate([local[i : i + 1] for i in mine], axis=1)
        value = jnp.broadcast_to(value, (TILE, n * TOK))
        x = x_ref[...]
        for b in range(RANGES):
            target = jnp.where(owner == b, position, -1)
            pick = one_hot(target == iota((rows, n * TOK), 0))
            send_ref[hh * RANGES + b, 0:rows, :] = dot(pick, x).astype(BF)
            send_ref[hh * RANGES + b, rows:, 0:rows] = dot(value, pick, NT).astype(BF)
            send_ref[hh * RANGES + b, rows:, rows:] = jnp.zeros((TILE, ALL - rows), BF)
        leave(send_ref, out_ref, sems, hh, HPZ).start()
    for hh in range(HPZ):
        leave(send_ref, out_ref, sems, hh, HPZ).wait()


def rank_rows(z, clusters):
    lanes = ZN * MOST
    dist = sum(CHUNKS, ())

    def source(shape, dim):
        segment = iota(shape, dim) // MOST
        value = jnp.zeros(shape, I32)
        for i, d in enumerate(dist):
            value = jnp.where(segment == i, (z - d) & (ZN - 1), value)
        return value

    square = (lanes, lanes)
    from_z, to_z = source(square, 0), source(square, 1)
    same = from_z == to_z
    within = one_hot(same & (iota(square, 0) < iota(square, 1)))
    segment = one_hot(same)
    earlier = one_hot(from_z < to_z)
    hot = jnp.concatenate(
        [(clusters == float(c + 1)).astype(F32) for c in range(CLUSTER_GROUP)], axis=0
    )
    low = hot.astype(BF)
    side = CLUSTER_GROUP * PLANE
    row, col = iota((side, side), 0), iota((side, side), 1)
    row_c, col_c = lax.shift_right_logical(row, 4), lax.shift_right_logical(col, 4)
    before = one_hot((row_c == col_c) & (col < row))
    together = one_hot(row_c == col_c)
    lower = one_hot(col_c < row_c)
    total = dot(low, jnp.ones(square, BF))
    rank = (
        dot(low, within)
        + dot(before, dot(low, segment).astype(BF))
        + dot(together, dot(low, earlier).astype(BF))
        + dot(lower, total.astype(BF))
    )
    rank = jnp.sum((hot * rank).reshape(CLUSTER_GROUP, PLANE, lanes), axis=0)
    rank = jnp.where(clusters > 0.5, rank, float(NONE))
    return jnp.concatenate([rank[s : s + 1, :] for s in range(PLANE)], axis=1)


def place_kernel(place_ref, *refs):
    n = len(CHUNKS)
    recvs, (sorted_ref, tail_ref, head_ref, rank_ref, x_ref) = refs[:n], refs[n:]
    clusters = []
    at = 0
    for chunk, recv_ref in zip(CHUNKS, recvs):
        rows = len(chunk) * MOST
        clusters.append(
            jnp.concatenate(
                [recv_ref[s, rows:, 0:rows].astype(F32)[0:1] for s in range(PLANE)], axis=0
            )
        )
        for s in range(PLANE):
            x_ref[s * ZN * MOST + at : s * ZN * MOST + at + rows, :] = recv_ref[s, 0:rows, :]
        at += rows
    rank = rank_rows(place_ref[0], jnp.concatenate(clusters, axis=1)).astype(I32)
    rank_ref[...] = rank
    x = x_ref[...]
    step = 2
    for c in range(0, SPANS, step):
        pick = one_hot(rank == iota((step * SPAN, SLOTS), 0) + c * SPAN)
        sorted_ref[c : c + step] = dot(pick, x).astype(BF).reshape(step, SPAN, ALL)
    tail_ref[...] = sorted_ref[SPANS - 1, :, WIDTH : 3 * WIDTH]
    head_ref[...] = sorted_ref[0]


def span_math(q, g, k0, k1, v0, v1, keep):
    s0 = dot(q, k0, NT)
    s1 = dot(q, k1, NT)
    if keep is not None:
        s0 = jnp.where(keep, s0, -1e30)
    peak = jnp.maximum(
        jnp.max(s0, axis=1, keepdims=True), jnp.max(s1, axis=1, keepdims=True)
    )
    factor = SCALING * math.log2(math.e)
    p0 = jnp.exp2((s0 - peak) * factor)
    p1 = jnp.exp2((s1 - peak) * factor)
    inverse = 1.0 / (
        jnp.sum(p0, axis=1, keepdims=True) + jnp.sum(p1, axis=1, keepdims=True)
    )
    w0 = p0 * inverse
    w1 = p1 * inverse
    l0 = w0.astype(BF)
    l1 = w1.astype(BF)
    attended = (dot(l0, v0) + dot(l1, v1)).astype(BF)
    e0 = dot(g, v0, NT)
    e1 = dot(g, v1, NT)
    inner = jnp.sum(w0 * e0, axis=1, keepdims=True) + jnp.sum(w1 * e1, axis=1, keepdims=True)
    h0 = (w0 * (e0 - inner) * SCALING).astype(BF)
    h1 = (w1 * (e1 - inner) * SCALING).astype(BF)
    dq = (dot(h0, k0) + dot(h1, k1)).astype(BF)
    return attended, dq, dot(h0, q, TN), dot(h1, q, TN), dot(l0, g, TN), dot(l1, g, TN)


Q, K, V, G = (slice(t * WIDTH, (t + 1) * WIDTH) for t in range(4))


def main_kernel(in_ref, o_ref, part_ref, d_ref):
    d_ref[0] = jnp.zeros((SPAN, PAIR), F32)

    def one(c, carry):
        att, dq, dk0, dk1, dv0, dv1 = span_math(
            in_ref[c, :, Q], in_ref[c, :, G], in_ref[c - 1, :, K], in_ref[c, :, K],
            in_ref[c - 1, :, V], in_ref[c, :, V], None,
        )
        o_ref[c, :, Q] = att
        o_ref[c, :, K] = dq
        d_ref[c - 1, :, Q] += dk0
        d_ref[c - 1, :, K] += dv0
        d_ref[c, :, Q] = dk1
        d_ref[c, :, K] = dv1
        o_ref[c - 1, :, 2 * WIDTH :] = d_ref[c - 1].astype(BF)
        return carry

    lax.fori_loop(1, SPANS, one, 0)
    part_ref[0] = d_ref[0]
    part_ref[1] = d_ref[SPANS - 1]
    o_ref[0, :, 0 : 2 * WIDTH] = jnp.zeros((SPAN, 2 * WIDTH), BF)
    o_ref[SPANS - 1, :, 2 * WIDTH :] = jnp.zeros((SPAN, 2 * WIDTH), BF)


def pick_out(at, rank_ref, o, out_ref, send_ref, sems):
    col = row_to_col(rank_ref[...].astype(F32)).astype(I32)
    rows = send_ref.shape[1]
    step = PLANE // PICKS
    for p in range(PICKS):
        span = range(p * step, (p + 1) * step)
        part = jnp.concatenate(
            [col[i * ZN * MOST + at : i * ZN * MOST + at + rows, :] for i in span], axis=0
        )
        pick = one_hot(part == iota((step * rows, BLOCK), 1))
        send_ref[p * step : (p + 1) * step] = dot(pick, o).astype(BF).reshape(step, rows, ALL)
        leave(send_ref, out_ref, sems, p, PICKS).start()
    for p in range(PICKS):
        leave(send_ref, out_ref, sems, p, PICKS).wait()


def edge_kernel(
    at, place_ref, rank_ref, in_ref, tail_ref, head_ref, main_ref, part_ref,
    done_ref, out_ref, o_ref, send_ref, sems, done_sem,
):
    o_ref[SPAN:BLOCK, :] = main_ref[1:].reshape(BLOCK - SPAN, ALL)
    keep = jnp.broadcast_to(place_ref[1], (SPAN, SPAN)) > 0
    att, dq, _, dk1, _, dv1 = span_math(
        in_ref[0, :, Q], in_ref[0, :, G], tail_ref[:, Q], in_ref[0, :, K],
        tail_ref[:, K], in_ref[0, :, V], keep,
    )
    o_ref[0:SPAN, Q] = att
    o_ref[0:SPAN, K] = dq
    o_ref[0:SPAN, V] = (part_ref[0, :, Q] + dk1).astype(BF)
    o_ref[0:SPAN, G] = (part_ref[0, :, K] + dv1).astype(BF)
    end = SPANS - 1
    _, _, dk0, _, dv0, _ = span_math(
        head_ref[:, Q], head_ref[:, G], in_ref[end, :, K], head_ref[:, K],
        in_ref[end, :, V], head_ref[:, V], None,
    )
    o_ref[BLOCK - SPAN :, V] = (part_ref[1, :, Q] + dk0).astype(BF)
    o_ref[BLOCK - SPAN :, G] = (part_ref[1, :, K] + dv0).astype(BF)
    done = pltpu.make_async_copy(o_ref, done_ref, done_sem.at[0])
    done.start()
    pick_out(at, rank_ref, o_ref[...], out_ref, send_ref, sems)
    done.wait()


def pick_kernel(at, rank_ref, o_ref, out_ref, send_ref, sems):
    pick_out(at, rank_ref, o_ref[...], out_ref, send_ref, sems)


def unpack_kernel(chunk, code_ref, recv_ref, *blocks):
    n = len(chunk)
    rows = n * MOST
    code = code_ref[...]
    for hh in range(HPZ):
        cols = []
        for i in range(n):
            mine = code[hh * n + i : hh * n + i + 1]
            target = lax.shift_right_logical(mine, 5) * rows + (mine & (STRIDE - 1)) + i * MOST
            cols.append(row_to_col(target.astype(F32)).astype(I32))
        col = jnp.concatenate(cols, axis=0)
        pick = one_hot(col == iota((n * TOK, RANGES * rows), 1))
        x = recv_ref[hh * RANGES : (hh + 1) * RANGES].reshape(RANGES * rows, ALL)
        got = dot(pick, x).astype(BF)
        for i in range(n):
            for t in range(4):
                blocks[i][t * TOK : (t + 1) * TOK, hh * WIDTH : (hh + 1) * WIDTH] = got[
                    i * TOK : (i + 1) * TOK, t * WIDTH : (t + 1) * WIDTH
                ]


def join_kernel(place_ref, *refs):
    blocks, outs, sems = refs[:ZN], refs[ZN : ZN + 4], refs[ZN + 4]
    z = place_ref[0]
    copies = []
    for d in range(ZN):
        cols = pl.ds(pl.multiple_of(((z + d) & (ZN - 1)) * PAIR, PAIR), PAIR)
        for t in range(4):
            copies.append(
                pltpu.make_async_copy(
                    blocks[d].at[t * TOK : (t + 1) * TOK, :],
                    outs[t].at[:, cols],
                    sems.at[d * 4 + t],
                )
            )
    for copy in copies:
        copy.start()
    for copy in copies:
        copy.wait()


def exchange(array, groups):
    return lax.all_to_all(
        array, "seq", split_axis=0, concat_axis=0, axis_index_groups=groups, tiled=True
    )


def shift_owner(value, by):
    pairs = []
    for base in range(0, ZN * PLANE, RANGES):
        pairs += [(base + i, base + i + by) for i in range(RANGES) if 0 <= i + by < RANGES]
    return lax.ppermute(value, "seq", pairs)


def body(queries, keys, values, out_grad, cluster_ids):
    index = lax.axis_index("seq")
    place = jnp.stack([index // PLANE, index % RANGES]).astype(I32)
    hbm = pl.BlockSpec(memory_space=pltpu.HBM)
    blocks = call(
        prep_kernel,
        [place, cluster_ids.T, queries, keys, values, out_grad],
        [out((4 * TOK + TILE, PAIR), BF)] * ZN,
        [pltpu.SemaphoreType.DMA((4 * ZN,))],
        specs={0: SMEM[0], 2: hbm, 3: hbm, 4: hbm, 5: hbm},
        limit=60,
    )
    moved = {0: blocks[0]}
    for d in sum(CHUNKS, ()):
        if d:
            moved[d] = lax.ppermute(blocks[d], "seq", z_pairs(d))
    codes, arrived = [], []
    for i, chunk in enumerate(CHUNKS):
        n = len(chunk)
        rows = n * MOST
        send, code = call(
            functools.partial(pack_kernel, chunk),
            [moved[d] for d in chunk] + codes[-1:],
            [out((PLANE, rows + TILE, ALL), BF), out((HPZ * n, TOK), I32)],
            [
                pltpu.VMEM((n * TOK, ALL), BF),
                pltpu.VMEM((PLANE, rows + TILE, ALL), BF),
                pltpu.SemaphoreType.DMA((HPZ,)),
            ],
            flops=PACK_HINT[i],
            out_specs={0: hbm},
        )
        codes.append(code)
        arrived.append(exchange(send, PLANES))
    rows_in, tail, head, rank = call(
        place_kernel,
        [place] + arrived,
        [
            out((SPANS, SPAN, ALL), BF),
            out((SPAN, PAIR), BF),
            out((SPAN, ALL), BF),
            out((1, SLOTS), I32),
        ],
        [pltpu.VMEM((SLOTS, ALL), BF)],
        flops=2 * BLOCK * SLOTS * ALL,
        specs=SMEM,
    )
    tail = shift_owner(tail, 1)
    head = shift_owner(head, -1)
    main, part = call(
        main_kernel,
        [rows_in],
        [out((SPANS, SPAN, ALL), BF), out((2, SPAN, PAIR), F32)],
        [pltpu.VMEM((SPANS, SPAN, PAIR), F32)],
        flops=14 * SPANS * SPAN * 2 * SPAN * WIDTH,
    )
    o = None
    back = {}
    at = ZN * MOST
    for chunk, code in reversed(list(zip(CHUNKS, codes))):
        rows = len(chunk) * MOST
        at -= rows
        send_shape = out((PLANE, rows, ALL), BF)
        flops = 2 * BLOCK * PLANE * rows * ALL
        stage = [pltpu.VMEM((PLANE, rows, ALL), BF), pltpu.SemaphoreType.DMA((PICKS,))]
        if o is None:
            o, send = call(
                functools.partial(edge_kernel, at),
                [place, rank, rows_in, tail, head, main, part],
                [out((BLOCK, ALL), BF), send_shape],
                [pltpu.VMEM((BLOCK, ALL), BF)] + stage + [pltpu.SemaphoreType.DMA((1,))],
                flops=flops,
                specs=SMEM,
                out_specs={0: hbm, 1: hbm},
            )
        else:
            (send,) = call(
                functools.partial(pick_kernel, at),
                [rank, o],
                [send_shape],
                stage,
                flops=flops,
                out_specs={0: hbm},
            )
        got = exchange(send, PLANES)
        pieces = call(
            functools.partial(unpack_kernel, chunk),
            [code, got],
            [out((4 * TOK, PAIR), BF)] * len(chunk),
            flops=4 * RANGES * rows * len(chunk) * TOK * ALL,
        )
        for d, piece in zip(chunk, pieces):
            back[d] = lax.ppermute(piece, "seq", z_pairs(-d)) if d else piece
    return call(
        join_kernel,
        [place] + [back[d] for d in range(ZN)],
        [out((TOK, ZN * PAIR), BF)] * 4,
        [pltpu.SemaphoreType.DMA((4 * ZN,))],
        specs=SMEM,
        out_specs={i: hbm for i in range(4)},
    )


def solution(mesh):
    spec = P("seq", "head")
    return jax.shard_map(
        body,
        mesh=mesh,
        in_specs=(spec,) * 5,
        out_specs=(spec,) * 4,
        check_vma=False,
    )
```

```python
import functools
import math

import jax
import jax.numpy as jnp
from jax import lax
from jax.experimental import pallas as pl
from jax.experimental.pallas import tpu as pltpu
from jax.sharding import PartitionSpec as P

WIDTH = 128
SPAN = 256
CLUSTER_GROUP = 16
RANGES = 8
TOK = 128
MOST = 24
ZN = 8
PLANE = 16
HPZ = 2
ALL = 4 * WIDTH
PAIR = HPZ * WIDTH
STRIDE = 32
SLOTS = PLANE * ZN * MOST
BLOCK = 2048
SPANS = BLOCK // SPAN
TILE = 16
PICKS = 2
NONE = 4095
SCALING = 1.0 / math.sqrt(WIDTH)
BF = jnp.bfloat16
F32 = jnp.float32
I32 = jnp.int32

CHUNKS = ((0, 1, 7, 2), (6, 3, 5, 4))
PICK_HINT = (0, 10**9, 10**11)
UNPACK_HINT = (10**9, 10**11, 10**9)
RETURNS = ((3, 5), (4, 2, 6, 7), (0, 1))
ORDER = sum(CHUNKS, ())
PACK_HINT = (10**6, 10**11)
PLANES = [[z * PLANE + i for i in range(PLANE)] for z in range(ZN)]


def z_pairs(step):
    return [
        (z * PLANE + i, ((z + step) % ZN) * PLANE + i)
        for z in range(ZN)
        for i in range(PLANE)
    ]


def whole():
    return pl.BlockSpec(memory_space=pltpu.VMEM)


def call(kernel, ins, outs, scratch=(), flops=0, specs=None, out_specs=None, out_spec=None, limit=28, aliases=None):
    size = sum(math.prod(o.shape) * o.dtype.itemsize for o in outs)
    size += sum(math.prod(a.shape) * a.dtype.itemsize for a in ins)
    specs = specs or {}
    return pl.pallas_call(
        kernel,
        out_shape=tuple(
            pltpu.HBM(o.shape, o.dtype) if i in (out_specs or {}) else o
            for i, o in enumerate(outs)
        ),
        in_specs=[specs.get(i) or whole() for i in range(len(ins))],
        out_specs=tuple((out_specs or {}).get(i) or out_spec or whole() for i in range(len(outs))),
        scratch_shapes=list(scratch),
        input_output_aliases=aliases or {},
        cost_estimate=pl.CostEstimate(flops=flops, bytes_accessed=size, transcendentals=0),
        compiler_params=pltpu.CompilerParams(vmem_limit_bytes=limit * 1024 * 1024),
    )(*ins)


SMEM = {0: pl.BlockSpec(memory_space=pltpu.SMEM)}


def out(shape, dtype):
    return jax.ShapeDtypeStruct(shape, dtype)


def iota(shape, dim):
    return lax.broadcasted_iota(I32, shape, dim)


def one_hot(mask):
    return mask.astype(F32).astype(BF)


def row_to_col(row):
    eye = iota((128, 128), 0) == iota((128, 128), 1)
    parts = []
    for i in range(row.shape[1] // 128):
        piece = row[:, i * 128 : (i + 1) * 128]
        parts.append(jnp.sum(jnp.where(eye, piece, 0.0), axis=1, keepdims=True))
    return jnp.concatenate(parts, axis=0)


def dot(a, b, dims=((1,), (0,))):
    return lax.dot_general(a, b, (dims, ((), ())), preferred_element_type=F32)


NT = ((1,), (1,))
TN = ((0,), (0,))


def prep_kernel(place_ref, ids_ref, *refs):
    arrays, blocks, sems = refs[:4], refs[4 : 4 + ZN], refs[4 + ZN]
    z = place_ref[0]
    copies = []
    for d in range(ZN):
        cols = pl.ds(pl.multiple_of(((z + d) & (ZN - 1)) * PAIR, PAIR), PAIR)
        for t in range(4):
            copies.append(
                pltpu.make_async_copy(
                    arrays[t].at[:, cols],
                    blocks[d].at[t * TOK : (t + 1) * TOK, :],
                    sems.at[d * 4 + t],
                )
            )
    for copy in copies:
        copy.start()
    for d in range(ZN):
        at = ((z + d) & (ZN - 1)) * HPZ
        rows = [ids_ref[pl.ds(at + hh, 1), :] for hh in range(HPZ)]
        tile = jnp.concatenate(rows + [jnp.zeros((TILE - HPZ, TOK), I32)], axis=0)
        blocks[d][4 * TOK :, 0:TOK] = tile.astype(F32).astype(BF)
        blocks[d][4 * TOK :, TOK:] = jnp.zeros((TILE, PAIR - TOK), BF)
    for copy in copies:
        copy.wait()


def leave(stage_ref, out_ref, sems, i, n):
    size = PLANE // n
    part = slice(i * size, (i + 1) * size)
    return pltpu.make_async_copy(stage_ref.at[part], out_ref.at[part], sems.at[i])


def pack_kernel(index, *refs):
    chunk = CHUNKS[index]
    n = len(chunk)
    blocks, notes = refs[:n], refs[n : n + index]
    out_ref, code_ref, note_ref, x_ref, send_ref, sems = refs[-6:]
    last = index == len(CHUNKS) - 1
    rows = n * MOST
    ids = [blocks[i][4 * TOK :, 0:TOK].astype(F32) for i in range(n)]
    ids = jnp.concatenate(
        [ids[i][hh : hh + 1] for hh in range(HPZ) for i in range(n)], axis=0
    ).astype(I32)
    group = lax.shift_right_logical(ids, 4)
    local = ((ids & (CLUSTER_GROUP - 1)) + 1).astype(F32).astype(BF)
    tri = one_hot(iota((TOK, TOK), 0) < iota((TOK, TOK), 1))
    slot = jnp.zeros(ids.shape, F32)
    for b in range(RANGES):
        hot = (group == b).astype(F32)
        slot = slot + hot * dot(hot.astype(BF), tri)
    code = group * STRIDE + slot.astype(I32)
    code_ref[...] = code
    zeros = jnp.zeros((TILE, WIDTH), BF)
    for hh in range(HPZ):
        for i in range(n):
            for t in range(4):
                x_ref[i * TOK : (i + 1) * TOK, t * WIDTH : (t + 1) * WIDTH] = blocks[i][
                    t * TOK : (t + 1) * TOK, hh * WIDTH : (hh + 1) * WIDTH
                ]
        found = [[] for _ in range(RANGES)]
        for p in range(0, n, 2):
            mine = [hh * n + p, hh * n + p + 1]
            position = jnp.concatenate(
                [(code[i : i + 1] & (STRIDE - 1)) + j * MOST for j, i in enumerate(mine)], axis=1
            )
            owner = jnp.concatenate([group[i : i + 1] for i in mine], axis=1)
            value = jnp.concatenate([local[i : i + 1] for i in mine], axis=1)
            value = jnp.broadcast_to(value, (TILE, 2 * TOK))
            x = x_ref[p * TOK : (p + 2) * TOK, :]
            for b in range(RANGES):
                target = jnp.where(owner == b, position, -1)
                pick = one_hot(target == iota((2 * MOST, 2 * TOK), 0))
                send_ref[hh * RANGES + b, p * MOST : (p + 2) * MOST, :] = dot(pick, x).astype(BF)
                found[b].append(dot(value, pick, NT).astype(BF))
        for b in range(RANGES):
            note = jnp.concatenate(found[b] + [zeros[:, n * MOST :]], axis=1)
            note_ref[hh * RANGES + b] = note
            if last:
                tile = [a[hh * RANGES + b] for a in notes] + [note]
                tile = tile + [zeros] * (4 - len(tile))
                send_ref[hh * RANGES + b, rows:, :] = jnp.concatenate(tile, axis=1)
        leave(send_ref, out_ref, sems, hh, HPZ).start()
    for hh in range(HPZ):
        leave(send_ref, out_ref, sems, hh, HPZ).wait()


def rank_rows(z, clusters):
    lanes = ZN * MOST

    def source(shape, dim):
        segment = iota(shape, dim) // MOST
        value = jnp.zeros(shape, I32)
        for i, d in enumerate(ORDER):
            value = jnp.where(segment == i, (z - d) & (ZN - 1), value)
        return value

    square = (lanes, lanes)
    from_z, to_z = source(square, 0), source(square, 1)
    same = from_z == to_z
    within = one_hot(same & (iota(square, 0) < iota(square, 1)))
    segment = one_hot(same)
    earlier = one_hot(from_z < to_z)
    hot = jnp.concatenate(
        [(clusters == float(c + 1)).astype(F32) for c in range(CLUSTER_GROUP)], axis=0
    )
    low = hot.astype(BF)
    side = CLUSTER_GROUP * PLANE
    row, col = iota((side, side), 0), iota((side, side), 1)
    row_c, col_c = lax.shift_right_logical(row, 4), lax.shift_right_logical(col, 4)
    before = one_hot((row_c == col_c) & (col < row))
    together = one_hot(row_c == col_c)
    lower = one_hot(col_c < row_c)
    total = dot(low, jnp.ones(square, BF))
    rank = (
        dot(low, within)
        + dot(before, dot(low, segment).astype(BF))
        + dot(together, dot(low, earlier).astype(BF))
        + dot(lower, total.astype(BF))
    )
    rank = jnp.sum((hot * rank).reshape(CLUSTER_GROUP, PLANE, lanes), axis=0)
    rank = jnp.where(clusters > 0.5, rank, float(NONE))
    return jnp.concatenate([rank[s : s + 1, :] for s in range(PLANE)], axis=1)


def place_kernel(place_ref, *refs):
    n = len(CHUNKS)
    recvs, (sorted_ref, tail_ref, head_ref, rank_ref, x_ref) = refs[:n], refs[n:]
    clusters = []
    at = 0
    for i, (chunk, recv_ref) in enumerate(zip(CHUNKS, recvs)):
        rows = len(chunk) * MOST
        tail = len(CHUNKS[-1]) * MOST
        clusters.append(
            jnp.concatenate(
                [
                    recvs[-1][s, tail:, i * WIDTH : i * WIDTH + rows].astype(F32)[0:1]
                    for s in range(PLANE)
                ],
                axis=0,
            )
        )
        for s in range(PLANE):
            x_ref[s * ZN * MOST + at : s * ZN * MOST + at + rows, :] = recv_ref[s, 0:rows, :]
        at += rows
    rank = rank_rows(place_ref[0], jnp.concatenate(clusters, axis=1)).astype(I32)
    rank_ref[...] = rank
    x = x_ref[...]
    step = 2
    for c in range(0, SPANS, step):
        pick = one_hot(rank == iota((step * SPAN, SLOTS), 0) + c * SPAN)
        sorted_ref[c : c + step] = dot(pick, x).astype(BF).reshape(step, SPAN, ALL)
    tail_ref[...] = sorted_ref[SPANS - 1, :, WIDTH : 3 * WIDTH]
    head_ref[...] = sorted_ref[0]


def span_math(q, g, k0, k1, v0, v1, keep):
    s0 = dot(k0, q, NT)
    s1 = dot(k1, q, NT)
    if keep is not None:
        s0 = jnp.where(keep, s0, -1e30)
    peak = jnp.maximum(
        jnp.max(s0, axis=0, keepdims=True), jnp.max(s1, axis=0, keepdims=True)
    )
    factor = SCALING * math.log2(math.e)
    p0 = jnp.exp2((s0 - peak) * factor)
    p1 = jnp.exp2((s1 - peak) * factor)
    inverse = 1.0 / (
        jnp.sum(p0, axis=0, keepdims=True) + jnp.sum(p1, axis=0, keepdims=True)
    )
    w0 = p0 * inverse
    w1 = p1 * inverse
    l0 = w0.astype(BF)
    l1 = w1.astype(BF)
    attended = (dot(v0, l0, TN) + dot(v1, l1, TN)).T.astype(BF)
    e0 = dot(v0, g, NT)
    e1 = dot(v1, g, NT)
    inner = jnp.sum(w0 * e0, axis=0, keepdims=True) + jnp.sum(w1 * e1, axis=0, keepdims=True)
    h0 = (w0 * (e0 - inner) * SCALING).astype(BF)
    h1 = (w1 * (e1 - inner) * SCALING).astype(BF)
    dq = (dot(k0, h0, TN) + dot(k1, h1, TN)).T.astype(BF)
    return attended, dq, dot(h0, q), dot(h1, q), dot(l0, g), dot(l1, g)


Q, K, V, G = (slice(t * WIDTH, (t + 1) * WIDTH) for t in range(4))


def main_kernel(in_ref, o_ref, part_ref, d_ref):
    d_ref[0] = jnp.zeros((SPAN, PAIR), F32)

    def one(c, carry):
        att, dq, dk0, dk1, dv0, dv1 = span_math(
            in_ref[c, :, Q], in_ref[c, :, G], in_ref[c - 1, :, K], in_ref[c, :, K],
            in_ref[c - 1, :, V], in_ref[c, :, V], None,
        )
        o_ref[c, :, Q] = att
        o_ref[c, :, K] = dq
        d_ref[c - 1, :, Q] += dk0
        d_ref[c - 1, :, K] += dv0
        d_ref[c, :, Q] = dk1
        d_ref[c, :, K] = dv1
        o_ref[c - 1, :, 2 * WIDTH :] = d_ref[c - 1].astype(BF)
        return carry

    for c in range(1, SPANS):
        one(c, 0)
    part_ref[0] = d_ref[0]
    part_ref[1] = d_ref[SPANS - 1]
    o_ref[0, :, 0 : 2 * WIDTH] = jnp.zeros((SPAN, 2 * WIDTH), BF)
    o_ref[SPANS - 1, :, 2 * WIDTH :] = jnp.zeros((SPAN, 2 * WIDTH), BF)


def pick_out(at, rank_ref, o, out_ref, send_ref, sems):
    col = row_to_col(rank_ref[...].astype(F32)).astype(I32)
    rows = send_ref.shape[1]
    step = PLANE // PICKS
    for p in range(PICKS):
        span = range(p * step, (p + 1) * step)
        part = jnp.concatenate(
            [
                col[i * ZN * MOST + j * MOST : i * ZN * MOST + (j + 1) * MOST, :]
                for i in span
                for j in at
            ],
            axis=0,
        )
        pick = one_hot(part == iota((step * rows, BLOCK), 1))
        send_ref[p * step : (p + 1) * step] = dot(pick, o).astype(BF).reshape(step, rows, ALL)
        leave(send_ref, out_ref, sems, p, PICKS).start()
    for p in range(PICKS):
        leave(send_ref, out_ref, sems, p, PICKS).wait()


def edge_kernel(
    at, place_ref, rank_ref, in_ref, tail_ref, head_ref, main_ref, part_ref,
    done_ref, out_ref, o_ref, send_ref, sems, done_sem,
):
    o_ref[SPAN:BLOCK, :] = main_ref[1:].reshape(BLOCK - SPAN, ALL)
    keep = jnp.broadcast_to(place_ref[1], (SPAN, SPAN)) > 0
    att, dq, _, dk1, _, dv1 = span_math(
        in_ref[0, :, Q], in_ref[0, :, G], tail_ref[:, Q], in_ref[0, :, K],
        tail_ref[:, K], in_ref[0, :, V], keep,
    )
    o_ref[0:SPAN, Q] = att
    o_ref[0:SPAN, K] = dq
    o_ref[0:SPAN, V] = (part_ref[0, :, Q] + dk1).astype(BF)
    o_ref[0:SPAN, G] = (part_ref[0, :, K] + dv1).astype(BF)
    end = SPANS - 1
    _, _, dk0, _, dv0, _ = span_math(
        head_ref[:, Q], head_ref[:, G], in_ref[end, :, K], head_ref[:, K],
        in_ref[end, :, V], head_ref[:, V], None,
    )
    o_ref[BLOCK - SPAN :, V] = (part_ref[1, :, Q] + dk0).astype(BF)
    o_ref[BLOCK - SPAN :, G] = (part_ref[1, :, K] + dv0).astype(BF)
    done = pltpu.make_async_copy(o_ref, done_ref, done_sem.at[0])
    done.start()
    pick_out(at, rank_ref, o_ref[...], out_ref, send_ref, sems)
    done.wait()


def pick_kernel(at, rank_ref, o_ref, *refs):
    pick_out(at, rank_ref, o_ref[...], *refs[-3:])


def unpack_kernel(places, *refs):
    codes, recv_ref, blocks = refs[: len(CHUNKS)], refs[len(CHUNKS)], refs[-len(places) :]
    for hh in range(HPZ):
        for p in range(0, len(places), 2):
            cols = []
            for j, (chunk, at) in enumerate(places[p : p + 2]):
                row = hh * len(CHUNKS[chunk]) + at
                mine = codes[chunk][row : row + 1, :]
                target = lax.shift_right_logical(mine, 5) * (2 * MOST) + (mine & (STRIDE - 1))
                cols.append(row_to_col((target + j * MOST).astype(F32)).astype(I32))
            col = jnp.concatenate(cols, axis=0)
            pick = one_hot(col == iota((2 * TOK, RANGES * 2 * MOST), 1))
            x = recv_ref[hh * RANGES : (hh + 1) * RANGES, p * MOST : (p + 2) * MOST, :]
            got = dot(pick, x.reshape(RANGES * 2 * MOST, ALL)).astype(BF)
            for j in range(2):
                for t in range(4):
                    blocks[p + j][t * TOK : (t + 1) * TOK, hh * WIDTH : (hh + 1) * WIDTH] = got[
                        j * TOK : (j + 1) * TOK, t * WIDTH : (t + 1) * WIDTH
                    ]


def join_kernel(place_ref, *refs):
    blocks, outs, sems = refs[:ZN], refs[ZN : ZN + 4], refs[ZN + 4]
    z = place_ref[0]
    copies = []
    for d in range(ZN):
        cols = pl.ds(pl.multiple_of(((z + d) & (ZN - 1)) * PAIR, PAIR), PAIR)
        for t in range(4):
            copies.append(
                pltpu.make_async_copy(
                    blocks[d].at[t * TOK : (t + 1) * TOK, :],
                    outs[t].at[:, cols],
                    sems.at[d * 4 + t],
                )
            )
    for copy in copies:
        copy.start()
    for copy in copies:
        copy.wait()


def exchange(array, groups):
    return lax.all_to_all(
        array, "seq", split_axis=0, concat_axis=0, axis_index_groups=groups, tiled=True
    )


def shift_owner(value, by):
    pairs = []
    for base in range(0, ZN * PLANE, RANGES):
        pairs += [(base + i, base + i + by) for i in range(RANGES) if 0 <= i + by < RANGES]
    return lax.ppermute(value, "seq", pairs)


def body(queries, keys, values, out_grad, cluster_ids):
    index = lax.axis_index("seq")
    place = jnp.stack([index // PLANE, index % RANGES]).astype(I32)
    hbm = pl.BlockSpec(memory_space=pltpu.HBM)
    anywhere = pl.BlockSpec(memory_space=pl.ANY)
    blocks = call(
        prep_kernel,
        [place, cluster_ids.T, queries, keys, values, out_grad],
        [out((4 * TOK + TILE, PAIR), BF)] * ZN,
        [pltpu.SemaphoreType.DMA((4 * ZN,))],
        specs={0: SMEM[0], 2: hbm, 3: hbm, 4: hbm, 5: hbm},
        limit=60,
    )
    moved = {0: blocks[0]}
    for d in ORDER:
        if d:
            moved[d] = lax.ppermute(blocks[d], "seq", z_pairs(d))
    codes, arrived, notes = [], [], []
    for i, chunk in enumerate(CHUNKS):
        n = len(chunk)
        rows = n * MOST
        extra = TILE if i == len(CHUNKS) - 1 else 0
        send, code, note = call(
            functools.partial(pack_kernel, i),
            [moved[d] for d in chunk] + notes,
            [
                out((PLANE, rows + extra, ALL), BF),
                out((HPZ * n, TOK), I32),
                out((PLANE, TILE, WIDTH), BF),
            ],
            [
                pltpu.VMEM((n * TOK, ALL), BF),
                pltpu.VMEM((PLANE, rows + extra, ALL), BF),
                pltpu.SemaphoreType.DMA((HPZ,)),
            ],
            flops=PACK_HINT[i],
            out_specs={0: hbm},
        )
        codes.append(code)
        notes.append(note)
        arrived.append(exchange(send, PLANES))
    rows_in, tail, head, rank = call(
        place_kernel,
        [place] + arrived,
        [
            out((SPANS, SPAN, ALL), BF),
            out((SPAN, PAIR), BF),
            out((SPAN, ALL), BF),
            out((1, SLOTS), I32),
        ],
        [pltpu.VMEM((SLOTS, ALL), BF)],
        flops=2 * BLOCK * SLOTS * ALL,
        specs=SMEM,
    )
    tail = shift_owner(tail, 1)
    head = shift_owner(head, -1)
    main, part = call(
        main_kernel,
        [rows_in],
        [out((SPANS, SPAN, ALL), BF), out((2, SPAN, PAIR), F32)],
        [pltpu.VMEM((SPANS, SPAN, PAIR), F32)],
        flops=14 * SPANS * SPAN * 2 * SPAN * WIDTH,
    )
    o = None
    back = {}
    waits = {}
    for step, chunk in enumerate(RETURNS):
        rows = len(chunk) * MOST
        at = tuple(ORDER.index(d) for d in chunk)
        send_shape = out((PLANE, rows, ALL), BF)
        flops = 2 * BLOCK * PLANE * rows * ALL
        stage = [pltpu.VMEM((PLANE, rows, ALL), BF), pltpu.SemaphoreType.DMA((PICKS,))]
        if o is None:
            o, send = call(
                functools.partial(edge_kernel, at),
                [place, rank, rows_in, tail, head, main, part],
                [out((BLOCK, ALL), BF), send_shape],
                [pltpu.VMEM((BLOCK, ALL), BF)] + stage + [pltpu.SemaphoreType.DMA((1,))],
                flops=flops,
                specs=SMEM,
                out_specs={0: hbm, 1: hbm},
            )
        else:
            (send,) = call(
                functools.partial(pick_kernel, at),
                [rank, o] + waits.get(("pick", step), []),
                [send_shape],
                stage,
                flops=PICK_HINT[step],
                specs={2: anywhere},
                out_specs={0: hbm},
            )
        got = exchange(send, PLANES)
        places = tuple(
            (i, c.index(d)) for d in chunk for i, c in enumerate(CHUNKS) if d in c
        )
        pieces = call(
            functools.partial(unpack_kernel, places),
            codes + [got] + waits.get(("unpack", step), []),
            [out((4 * TOK, PAIR), BF)] * len(chunk),
            flops=UNPACK_HINT[step],
            specs={j: anywhere for j in range(len(codes) + 1, len(codes) + 5)},
        )
        for d, piece in zip(chunk, pieces):
            back[d] = lax.ppermute(piece, "seq", z_pairs(-d)) if d else piece
        waits["pick", step + 2] = [pieces[0]]
        if step == 0:
            waits["unpack", 1] = [back[d] for d in chunk]
    return call(
        join_kernel,
        [place] + [back[d] for d in range(ZN)],
        [out((TOK, ZN * PAIR), BF)] * 4,
        [pltpu.SemaphoreType.DMA((4 * ZN,))],
        specs=SMEM,
        out_specs={i: hbm for i in range(4)},
    )


def solution(mesh):
    spec = P("seq", "head")
    return jax.shard_map(
        body,
        mesh=mesh,
        in_specs=(spec,) * 5,
        out_specs=(spec,) * 4,
        check_vma=False,
    )
```

```python
import functools
import math

import jax
import jax.numpy as jnp
from jax import lax
from jax.experimental import pallas as pl
from jax.experimental.pallas import tpu as pltpu
from jax.sharding import PartitionSpec as P

WIDTH = 128
SPAN = 256
CLUSTER_GROUP = 16
RANGES = 8
TOK = 128
MOST = 24
ZN = 8
PLANE = 16
HPZ = 2
STRIDE = 32
TILE = 16
NONE = 4095
TWO = 2 * WIDTH
LINE = ZN * MOST
FLAT = PLANE * MOST
SLOTS = PLANE * LINE
HOPS = (1, 7, 2, 6, 3, 5, 4)
BLOCK = 2048
SPANS = BLOCK // SPAN
SCALING = 1.0 / math.sqrt(WIDTH)
BF = jnp.bfloat16
F32 = jnp.float32
I32 = jnp.int32

PLANES = [[z * PLANE + i for i in range(PLANE)] for z in range(ZN)]


def z_pairs(step):
    return [
        (z * PLANE + i, ((z + step) % ZN) * PLANE + i)
        for z in range(ZN)
        for i in range(PLANE)
    ]


def whole():
    return pl.BlockSpec(memory_space=pltpu.VMEM)


def call(kernel, ins, outs, scratch=(), flops=0, specs=None, out_specs=None, out_spec=None, limit=28, aliases=None):
    size = sum(math.prod(o.shape) * o.dtype.itemsize for o in outs)
    size += sum(math.prod(a.shape) * a.dtype.itemsize for a in ins)
    specs = specs or {}
    return pl.pallas_call(
        kernel,
        out_shape=tuple(
            pltpu.HBM(o.shape, o.dtype) if i in (out_specs or {}) else o
            for i, o in enumerate(outs)
        ),
        in_specs=[specs.get(i) or whole() for i in range(len(ins))],
        out_specs=tuple((out_specs or {}).get(i) or out_spec or whole() for i in range(len(outs))),
        scratch_shapes=list(scratch),
        input_output_aliases=aliases or {},
        cost_estimate=pl.CostEstimate(flops=flops, bytes_accessed=size, transcendentals=0),
        compiler_params=pltpu.CompilerParams(vmem_limit_bytes=limit * 1024 * 1024),
    )(*ins)


SMEM = {0: pl.BlockSpec(memory_space=pltpu.SMEM)}


def out(shape, dtype):
    return jax.ShapeDtypeStruct(shape, dtype)


def iota(shape, dim):
    return lax.broadcasted_iota(I32, shape, dim)


def one_hot(mask):
    return mask.astype(F32).astype(BF)


def row_to_col(row):
    eye = iota((128, 128), 0) == iota((128, 128), 1)
    parts = []
    for i in range(row.shape[1] // 128):
        piece = row[:, i * 128 : (i + 1) * 128]
        parts.append(jnp.sum(jnp.where(eye, piece, 0.0), axis=1, keepdims=True))
    return jnp.concatenate(parts, axis=0)


def dot(a, b, dims=((1,), (0,))):
    return lax.dot_general(a, b, (dims, ((), ())), preferred_element_type=F32)


NT = ((1,), (1,))
TN = ((0,), (0,))


A, B = slice(0, WIDTH), slice(WIDTH, TWO)


def prep_kernel(place_ref, ids_ref, *refs):
    arrays, blocks, sems = refs[:2], refs[2 : 2 + ZN], refs[2 + ZN]
    z = place_ref[0]
    copies = []
    for d in HOPS + (0,):
        cols = pl.ds(pl.multiple_of(((z + d) & (ZN - 1)) * TWO, TWO), TWO)
        for t in range(2):
            copies.append(
                pltpu.make_async_copy(
                    arrays[t].at[:, cols],
                    blocks[d].at[t * TOK : (t + 1) * TOK, :],
                    sems.at[d * 2 + t],
                )
            )
    for copy in copies:
        copy.start()
    for d in range(ZN):
        at = ((z + d) & (ZN - 1)) * HPZ
        rows = [ids_ref[pl.ds(at + hh, 1), :] for hh in range(HPZ)]
        tile = jnp.concatenate(rows + [jnp.zeros((TILE - HPZ, TOK), I32)], axis=0)
        blocks[d][2 * TOK :, 0:TOK] = tile.astype(F32).astype(BF)
        blocks[d][2 * TOK :, TOK:] = jnp.zeros((TILE, TWO - TOK), BF)
    for copy in copies:
        copy.wait()


def leave(stage_ref, out_ref, sems, i, n):
    size = PLANE // n
    part = slice(i * size, (i + 1) * size)
    return pltpu.make_async_copy(stage_ref.at[part], out_ref.at[part], sems.at[i])


def codes_of(ids):
    group = lax.shift_right_logical(ids, 4)
    tri = one_hot(iota((TOK, TOK), 0) < iota((TOK, TOK), 1))
    slot = jnp.zeros(ids.shape, F32)
    for b in range(RANGES):
        hot = (group == b).astype(F32)
        slot = slot + hot * dot(hot.astype(BF), tri)
    return group * STRIDE + slot.astype(I32)


def pair_rows(rows):
    owner = jnp.concatenate([lax.shift_right_logical(r, 5) for r in rows], axis=1)
    place = jnp.concatenate(
        [(r & (STRIDE - 1)) + j * MOST for j, r in enumerate(rows)], axis=1
    )
    return owner, place


def slot_pick(owner, place, b):
    target = jnp.where(owner == b, place, -1)
    return one_hot(target == iota((2 * MOST, 2 * TOK), 0))


def pack_own_kernel(ids_ref, v_ref, g_ref, out_ref, code_ref, send_ref, sems):
    code = codes_of(ids_ref[...])
    code_ref[...] = code
    for hh in range(HPZ):
        for p in range(0, ZN, 2):
            heads = [(p + j) * HPZ + hh for j in range(2)]
            owner, place = pair_rows([code[h : h + 1, :] for h in heads])
            x = jnp.concatenate(
                [
                    jnp.concatenate(
                        [ref[:, h * WIDTH : (h + 1) * WIDTH] for ref in (v_ref, g_ref)], axis=1
                    )
                    for h in heads
                ],
                axis=0,
            )
            for b in range(RANGES):
                send_ref[hh * RANGES + b, p * MOST : (p + 2) * MOST, :] = dot(
                    slot_pick(owner, place, b), x
                ).astype(BF)
        leave(send_ref, out_ref, sems, hh, HPZ).start()
    for hh in range(HPZ):
        leave(send_ref, out_ref, sems, hh, HPZ).wait()


def pack_kernel(*refs):
    blocks, (out_ref, code_ref, send_ref, sems) = refs[:ZN], refs[ZN:]
    ids = [blocks[d][2 * TOK :, 0:TOK].astype(F32) for d in range(ZN)]
    ids = jnp.concatenate(
        [ids[d][hh : hh + 1] for hh in range(HPZ) for d in range(ZN)], axis=0
    ).astype(I32)
    code = codes_of(ids)
    code_ref[...] = code
    local = ((ids & (CLUSTER_GROUP - 1)) + 1).astype(F32).astype(BF)
    for hh in range(HPZ):
        cols = slice(hh * WIDTH, (hh + 1) * WIDTH)
        found = [[] for _ in range(RANGES)]
        for p in range(0, ZN, 2):
            mine = [hh * ZN + p, hh * ZN + p + 1]
            owner, place = pair_rows([code[i : i + 1, :] for i in mine])
            value = jnp.concatenate([local[i : i + 1, :] for i in mine], axis=1)
            value = jnp.broadcast_to(value, (TILE, 2 * TOK))
            x = jnp.concatenate(
                [
                    jnp.concatenate(
                        [blocks[d][t * TOK : (t + 1) * TOK, cols] for t in range(2)], axis=1
                    )
                    for d in (p, p + 1)
                ],
                axis=0,
            )
            for b in range(RANGES):
                pick = slot_pick(owner, place, b)
                send_ref[hh * RANGES + b, p * MOST : (p + 2) * MOST, :] = dot(pick, x).astype(BF)
                found[b].append(dot(value, pick, NT).astype(BF))
        for b in range(RANGES):
            send_ref[hh * RANGES + b, LINE:, :] = jnp.concatenate(
                found[b] + [jnp.zeros((TILE, TWO - LINE), BF)], axis=1
            )
        leave(send_ref, out_ref, sems, hh, HPZ).start()
    for hh in range(HPZ):
        leave(send_ref, out_ref, sems, hh, HPZ).wait()


def spread_kernel(place_ref, recv_ref, *refs):
    blocks, wide_ref = refs[:ZN], refs[ZN]
    z = place_ref[0]
    for s in range(PLANE):
        wide_ref[s] = recv_ref[s].astype(F32).reshape(ZN, MOST, TWO)
    for d in range(ZN):
        at = (z + d) & (ZN - 1)
        for s in range(0, PLANE, 2):
            both = jnp.concatenate([wide_ref[s, at], wide_ref[s + 1, at]], axis=0)
            blocks[d][s * MOST : (s + 2) * MOST, :] = both.astype(BF)


def gather_kernel(*refs):
    blocks, (out_ref, send_ref, sems) = refs[:ZN], refs[ZN:]
    for s in range(0, PLANE, 2):
        both = [blocks[d][s * MOST : (s + 2) * MOST, :].astype(F32) for d in range(ZN)]
        for j in range(2):
            send_ref[s + j] = jnp.concatenate(
                [v[j * MOST : (j + 1) * MOST] for v in both], axis=0
            ).astype(BF)
        if s % 8 == 6:
            leave(send_ref, out_ref, sems, s // 8, 2).start()
    for i in range(2):
        leave(send_ref, out_ref, sems, i, 2).wait()


def rank_rows(z, clusters):
    lanes = LINE

    def source(shape, dim):
        return (z - iota(shape, dim) // MOST) & (ZN - 1)

    square = (lanes, lanes)
    from_z, to_z = source(square, 0), source(square, 1)
    same = from_z == to_z
    within = one_hot(same & (iota(square, 0) < iota(square, 1)))
    segment = one_hot(same)
    earlier = one_hot(from_z < to_z)
    hot = jnp.concatenate(
        [(clusters == float(c + 1)).astype(F32) for c in range(CLUSTER_GROUP)], axis=0
    )
    low = hot.astype(BF)
    side = CLUSTER_GROUP * PLANE
    row, col = iota((side, side), 0), iota((side, side), 1)
    row_c, col_c = lax.shift_right_logical(row, 4), lax.shift_right_logical(col, 4)
    before = one_hot((row_c == col_c) & (col < row))
    together = one_hot(row_c == col_c)
    lower = one_hot(col_c < row_c)
    total = dot(low, jnp.ones(square, BF))
    rank = (
        dot(low, within)
        + dot(before, dot(low, segment).astype(BF))
        + dot(together, dot(low, earlier).astype(BF))
        + dot(lower, total.astype(BF))
    )
    rank = jnp.sum((hot * rank).reshape(CLUSTER_GROUP, PLANE, lanes), axis=0)
    rank = jnp.where(clusters > 0.5, rank, float(NONE))
    return rank


def sort_rows(rank, x, sorted_ref):
    step = 4
    for c in range(0, SPANS, step):
        pick = one_hot(rank == iota((step * SPAN, SLOTS), 0) + c * SPAN)
        sorted_ref[c : c + step] = dot(pick, x).astype(BF).reshape(step, SPAN, TWO)


def place_kernel(place_ref, recv_ref, sorted_ref, tail_ref, head_ref, by_s_ref, by_z_ref, x_ref):
    clusters = jnp.concatenate(
        [recv_ref[s, LINE:, 0:LINE].astype(F32)[0:1] for s in range(PLANE)], axis=0
    )
    for s in range(PLANE):
        x_ref[s * LINE : (s + 1) * LINE, :] = recv_ref[s, 0:LINE, :]
    rank = rank_rows(place_ref[0], clusters)
    row = jnp.concatenate([rank[s : s + 1, :] for s in range(PLANE)], axis=1).astype(I32)
    by_s_ref[...] = row
    whole_rank = rank.astype(I32)
    halves = jnp.concatenate(
        [lax.shift_right_logical(whole_rank, 8), whole_rank & 255], axis=0
    ).astype(F32).astype(BF)
    lane = iota((1, FLAT), 1)
    source = lane // MOST
    slot = lane - source * MOST
    mine = iota((PLANE, FLAT), 0) == source
    for d in range(ZN):
        spread = one_hot(iota((LINE, FLAT), 0) == slot + d * MOST)
        both = dot(halves, spread)
        both = both[0:PLANE] * 256.0 + both[PLANE:]
        by_z_ref[:, d * FLAT : (d + 1) * FLAT] = jnp.sum(
            jnp.where(mine, both, 0.0), axis=0, keepdims=True
        ).astype(I32)
    sort_rows(row, x_ref[...], sorted_ref)
    tail_ref[...] = sorted_ref[SPANS - 1, :, B]
    head_ref[...] = sorted_ref[0]


def place_late_kernel(rank_ref, *refs):
    blocks, (sorted_ref, tail_ref, head_ref, x_ref) = refs[:ZN], refs[ZN:]
    for d in range(ZN):
        x_ref[d * FLAT : (d + 1) * FLAT, :] = blocks[d][...]
    sort_rows(rank_ref[...], x_ref[...], sorted_ref)
    tail_ref[...] = sorted_ref[SPANS - 1, :, A]
    head_ref[...] = sorted_ref[0]


def span_math(q, g, k0, k1, v0, v1, keep):
    s0 = dot(k0, q, NT)
    s1 = dot(k1, q, NT)
    if keep is not None:
        s0 = jnp.where(keep, s0, -1e30)
    peak = jnp.maximum(
        jnp.max(s0, axis=0, keepdims=True), jnp.max(s1, axis=0, keepdims=True)
    )
    factor = SCALING * math.log2(math.e)
    p0 = jnp.exp2((s0 - peak) * factor)
    p1 = jnp.exp2((s1 - peak) * factor)
    inverse = 1.0 / (
        jnp.sum(p0, axis=0, keepdims=True) + jnp.sum(p1, axis=0, keepdims=True)
    )
    w0 = p0 * inverse
    w1 = p1 * inverse
    l0 = w0.astype(BF)
    l1 = w1.astype(BF)
    attended = (dot(v0, l0, TN) + dot(v1, l1, TN)).T.astype(BF)
    e0 = dot(v0, g, NT)
    e1 = dot(v1, g, NT)
    inner = jnp.sum(w0 * e0, axis=0, keepdims=True) + jnp.sum(w1 * e1, axis=0, keepdims=True)
    h0 = (w0 * (e0 - inner) * SCALING).astype(BF)
    h1 = (w1 * (e1 - inner) * SCALING).astype(BF)
    dq = (dot(k0, h0, TN) + dot(k1, h1, TN)).T.astype(BF)
    return attended, dq, dot(h0, q), dot(h1, q), dot(l0, g), dot(l1, g)


def main_kernel(qk_ref, vg_ref, early_ref, late_ref, part_ref, d_ref):
    d_ref[0] = jnp.zeros((SPAN, TWO), F32)
    for c in range(1, SPANS):
        att, dq, dk0, dk1, dv0, dv1 = span_math(
            qk_ref[c, :, A], vg_ref[c, :, B], qk_ref[c - 1, :, B], qk_ref[c, :, B],
            vg_ref[c - 1, :, A], vg_ref[c, :, A], None,
        )
        early_ref[c, :, A] = att
        early_ref[c, :, B] = dq
        d_ref[c - 1, :, A] += dk0
        d_ref[c - 1, :, B] += dv0
        d_ref[c, :, A] = dk1
        d_ref[c, :, B] = dv1
        late_ref[c - 1] = d_ref[c - 1].astype(BF)
    part_ref[0] = d_ref[0]
    part_ref[1] = d_ref[SPANS - 1]
    early_ref[0] = jnp.zeros((SPAN, TWO), BF)
    late_ref[SPANS - 1] = jnp.zeros((SPAN, TWO), BF)


def column(rank_ref):
    return row_to_col(rank_ref[...].astype(F32)).astype(I32)


def edge_kernel(
    place_ref, by_z_ref, qk_ref, vg_ref, tail_k_ref, head_qk_ref, tail_v_ref, head_vg_ref,
    early_ref, late_ref, part_ref, done_ref, *refs,
):
    blocks, o_ref = refs[:ZN], refs[ZN]
    keep = jnp.broadcast_to(place_ref[1], (SPAN, SPAN)) > 0
    end = SPANS - 1
    o_ref[SPAN:, :] = early_ref[1:].reshape(BLOCK - SPAN, TWO)
    done_ref[SPAN : BLOCK - SPAN, :] = late_ref[1:end].reshape(BLOCK - 2 * SPAN, TWO)
    att, dq, _, dk1, _, dv1 = span_math(
        qk_ref[0, :, A], vg_ref[0, :, B], tail_k_ref[...], qk_ref[0, :, B],
        tail_v_ref[...], vg_ref[0, :, A], keep,
    )
    o_ref[0:SPAN, A] = att
    o_ref[0:SPAN, B] = dq
    done_ref[0:SPAN, A] = (part_ref[0, :, A] + dk1).astype(BF)
    done_ref[0:SPAN, B] = (part_ref[0, :, B] + dv1).astype(BF)
    _, _, dk0, _, dv0, _ = span_math(
        head_qk_ref[:, A], head_vg_ref[:, B], qk_ref[end, :, B], head_qk_ref[:, B],
        vg_ref[end, :, A], head_vg_ref[:, A], None,
    )
    done_ref[BLOCK - SPAN :, A] = (part_ref[1, :, A] + dk0).astype(BF)
    done_ref[BLOCK - SPAN :, B] = (part_ref[1, :, B] + dv0).astype(BF)
    col = column(by_z_ref)
    o = o_ref[...]
    for d in range(0, ZN, 2):
        pick = one_hot(col[d * FLAT : (d + 2) * FLAT, :] == iota((2 * FLAT, BLOCK), 1))
        got = dot(pick, o).astype(BF)
        blocks[d][...] = got[0:FLAT]
        blocks[d + 1][...] = got[FLAT:]


def pick_kernel(by_s_ref, o_ref, out_ref, send_ref, sems):
    col = column(by_s_ref)
    o = o_ref[...]
    step = 4
    for s in range(0, PLANE, step):
        pick = one_hot(col[s * LINE : (s + step) * LINE, :] == iota((step * LINE, BLOCK), 1))
        send_ref[s : s + step] = dot(pick, o).astype(BF).reshape(step, LINE, TWO)
        leave(send_ref, out_ref, sems, s // step, 4).start()
    for i in range(4):
        leave(send_ref, out_ref, sems, i, 4).wait()


def take_pair(codes, recv_ref, hh, p):
    cols = []
    for j, code in enumerate(codes):
        target = lax.shift_right_logical(code, 5) * (2 * MOST) + (code & (STRIDE - 1))
        cols.append(row_to_col((target + j * MOST).astype(F32)).astype(I32))
    pick = one_hot(jnp.concatenate(cols, axis=0) == iota((2 * TOK, RANGES * 2 * MOST), 1))
    x = recv_ref[hh * RANGES : (hh + 1) * RANGES, p * MOST : (p + 2) * MOST, :]
    return dot(pick, x.reshape(RANGES * 2 * MOST, TWO)).astype(BF)


def unpack_kernel(code_ref, recv_ref, *blocks):
    code = code_ref[...]
    for hh in range(HPZ):
        for p in range(0, ZN, 2):
            rows = [code[hh * ZN + d : hh * ZN + d + 1, :] for d in (p, p + 1)]
            got = take_pair(rows, recv_ref, hh, p)
            for j in range(2):
                for t in range(2):
                    blocks[p + j][t * TOK : (t + 1) * TOK, hh * WIDTH : (hh + 1) * WIDTH] = got[
                        j * TOK : (j + 1) * TOK, t * WIDTH : (t + 1) * WIDTH
                    ]


def unpack_own_kernel(place_ref, code_ref, recv_ref, *refs):
    outs, stages, sems = refs[:2], refs[2:4], refs[4]
    z = place_ref[0]
    for hh in range(HPZ):
        for p in range(0, ZN, 2):
            heads = [((z + d) & (ZN - 1)) * HPZ + hh for d in (p, p + 1)]
            got = take_pair([code_ref[pl.ds(h, 1), :] for h in heads], recv_ref, hh, p)
            for j, h in enumerate(heads):
                cols = pl.ds(pl.multiple_of(h * WIDTH, WIDTH), WIDTH)
                for t in range(2):
                    stages[t][:, cols] = got[
                        j * TOK : (j + 1) * TOK, t * WIDTH : (t + 1) * WIDTH
                    ]
    copies = [pltpu.make_async_copy(stages[t], outs[t], sems.at[t]) for t in range(2)]
    for copy in copies:
        copy.start()
    for copy in copies:
        copy.wait()


def join_kernel(place_ref, *refs):
    blocks, outs, sems = refs[:ZN], refs[ZN : ZN + 2], refs[ZN + 2]
    z = place_ref[0]
    copies = []
    for d in range(ZN):
        cols = pl.ds(pl.multiple_of(((z + d) & (ZN - 1)) * TWO, TWO), TWO)
        for t in range(2):
            copies.append(
                pltpu.make_async_copy(
                    blocks[d].at[t * TOK : (t + 1) * TOK, :],
                    outs[t].at[:, cols],
                    sems.at[d * 2 + t],
                )
            )
    for copy in copies:
        copy.start()
    for copy in copies:
        copy.wait()


def exchange(array, groups):
    return lax.all_to_all(
        array, "seq", split_axis=0, concat_axis=0, axis_index_groups=groups, tiled=True
    )


def shift_owner(value, by):
    pairs = []
    for base in range(0, ZN * PLANE, RANGES):
        pairs += [(base + i, base + i + by) for i in range(RANGES) if 0 <= i + by < RANGES]
    return lax.ppermute(value, "seq", pairs)


def along_z(blocks, sign):
    moved = [blocks[0]] + [None] * (ZN - 1)
    for d in HOPS:
        moved[d] = lax.ppermute(blocks[d], "seq", z_pairs(sign * d))
    return moved


def body(queries, keys, values, out_grad, cluster_ids):
    index = lax.axis_index("seq")
    place = jnp.stack([index // PLANE, index % RANGES]).astype(I32)
    hbm = pl.BlockSpec(memory_space=pltpu.HBM)
    ids = cluster_ids.T
    line = out((PLANE, LINE, TWO), BF)
    stage = pltpu.VMEM((PLANE, LINE, TWO), BF)
    dma = pltpu.SemaphoreType.DMA
    tall = out((SPANS, SPAN, TWO), BF)
    half, full = out((SPAN, WIDTH), BF), out((SPAN, TWO), BF)
    flat = [out((FLAT, TWO), BF)] * ZN
    rank_shape = out((1, SLOTS), I32)
    sort_flops = 2 * BLOCK * SLOTS * TWO

    blocks = call(
        prep_kernel,
        [place, ids, queries, keys],
        [out((2 * TOK + TILE, TWO), BF)] * ZN,
        [dma((2 * ZN,))],
        specs={0: SMEM[0], 2: hbm, 3: hbm},
        limit=60,
    )
    moved = along_z(blocks, 1)
    send, own_code = call(
        pack_own_kernel,
        [ids, values, out_grad],
        [line, out((HPZ * ZN, TOK), I32)],
        [stage, dma((HPZ,))],
        out_specs={0: hbm},
        flops=10**8,
    )
    crossed = exchange(send, PLANES)
    spread = call(
        spread_kernel,
        [place, crossed],
        flat,
        [pltpu.VMEM((PLANE, ZN, MOST, TWO), F32)],
        specs=SMEM,
    )
    late = along_z(spread, 1)
    send, code = call(
        pack_kernel,
        moved,
        [out((PLANE, LINE + TILE, TWO), BF), out((HPZ * ZN, TOK), I32)],
        [pltpu.VMEM((PLANE, LINE + TILE, TWO), BF), dma((HPZ,))],
        out_specs={0: hbm},
        flops=10**8,
    )
    qk, tail_k, head_qk, by_s, by_z = call(
        place_kernel,
        [place, exchange(send, PLANES)],
        [tall, half, full, rank_shape, rank_shape],
        [pltpu.VMEM((SLOTS, TWO), BF)],
        flops=sort_flops,
        specs=SMEM,
    )
    tail_k, head_qk = shift_owner(tail_k, 1), shift_owner(head_qk, -1)
    vg, tail_v, head_vg = call(
        place_late_kernel,
        [by_z] + late,
        [tall, half, full],
        [pltpu.VMEM((SLOTS, TWO), BF)],
        flops=sort_flops,
    )
    tail_v, head_vg = shift_owner(tail_v, 1), shift_owner(head_vg, -1)
    early, rest, part = call(
        main_kernel,
        [qk, vg],
        [tall, tall, out((2, SPAN, TWO), F32)],
        [pltpu.VMEM((SPANS, SPAN, TWO), F32)],
        flops=14 * SPANS * SPAN * 2 * SPAN * WIDTH,
    )
    done, *picked = call(
        edge_kernel,
        [place, by_z, qk, vg, tail_k, head_qk, tail_v, head_vg, early, rest, part],
        [out((BLOCK, TWO), BF)] + flat,
        [pltpu.VMEM((BLOCK, TWO), BF)],
        flops=sort_flops,
        specs=SMEM,
    )
    (send,) = call(
        pick_kernel, [by_s, done], [line], [stage, dma((4,))], flops=sort_flops, out_specs={0: hbm}
    )
    got = exchange(send, PLANES)
    returned = along_z(picked, -1)
    pieces = call(
        unpack_kernel, [code, got], [out((2 * TOK, TWO), BF)] * ZN, flops=10**8
    )
    (send,) = call(
        gather_kernel, returned, [line], [stage, dma((2,))], out_specs={0: hbm}
    )
    got = exchange(send, PLANES)
    back = along_z(pieces, -1)
    wide = out((TOK, ZN * TWO), BF)
    attended, grad_queries = call(
        unpack_own_kernel,
        [place, own_code, got],
        [wide] * 2,
        [pltpu.VMEM((TOK, ZN * TWO), BF)] * 2 + [dma((2,))],
        flops=10**8,
        specs=SMEM,
        out_specs={0: hbm, 1: hbm},
    )
    grad_keys, grad_values = call(
        join_kernel,
        [place] + back,
        [wide] * 2,
        [dma((2 * ZN,))],
        specs=SMEM,
        out_specs={0: hbm, 1: hbm},
    )
    return attended, grad_queries, grad_keys, grad_values


def solution(mesh):
    spec = P("seq", "head")
    return jax.shard_map(
        body,
        mesh=mesh,
        in_specs=(spec,) * 5,
        out_specs=(spec,) * 4,
        check_vma=False,
    )
```

```python
import functools
import math

import jax
import jax.numpy as jnp
from jax import lax
from jax.experimental import pallas as pl
from jax.experimental.pallas import tpu as pltpu
from jax.sharding import PartitionSpec as P

WIDTH = 128
SPAN = 256
CLUSTER_GROUP = 16
RANGES = 8
TOK = 128
MOST = 24
ZN = 8
PLANE = 16
HPZ = 2
ALL = 4 * WIDTH
PAIR = HPZ * WIDTH
STRIDE = 32
SLOTS = PLANE * ZN * MOST
BLOCK = 2048
SPANS = BLOCK // SPAN
TILE = 16
PICKS = 2
NONE = 4095
SCALING = 1.0 / math.sqrt(WIDTH)
BF = jnp.bfloat16
F32 = jnp.float32
I32 = jnp.int32

CHUNKS = ((0, 1, 7, 2), (6, 3, 5, 4))
PICK_HINT = (0, 10**9, 10**9)
UNPACK_HINT = (10**9, 10**11, 10**9)
RETURNS = ((3, 5), (4, 2, 6, 7), (0, 1))
ORDER = sum(CHUNKS, ())
SOON = (2, 6)
PACK_HINT = (10**6, 10**11)
PLANES = [[z * PLANE + i for i in range(PLANE)] for z in range(ZN)]


def z_pairs(step):
    return [
        (z * PLANE + i, ((z + step) % ZN) * PLANE + i)
        for z in range(ZN)
        for i in range(PLANE)
    ]


def whole():
    return pl.BlockSpec(memory_space=pltpu.VMEM)


def call(kernel, ins, outs, scratch=(), flops=0, specs=None, out_specs=None, out_spec=None, limit=28, aliases=None):
    size = sum(math.prod(o.shape) * o.dtype.itemsize for o in outs)
    size += sum(math.prod(a.shape) * a.dtype.itemsize for a in ins)
    specs = specs or {}
    return pl.pallas_call(
        kernel,
        out_shape=tuple(
            pltpu.HBM(o.shape, o.dtype) if i in (out_specs or {}) else o
            for i, o in enumerate(outs)
        ),
        in_specs=[specs.get(i) or whole() for i in range(len(ins))],
        out_specs=tuple((out_specs or {}).get(i) or out_spec or whole() for i in range(len(outs))),
        scratch_shapes=list(scratch),
        input_output_aliases=aliases or {},
        cost_estimate=pl.CostEstimate(flops=flops, bytes_accessed=size, transcendentals=0),
        compiler_params=pltpu.CompilerParams(vmem_limit_bytes=limit * 1024 * 1024),
    )(*ins)


SMEM = {0: pl.BlockSpec(memory_space=pltpu.SMEM)}


def out(shape, dtype):
    return jax.ShapeDtypeStruct(shape, dtype)


def iota(shape, dim):
    return lax.broadcasted_iota(I32, shape, dim)


def one_hot(mask):
    return mask.astype(F32).astype(BF)


def row_to_col(row):
    eye = iota((128, 128), 0) == iota((128, 128), 1)
    parts = []
    for i in range(row.shape[1] // 128):
        piece = row[:, i * 128 : (i + 1) * 128]
        parts.append(jnp.sum(jnp.where(eye, piece, 0.0), axis=1, keepdims=True))
    return jnp.concatenate(parts, axis=0)


def dot(a, b, dims=((1,), (0,))):
    return lax.dot_general(a, b, (dims, ((), ())), preferred_element_type=F32)


NT = ((1,), (1,))
TN = ((0,), (0,))


def prep_kernel(place_ref, ids_ref, *refs):
    arrays, blocks, sems = refs[:4], refs[4 : 4 + ZN], refs[4 + ZN]
    z = place_ref[0]
    copies = []
    for d in range(ZN):
        cols = pl.ds(pl.multiple_of(((z + d) & (ZN - 1)) * PAIR, PAIR), PAIR)
        for t in range(4):
            copies.append(
                pltpu.make_async_copy(
                    arrays[t].at[:, cols],
                    blocks[d].at[t * TOK : (t + 1) * TOK, :],
                    sems.at[d * 4 + t],
                )
            )
    for copy in copies:
        copy.start()
    for d in range(ZN):
        at = ((z + d) & (ZN - 1)) * HPZ
        rows = [ids_ref[pl.ds(at + hh, 1), :] for hh in range(HPZ)]
        tile = jnp.concatenate(rows + [jnp.zeros((TILE - HPZ, TOK), I32)], axis=0)
        blocks[d][4 * TOK :, 0:TOK] = tile.astype(F32).astype(BF)
        blocks[d][4 * TOK :, TOK:] = jnp.zeros((TILE, PAIR - TOK), BF)
    for copy in copies:
        copy.wait()


def leave(stage_ref, out_ref, sems, i, n):
    size = PLANE // n
    part = slice(i * size, (i + 1) * size)
    return pltpu.make_async_copy(stage_ref.at[part], out_ref.at[part], sems.at[i])


def pack_kernel(index, *refs):
    chunk = CHUNKS[index]
    n = len(chunk)
    blocks, notes = refs[:n], refs[n : n + index]
    out_ref, code_ref, note_ref, x_ref, send_ref, sems = refs[-6:]
    last = index == len(CHUNKS) - 1
    rows = n * MOST
    ids = [blocks[i][4 * TOK :, 0:TOK].astype(F32) for i in range(n)]
    ids = jnp.concatenate(
        [ids[i][hh : hh + 1] for hh in range(HPZ) for i in range(n)], axis=0
    ).astype(I32)
    group = lax.shift_right_logical(ids, 4)
    local = ((ids & (CLUSTER_GROUP - 1)) + 1).astype(F32).astype(BF)
    tri = one_hot(iota((TOK, TOK), 0) < iota((TOK, TOK), 1))
    slot = jnp.zeros(ids.shape, F32)
    for b in range(RANGES):
        hot = (group == b).astype(F32)
        slot = slot + hot * dot(hot.astype(BF), tri)
    code = group * STRIDE + slot.astype(I32)
    code_ref[...] = code
    zeros = jnp.zeros((TILE, WIDTH), BF)
    for hh in range(HPZ):
        for i in range(n):
            for t in range(4):
                x_ref[i * TOK : (i + 1) * TOK, t * WIDTH : (t + 1) * WIDTH] = blocks[i][
                    t * TOK : (t + 1) * TOK, hh * WIDTH : (hh + 1) * WIDTH
                ]
        found = [[] for _ in range(RANGES)]
        for p in range(0, n, 2):
            mine = [hh * n + p, hh * n + p + 1]
            position = jnp.concatenate(
                [(code[i : i + 1] & (STRIDE - 1)) + j * MOST for j, i in enumerate(mine)], axis=1
            )
            owner = jnp.concatenate([group[i : i + 1] for i in mine], axis=1)
            value = jnp.concatenate([local[i : i + 1] for i in mine], axis=1)
            value = jnp.broadcast_to(value, (TILE, 2 * TOK))
            x = x_ref[p * TOK : (p + 2) * TOK, :]
            for b in range(RANGES):
                target = jnp.where(owner == b, position, -1)
                pick = one_hot(target == iota((2 * MOST, 2 * TOK), 0))
                send_ref[hh * RANGES + b, p * MOST : (p + 2) * MOST, :] = dot(pick, x).astype(BF)
                found[b].append(dot(value, pick, NT).astype(BF))
        for b in range(RANGES):
            note = jnp.concatenate(found[b] + [zeros[:, n * MOST :]], axis=1)
            note_ref[hh * RANGES + b] = note
            if last:
                tile = [a[hh * RANGES + b] for a in notes] + [note]
                tile = tile + [zeros] * (4 - len(tile))
                send_ref[hh * RANGES + b, rows:, :] = jnp.concatenate(tile, axis=1)
        leave(send_ref, out_ref, sems, hh, HPZ).start()
    for hh in range(HPZ):
        leave(send_ref, out_ref, sems, hh, HPZ).wait()


def rank_rows(z, clusters):
    lanes = ZN * MOST

    def source(shape, dim):
        segment = iota(shape, dim) // MOST
        value = jnp.zeros(shape, I32)
        for i, d in enumerate(ORDER):
            value = jnp.where(segment == i, (z - d) & (ZN - 1), value)
        return value

    square = (lanes, lanes)
    from_z, to_z = source(square, 0), source(square, 1)
    same = from_z == to_z
    within = one_hot(same & (iota(square, 0) < iota(square, 1)))
    segment = one_hot(same)
    earlier = one_hot(from_z < to_z)
    hot = jnp.concatenate(
        [(clusters == float(c + 1)).astype(F32) for c in range(CLUSTER_GROUP)], axis=0
    )
    low = hot.astype(BF)
    side = CLUSTER_GROUP * PLANE
    row, col = iota((side, side), 0), iota((side, side), 1)
    row_c, col_c = lax.shift_right_logical(row, 4), lax.shift_right_logical(col, 4)
    before = one_hot((row_c == col_c) & (col < row))
    together = one_hot(row_c == col_c)
    lower = one_hot(col_c < row_c)
    total = dot(low, jnp.ones(square, BF))
    rank = (
        dot(low, within)
        + dot(before, dot(low, segment).astype(BF))
        + dot(together, dot(low, earlier).astype(BF))
        + dot(lower, total.astype(BF))
    )
    rank = jnp.sum((hot * rank).reshape(CLUSTER_GROUP, PLANE, lanes), axis=0)
    rank = jnp.where(clusters > 0.5, rank, float(NONE))
    return jnp.concatenate([rank[s : s + 1, :] for s in range(PLANE)], axis=1)


def place_kernel(place_ref, *refs):
    n = len(CHUNKS)
    recvs, (sorted_ref, tail_ref, head_ref, rank_ref, x_ref) = refs[:n], refs[n:]
    clusters = []
    at = 0
    for i, (chunk, recv_ref) in enumerate(zip(CHUNKS, recvs)):
        rows = len(chunk) * MOST
        tail = len(CHUNKS[-1]) * MOST
        clusters.append(
            jnp.concatenate(
                [
                    recvs[-1][s, tail:, i * WIDTH : i * WIDTH + rows].astype(F32)[0:1]
                    for s in range(PLANE)
                ],
                axis=0,
            )
        )
        for s in range(PLANE):
            x_ref[s * ZN * MOST + at : s * ZN * MOST + at + rows, :] = recv_ref[s, 0:rows, :]
        at += rows
    rank = rank_rows(place_ref[0], jnp.concatenate(clusters, axis=1)).astype(I32)
    rank_ref[...] = rank
    x = x_ref[...]
    step = 2
    for c in range(0, SPANS, step):
        pick = one_hot(rank == iota((step * SPAN, SLOTS), 0) + c * SPAN)
        sorted_ref[c : c + step] = dot(pick, x).astype(BF).reshape(step, SPAN, ALL)
    tail_ref[...] = sorted_ref[SPANS - 1, :, WIDTH : 3 * WIDTH]
    head_ref[...] = sorted_ref[0]


def span_math(q, g, k0, k1, v0, v1, keep):
    s0 = dot(k0, q, NT)
    s1 = dot(k1, q, NT)
    if keep is not None:
        s0 = jnp.where(keep, s0, -1e30)
    peak = jnp.maximum(
        jnp.max(s0, axis=0, keepdims=True), jnp.max(s1, axis=0, keepdims=True)
    )
    factor = SCALING * math.log2(math.e)
    p0 = jnp.exp2((s0 - peak) * factor)
    p1 = jnp.exp2((s1 - peak) * factor)
    inverse = 1.0 / (
        jnp.sum(p0, axis=0, keepdims=True) + jnp.sum(p1, axis=0, keepdims=True)
    )
    w0 = p0 * inverse
    w1 = p1 * inverse
    l0 = w0.astype(BF)
    l1 = w1.astype(BF)
    attended = (dot(v0, l0, TN) + dot(v1, l1, TN)).T.astype(BF)
    e0 = dot(v0, g, NT)
    e1 = dot(v1, g, NT)
    inner = jnp.sum(w0 * e0, axis=0, keepdims=True) + jnp.sum(w1 * e1, axis=0, keepdims=True)
    h0 = (w0 * (e0 - inner) * SCALING).astype(BF)
    h1 = (w1 * (e1 - inner) * SCALING).astype(BF)
    dq = (dot(k0, h0, TN) + dot(k1, h1, TN)).T.astype(BF)
    return attended, dq, dot(h0, q), dot(h1, q), dot(l0, g), dot(l1, g)


Q, K, V, G = (slice(t * WIDTH, (t + 1) * WIDTH) for t in range(4))


def main_kernel(in_ref, o_ref, part_ref, d_ref):
    d_ref[0] = jnp.zeros((SPAN, PAIR), F32)

    def one(c, carry):
        att, dq, dk0, dk1, dv0, dv1 = span_math(
            in_ref[c, :, Q], in_ref[c, :, G], in_ref[c - 1, :, K], in_ref[c, :, K],
            in_ref[c - 1, :, V], in_ref[c, :, V], None,
        )
        o_ref[c, :, Q] = att
        o_ref[c, :, K] = dq
        d_ref[c - 1, :, Q] += dk0
        d_ref[c - 1, :, K] += dv0
        d_ref[c, :, Q] = dk1
        d_ref[c, :, K] = dv1
        o_ref[c - 1, :, 2 * WIDTH :] = d_ref[c - 1].astype(BF)
        return carry

    for c in range(1, SPANS):
        one(c, 0)
    part_ref[0] = d_ref[0]
    part_ref[1] = d_ref[SPANS - 1]
    o_ref[0, :, 0 : 2 * WIDTH] = jnp.zeros((SPAN, 2 * WIDTH), BF)
    o_ref[SPANS - 1, :, 2 * WIDTH :] = jnp.zeros((SPAN, 2 * WIDTH), BF)


def pick_out(at, rank_ref, o, out_ref, send_ref, sems):
    col = row_to_col(rank_ref[...].astype(F32)).astype(I32)
    rows = send_ref.shape[1]
    step = PLANE // PICKS
    for p in range(PICKS):
        span = range(p * step, (p + 1) * step)
        part = jnp.concatenate(
            [
                col[i * ZN * MOST + j * MOST : i * ZN * MOST + (j + 1) * MOST, :]
                for i in span
                for j in at
            ],
            axis=0,
        )
        pick = one_hot(part == iota((step * rows, BLOCK), 1))
        send_ref[p * step : (p + 1) * step] = dot(pick, o).astype(BF).reshape(step, rows, ALL)
        leave(send_ref, out_ref, sems, p, PICKS).start()
    for p in range(PICKS):
        leave(send_ref, out_ref, sems, p, PICKS).wait()


def edge_kernel(
    at, place_ref, rank_ref, in_ref, tail_ref, head_ref, main_ref, part_ref,
    done_ref, out_ref, o_ref, send_ref, sems, done_sem,
):
    o_ref[SPAN:BLOCK, :] = main_ref[1:].reshape(BLOCK - SPAN, ALL)
    keep = jnp.broadcast_to(place_ref[1], (SPAN, SPAN)) > 0
    att, dq, _, dk1, _, dv1 = span_math(
        in_ref[0, :, Q], in_ref[0, :, G], tail_ref[:, Q], in_ref[0, :, K],
        tail_ref[:, K], in_ref[0, :, V], keep,
    )
    o_ref[0:SPAN, Q] = att
    o_ref[0:SPAN, K] = dq
    o_ref[0:SPAN, V] = (part_ref[0, :, Q] + dk1).astype(BF)
    o_ref[0:SPAN, G] = (part_ref[0, :, K] + dv1).astype(BF)
    end = SPANS - 1
    _, _, dk0, _, dv0, _ = span_math(
        head_ref[:, Q], head_ref[:, G], in_ref[end, :, K], head_ref[:, K],
        in_ref[end, :, V], head_ref[:, V], None,
    )
    o_ref[BLOCK - SPAN :, V] = (part_ref[1, :, Q] + dk0).astype(BF)
    o_ref[BLOCK - SPAN :, G] = (part_ref[1, :, K] + dv0).astype(BF)
    done = pltpu.make_async_copy(o_ref, done_ref, done_sem.at[0])
    done.start()
    pick_out(at, rank_ref, o_ref[...], out_ref, send_ref, sems)
    done.wait()


def pick_kernel(at, rank_ref, o_ref, *refs):
    pick_out(at, rank_ref, o_ref[...], *refs[-3:])


def unpack_kernel(places, *refs):
    codes, recv_ref, blocks = refs[: len(CHUNKS)], refs[len(CHUNKS)], refs[-len(places) :]
    for hh in range(HPZ):
        for p in range(0, len(places), 2):
            cols = []
            for j, (chunk, at) in enumerate(places[p : p + 2]):
                row = hh * len(CHUNKS[chunk]) + at
                mine = codes[chunk][row : row + 1, :]
                target = lax.shift_right_logical(mine, 5) * (2 * MOST) + (mine & (STRIDE - 1))
                cols.append(row_to_col((target + j * MOST).astype(F32)).astype(I32))
            col = jnp.concatenate(cols, axis=0)
            pick = one_hot(col == iota((2 * TOK, RANGES * 2 * MOST), 1))
            x = recv_ref[hh * RANGES : (hh + 1) * RANGES, p * MOST : (p + 2) * MOST, :]
            got = dot(pick, x.reshape(RANGES * 2 * MOST, ALL)).astype(BF)
            for j in range(2):
                for t in range(4):
                    blocks[p + j][t * TOK : (t + 1) * TOK, hh * WIDTH : (hh + 1) * WIDTH] = got[
                        j * TOK : (j + 1) * TOK, t * WIDTH : (t + 1) * WIDTH
                    ]


def mark_kernel(place_ref, *refs):
    mark_ref = refs[-1]
    mark_ref[...] = jnp.broadcast_to(place_ref[0], mark_ref.shape).astype(F32)


def join_kernel(place_ref, *refs):
    blocks, outs, sems = refs[:ZN], refs[ZN : ZN + 4], refs[ZN + 4]
    z = place_ref[0]
    copies = []
    for d in range(ZN):
        cols = pl.ds(pl.multiple_of(((z + d) & (ZN - 1)) * PAIR, PAIR), PAIR)
        for t in range(4):
            copies.append(
                pltpu.make_async_copy(
                    blocks[d].at[t * TOK : (t + 1) * TOK, :],
                    outs[t].at[:, cols],
                    sems.at[d * 4 + t],
                )
            )
    for copy in copies:
        copy.start()
    for copy in copies:
        copy.wait()


def exchange(array, groups):
    return lax.all_to_all(
        array, "seq", split_axis=0, concat_axis=0, axis_index_groups=groups, tiled=True
    )


def shift_owner(value, by):
    pairs = []
    for base in range(0, ZN * PLANE, RANGES):
        pairs += [(base + i, base + i + by) for i in range(RANGES) if 0 <= i + by < RANGES]
    return lax.ppermute(value, "seq", pairs)


def body(queries, keys, values, out_grad, cluster_ids):
    index = lax.axis_index("seq")
    place = jnp.stack([index // PLANE, index % RANGES]).astype(I32)
    hbm = pl.BlockSpec(memory_space=pltpu.HBM)
    anywhere = pl.BlockSpec(memory_space=pl.ANY)
    blocks = call(
        prep_kernel,
        [place, cluster_ids.T, queries, keys, values, out_grad],
        [out((4 * TOK + TILE, PAIR), BF)] * ZN,
        [pltpu.SemaphoreType.DMA((4 * ZN,))],
        specs={0: SMEM[0], 2: hbm, 3: hbm, 4: hbm, 5: hbm},
        limit=60,
    )
    moved = {0: blocks[0]}
    for d in ORDER:
        if d:
            moved[d] = lax.ppermute(blocks[d], "seq", z_pairs(d))
    codes, arrived, notes = [], [], []
    for i, chunk in enumerate(CHUNKS):
        n = len(chunk)
        rows = n * MOST
        extra = TILE if i == len(CHUNKS) - 1 else 0
        send, code, note = call(
            functools.partial(pack_kernel, i),
            [moved[d] for d in chunk] + notes,
            [
                out((PLANE, rows + extra, ALL), BF),
                out((HPZ * n, TOK), I32),
                out((PLANE, TILE, WIDTH), BF),
            ],
            [
                pltpu.VMEM((n * TOK, ALL), BF),
                pltpu.VMEM((PLANE, rows + extra, ALL), BF),
                pltpu.SemaphoreType.DMA((HPZ,)),
            ],
            flops=PACK_HINT[i],
            out_specs={0: hbm},
        )
        codes.append(code)
        notes.append(note)
        arrived.append(exchange(send, PLANES))
    rows_in, tail, head, rank = call(
        place_kernel,
        [place] + arrived,
        [
            out((SPANS, SPAN, ALL), BF),
            out((SPAN, PAIR), BF),
            out((SPAN, ALL), BF),
            out((1, SLOTS), I32),
        ],
        [pltpu.VMEM((SLOTS, ALL), BF)],
        flops=2 * BLOCK * SLOTS * ALL,
        specs=SMEM,
    )
    tail = shift_owner(tail, 1)
    head = shift_owner(head, -1)
    main, part = call(
        main_kernel,
        [rows_in],
        [out((SPANS, SPAN, ALL), BF), out((2, SPAN, PAIR), F32)],
        [pltpu.VMEM((SPANS, SPAN, PAIR), F32)],
        flops=14 * SPANS * SPAN * 2 * SPAN * WIDTH,
    )
    sends = []
    for step, chunk in enumerate(RETURNS):
        rows = len(chunk) * MOST
        at = tuple(ORDER.index(d) for d in chunk)
        send_shape = out((PLANE, rows, ALL), BF)
        stage = [pltpu.VMEM((PLANE, rows, ALL), BF), pltpu.SemaphoreType.DMA((PICKS,))]
        if step == 0:
            o, send = call(
                functools.partial(edge_kernel, at),
                [place, rank, rows_in, tail, head, main, part],
                [out((BLOCK, ALL), BF), send_shape],
                [pltpu.VMEM((BLOCK, ALL), BF)] + stage + [pltpu.SemaphoreType.DMA((1,))],
                flops=2 * BLOCK * PLANE * rows * ALL,
                specs=SMEM,
                out_specs={0: hbm, 1: hbm},
            )
        else:
            (send,) = call(
                functools.partial(pick_kernel, at),
                [rank, o],
                [send_shape],
                stage,
                flops=PICK_HINT[step],
                out_specs={0: hbm},
            )
        sends.append(send)
    back = {}
    waits = {}
    for step, chunk in enumerate(RETURNS):
        got = exchange(sends[step], PLANES)
        places = tuple(
            (i, c.index(d)) for d in chunk for i, c in enumerate(CHUNKS) if d in c
        )
        wait = waits.get(step, [])
        pieces = call(
            functools.partial(unpack_kernel, places),
            codes + [got] + wait,
            [out((4 * TOK, PAIR), BF)] * len(chunk),
            flops=UNPACK_HINT[step],
            specs={len(codes) + 1 + j: anywhere for j in range(len(wait))},
        )
        for d, piece in zip(chunk, pieces):
            back[d] = lax.ppermute(piece, "seq", z_pairs(-d)) if d else piece
        if step == 0:
            waits[1] = [back[d] for d in chunk] + [sends[2]]
        if step == 1:
            waits[2] = list(
                call(
                    mark_kernel,
                    [place] + [back[d] for d in SOON],
                    [out((8, WIDTH), F32)],
                    specs={0: SMEM[0]} | {j + 1: anywhere for j in range(len(SOON))},
                    flops=10**11,
                )
            )
    return call(
        join_kernel,
        [place] + [back[d] for d in range(ZN)],
        [out((TOK, ZN * PAIR), BF)] * 4,
        [pltpu.SemaphoreType.DMA((4 * ZN,))],
        specs=SMEM,
        out_specs={i: hbm for i in range(4)},
    )


def solution(mesh):
    spec = P("seq", "head")
    return jax.shard_map(
        body,
        mesh=mesh,
        in_specs=(spec,) * 5,
        out_specs=(spec,) * 4,
        check_vma=False,
    )
```

```python
import functools
import math

import jax
import jax.numpy as jnp
from jax import lax
from jax.experimental import pallas as pl
from jax.experimental.pallas import tpu as pltpu
from jax.sharding import PartitionSpec as P

WIDTH = 128
SPAN = 256
CLUSTER_GROUP = 16
RANGES = 8
TOK = 128
MOST = 24
ZN = 8
PLANE = 16
HPZ = 2
ALL = 4 * WIDTH
PAIR = HPZ * WIDTH
STRIDE = 32
SLOTS = PLANE * ZN * MOST
BLOCK = 2048
SPANS = BLOCK // SPAN
TILE = 16
PICKS = 2
NONE = 4095
SCALING = 1.0 / math.sqrt(WIDTH)
BF = jnp.bfloat16
F32 = jnp.float32
I32 = jnp.int32

CHUNKS = ((0, 1, 7, 2), (6, 3, 5, 4))
PICK_HINT = (0, 10**9, 10**9)
UNPACK_HINT = (10**9, 10**11, 10**9)
RETURNS = ((3, 5), (4, 2, 6, 7), (0, 1))
ORDER = sum(CHUNKS, ())
SOON = (2, 6)
PACK_HINT = (10**6, 10**11)
PLANES = [[z * PLANE + i for i in range(PLANE)] for z in range(ZN)]


def z_pairs(step):
    return [
        (z * PLANE + i, ((z + step) % ZN) * PLANE + i)
        for z in range(ZN)
        for i in range(PLANE)
    ]


def whole():
    return pl.BlockSpec(memory_space=pltpu.VMEM)


def call(kernel, ins, outs, scratch=(), flops=0, specs=None, out_specs=None, out_spec=None, limit=28, aliases=None):
    size = sum(math.prod(o.shape) * o.dtype.itemsize for o in outs)
    size += sum(math.prod(a.shape) * a.dtype.itemsize for a in ins)
    specs = specs or {}
    return pl.pallas_call(
        kernel,
        out_shape=tuple(
            pltpu.HBM(o.shape, o.dtype) if i in (out_specs or {}) else o
            for i, o in enumerate(outs)
        ),
        in_specs=[specs.get(i) or whole() for i in range(len(ins))],
        out_specs=tuple((out_specs or {}).get(i) or out_spec or whole() for i in range(len(outs))),
        scratch_shapes=list(scratch),
        input_output_aliases=aliases or {},
        cost_estimate=pl.CostEstimate(flops=flops, bytes_accessed=size, transcendentals=0),
        compiler_params=pltpu.CompilerParams(vmem_limit_bytes=limit * 1024 * 1024),
    )(*ins)


SMEM = {0: pl.BlockSpec(memory_space=pltpu.SMEM)}


def out(shape, dtype):
    return jax.ShapeDtypeStruct(shape, dtype)


def iota(shape, dim):
    return lax.broadcasted_iota(I32, shape, dim)


def one_hot(mask):
    return mask.astype(F32).astype(BF)


def row_to_col(row):
    eye = iota((128, 128), 0) == iota((128, 128), 1)
    parts = []
    for i in range(row.shape[1] // 128):
        piece = row[:, i * 128 : (i + 1) * 128]
        parts.append(jnp.sum(jnp.where(eye, piece, 0.0), axis=1, keepdims=True))
    return jnp.concatenate(parts, axis=0)


def dot(a, b, dims=((1,), (0,))):
    return lax.dot_general(a, b, (dims, ((), ())), preferred_element_type=F32)


NT = ((1,), (1,))
TN = ((0,), (0,))


def prep_kernel(ids_ref, *refs):
    arrays, blocks, stages, sems = refs[:4], refs[4 : 4 + ZN], refs[4 + ZN : 8 + ZN], refs[8 + ZN]
    z = lax.axis_index("seq") // PLANE
    copies = [pltpu.make_async_copy(arrays[t], stages[t], sems.at[t]) for t in range(4)]
    for copy in copies:
        copy.start()
    for d in range(ZN):
        at = ((z + d) & (ZN - 1)) * HPZ
        rows = [ids_ref[pl.ds(at + hh, 1), :] for hh in range(HPZ)]
        tile = jnp.concatenate(rows + [jnp.zeros((TILE - HPZ, TOK), I32)], axis=0)
        blocks[d][4 * TOK :, 0:TOK] = tile.astype(F32).astype(BF)
        blocks[d][4 * TOK :, TOK:] = jnp.zeros((TILE, PAIR - TOK), BF)
    for t in range(4):
        copies[t].wait()
        for d in range(ZN):
            cols = pl.ds(pl.multiple_of(((z + d) & (ZN - 1)) * PAIR, PAIR), PAIR)
            blocks[d][t * TOK : (t + 1) * TOK, :] = stages[t][:, cols]


def leave(stage_ref, out_ref, sems, i, n):
    size = PLANE // n
    part = slice(i * size, (i + 1) * size)
    return pltpu.make_async_copy(stage_ref.at[part], out_ref.at[part], sems.at[i])


def pack_kernel(index, *refs):
    chunk = CHUNKS[index]
    n = len(chunk)
    blocks, notes = refs[:n], refs[n : n + index]
    out_ref, code_ref, note_ref, x_ref, send_ref, sems = refs[-6:]
    last = index == len(CHUNKS) - 1
    rows = n * MOST
    ids = [blocks[i][4 * TOK :, 0:TOK].astype(F32) for i in range(n)]
    ids = jnp.concatenate(
        [ids[i][hh : hh + 1] for hh in range(HPZ) for i in range(n)], axis=0
    ).astype(I32)
    group = lax.shift_right_logical(ids, 4)
    local = ((ids & (CLUSTER_GROUP - 1)) + 1).astype(F32).astype(BF)
    tri = one_hot(iota((TOK, TOK), 0) < iota((TOK, TOK), 1))
    slot = jnp.zeros(ids.shape, F32)
    for b in range(RANGES):
        hot = (group == b).astype(F32)
        slot = slot + hot * dot(hot.astype(BF), tri)
    code = group * STRIDE + slot.astype(I32)
    code_ref[...] = code
    zeros = jnp.zeros((TILE, WIDTH), BF)
    for hh in range(HPZ):
        for i in range(n):
            for t in range(4):
                x_ref[i * TOK : (i + 1) * TOK, t * WIDTH : (t + 1) * WIDTH] = blocks[i][
                    t * TOK : (t + 1) * TOK, hh * WIDTH : (hh + 1) * WIDTH
                ]
        pairs = []
        for p in range(0, n, 2):
            mine = [hh * n + p, hh * n + p + 1]
            position = jnp.concatenate(
                [(code[i : i + 1] & (STRIDE - 1)) + j * MOST for j, i in enumerate(mine)], axis=1
            )
            owner = jnp.concatenate([group[i : i + 1] for i in mine], axis=1)
            value = jnp.concatenate([local[i : i + 1] for i in mine], axis=1)
            pairs.append((position, owner, jnp.broadcast_to(value, (TILE, 2 * TOK))))
        for b in range(RANGES):
            to = hh * RANGES + b
            found = []
            for p, (position, owner, value) in enumerate(pairs):
                target = jnp.where(owner == b, position, -1)
                pick = one_hot(target == iota((2 * MOST, 2 * TOK), 0))
                x = x_ref[p * 2 * TOK : (p + 1) * 2 * TOK, :]
                send_ref[to, p * 2 * MOST : (p + 1) * 2 * MOST, :] = dot(pick, x).astype(BF)
                found.append(dot(value, pick, NT).astype(BF))
            note = jnp.concatenate(found + [zeros[:, n * MOST :]], axis=1)
            note_ref[to] = note
            if last:
                tile = [a[to] for a in notes] + [note]
                tile = tile + [zeros] * (4 - len(tile))
                send_ref[to, rows:, :] = jnp.concatenate(tile, axis=1)
            if b % 2:
                leave(send_ref, out_ref, sems, to // 2, RANGES).start()
    for i in range(RANGES):
        leave(send_ref, out_ref, sems, i, RANGES).wait()


def rank_rows(z, clusters):
    lanes = ZN * MOST

    def source(shape, dim):
        segment = iota(shape, dim) // MOST
        value = jnp.zeros(shape, I32)
        for i, d in enumerate(ORDER):
            value = jnp.where(segment == i, (z - d) & (ZN - 1), value)
        return value

    square = (lanes, lanes)
    from_z, to_z = source(square, 0), source(square, 1)
    same = from_z == to_z
    within = one_hot(same & (iota(square, 0) < iota(square, 1)))
    segment = one_hot(same)
    earlier = one_hot(from_z < to_z)
    hot = jnp.concatenate(
        [(clusters == float(c + 1)).astype(F32) for c in range(CLUSTER_GROUP)], axis=0
    )
    low = hot.astype(BF)
    side = CLUSTER_GROUP * PLANE
    row, col = iota((side, side), 0), iota((side, side), 1)
    row_c, col_c = lax.shift_right_logical(row, 4), lax.shift_right_logical(col, 4)
    before = one_hot((row_c == col_c) & (col < row))
    together = one_hot(row_c == col_c)
    lower = one_hot(col_c < row_c)
    total = dot(low, jnp.ones(square, BF))
    rank = (
        dot(low, within)
        + dot(before, dot(low, segment).astype(BF))
        + dot(together, dot(low, earlier).astype(BF))
        + dot(lower, total.astype(BF))
    )
    rank = jnp.sum((hot * rank).reshape(CLUSTER_GROUP, PLANE, lanes), axis=0)
    rank = jnp.where(clusters > 0.5, rank, float(NONE))
    return rank


def place_kernel(place_ref, *refs):
    n = len(CHUNKS)
    recvs, (sorted_ref, tail_ref, head_ref, rank_ref) = refs[:n], refs[n:]
    clusters = []
    end = len(CHUNKS[-1]) * MOST
    for i, chunk in enumerate(CHUNKS):
        rows = len(chunk) * MOST
        clusters.append(
            jnp.concatenate(
                [
                    recvs[-1][s, end:, i * WIDTH : i * WIDTH + rows].astype(F32)[0:1]
                    for s in range(PLANE)
                ],
                axis=0,
            )
        )
    rank = rank_rows(place_ref[0], jnp.concatenate(clusters, axis=1))
    rank_ref[...] = jnp.concatenate(
        [rank[s : s + 1, :] for s in range(PLANE)], axis=1
    ).astype(I32)
    parts = []
    at = 0
    for chunk, recv_ref in zip(CHUNKS, recvs):
        rows = len(chunk) * MOST
        row = jnp.concatenate([rank[s : s + 1, at : at + rows] for s in range(PLANE)], axis=1)
        parts.append((row.astype(I32), recv_ref[:, 0:rows, :].reshape(PLANE * rows, ALL)))
        at += rows
    step = 2
    for c in range(0, SPANS, step):
        got = jnp.zeros((step * SPAN, ALL), F32)
        for row, x in parts:
            pick = one_hot(row == iota((step * SPAN, row.shape[1]), 0) + c * SPAN)
            got = got + dot(pick, x)
        sorted_ref[c : c + step] = got.astype(BF).reshape(step, SPAN, ALL)
    tail_ref[...] = sorted_ref[SPANS - 1, :, WIDTH : 3 * WIDTH]
    head_ref[...] = sorted_ref[0]


def span_math(q, g, k0, k1, v0, v1, keep):
    s0 = dot(k0, q, NT)
    s1 = dot(k1, q, NT)
    if keep is not None:
        s0 = jnp.where(keep, s0, -1e30)
    peak = jnp.maximum(
        jnp.max(s0, axis=0, keepdims=True), jnp.max(s1, axis=0, keepdims=True)
    )
    factor = SCALING * math.log2(math.e)
    p0 = jnp.exp2((s0 - peak) * factor)
    p1 = jnp.exp2((s1 - peak) * factor)
    inverse = 1.0 / (
        jnp.sum(p0, axis=0, keepdims=True) + jnp.sum(p1, axis=0, keepdims=True)
    )
    w0 = p0 * inverse
    w1 = p1 * inverse
    l0 = w0.astype(BF)
    l1 = w1.astype(BF)
    attended = (dot(v0, l0, TN) + dot(v1, l1, TN)).T.astype(BF)
    e0 = dot(v0, g, NT)
    e1 = dot(v1, g, NT)
    inner = jnp.sum(w0 * e0, axis=0, keepdims=True) + jnp.sum(w1 * e1, axis=0, keepdims=True)
    h0 = (w0 * (e0 - inner) * SCALING).astype(BF)
    h1 = (w1 * (e1 - inner) * SCALING).astype(BF)
    dq = (dot(k0, h0, TN) + dot(k1, h1, TN)).T.astype(BF)
    return attended, dq, dot(h0, q), dot(h1, q), dot(l0, g), dot(l1, g)


Q, K, V, G = (slice(t * WIDTH, (t + 1) * WIDTH) for t in range(4))


def main_kernel(in_ref, o_ref, part_ref):
    held = (jnp.zeros((SPAN, WIDTH), F32),) * 2
    for c in range(1, SPANS):
        att, dq, dk0, dk1, dv0, dv1 = span_math(
            in_ref[c, :, Q], in_ref[c, :, G], in_ref[c - 1, :, K], in_ref[c, :, K],
            in_ref[c - 1, :, V], in_ref[c, :, V], None,
        )
        o_ref[c, :, Q] = att
        o_ref[c, :, K] = dq
        dk, dv = held[0] + dk0, held[1] + dv0
        if c == 1:
            part_ref[0, :, Q] = dk
            part_ref[0, :, K] = dv
        o_ref[c - 1, :, V] = dk.astype(BF)
        o_ref[c - 1, :, G] = dv.astype(BF)
        held = (dk1, dv1)
    part_ref[1, :, Q] = held[0]
    part_ref[1, :, K] = held[1]
    o_ref[0, :, 0 : 2 * WIDTH] = jnp.zeros((SPAN, 2 * WIDTH), BF)
    o_ref[SPANS - 1, :, 2 * WIDTH :] = jnp.zeros((SPAN, 2 * WIDTH), BF)


def pick_out(at, rank_ref, o, out_ref, send_ref, sems):
    col = row_to_col(rank_ref[...].astype(F32)).astype(I32)
    rows = send_ref.shape[1]
    step = PLANE // PICKS
    for p in range(PICKS):
        span = range(p * step, (p + 1) * step)
        part = jnp.concatenate(
            [
                col[i * ZN * MOST + j * MOST : i * ZN * MOST + (j + 1) * MOST, :]
                for i in span
                for j in at
            ],
            axis=0,
        )
        pick = one_hot(part == iota((step * rows, BLOCK), 1))
        send_ref[p * step : (p + 1) * step] = dot(pick, o).astype(BF).reshape(step, rows, ALL)
        leave(send_ref, out_ref, sems, p, PICKS).start()
    for p in range(PICKS):
        leave(send_ref, out_ref, sems, p, PICKS).wait()


def edge_kernel(
    at, place_ref, rank_ref, in_ref, tail_ref, head_ref, main_ref, part_ref,
    done_ref, out_ref, o_ref, send_ref, sems, done_sem,
):
    o_ref[SPAN:BLOCK, :] = main_ref[1:].reshape(BLOCK - SPAN, ALL)
    keep = jnp.broadcast_to(place_ref[1], (SPAN, SPAN)) > 0
    att, dq, _, dk1, _, dv1 = span_math(
        in_ref[0, :, Q], in_ref[0, :, G], tail_ref[:, Q], in_ref[0, :, K],
        tail_ref[:, K], in_ref[0, :, V], keep,
    )
    o_ref[0:SPAN, Q] = att
    o_ref[0:SPAN, K] = dq
    o_ref[0:SPAN, V] = (part_ref[0, :, Q] + dk1).astype(BF)
    o_ref[0:SPAN, G] = (part_ref[0, :, K] + dv1).astype(BF)
    end = SPANS - 1
    _, _, dk0, _, dv0, _ = span_math(
        head_ref[:, Q], head_ref[:, G], in_ref[end, :, K], head_ref[:, K],
        in_ref[end, :, V], head_ref[:, V], None,
    )
    o_ref[BLOCK - SPAN :, V] = (part_ref[1, :, Q] + dk0).astype(BF)
    o_ref[BLOCK - SPAN :, G] = (part_ref[1, :, K] + dv0).astype(BF)
    done = pltpu.make_async_copy(o_ref, done_ref, done_sem.at[0])
    done.start()
    pick_out(at, rank_ref, o_ref[...], out_ref, send_ref, sems)
    done.wait()


def pick_kernel(at, rank_ref, o_ref, *refs):
    pick_out(at, rank_ref, o_ref[...], *refs[-3:])


def unpack_kernel(places, *refs):
    codes, recv_ref, blocks = refs[: len(CHUNKS)], refs[len(CHUNKS)], refs[-len(places) :]
    for hh in range(HPZ):
        for p in range(0, len(places), 2):
            cols = []
            for j, (chunk, at) in enumerate(places[p : p + 2]):
                row = hh * len(CHUNKS[chunk]) + at
                mine = codes[chunk][row : row + 1, :]
                target = lax.shift_right_logical(mine, 5) * (2 * MOST) + (mine & (STRIDE - 1))
                cols.append(row_to_col((target + j * MOST).astype(F32)).astype(I32))
            col = jnp.concatenate(cols, axis=0)
            pick = one_hot(col == iota((2 * TOK, RANGES * 2 * MOST), 1))
            x = recv_ref[hh * RANGES : (hh + 1) * RANGES, p * MOST : (p + 2) * MOST, :]
            got = dot(pick, x.reshape(RANGES * 2 * MOST, ALL)).astype(BF)
            for j in range(2):
                for t in range(4):
                    blocks[p + j][t * TOK : (t + 1) * TOK, hh * WIDTH : (hh + 1) * WIDTH] = got[
                        j * TOK : (j + 1) * TOK, t * WIDTH : (t + 1) * WIDTH
                    ]


def mark_kernel(place_ref, *refs):
    mark_ref = refs[-1]
    mark_ref[...] = jnp.broadcast_to(place_ref[0], mark_ref.shape).astype(F32)


def join_kernel(place_ref, *refs):
    blocks, outs, sems = refs[:ZN], refs[ZN : ZN + 4], refs[ZN + 4]
    z = place_ref[0]
    copies = []
    for d in range(ZN):
        cols = pl.ds(pl.multiple_of(((z + d) & (ZN - 1)) * PAIR, PAIR), PAIR)
        for t in range(4):
            copies.append(
                pltpu.make_async_copy(
                    blocks[d].at[t * TOK : (t + 1) * TOK, :],
                    outs[t].at[:, cols],
                    sems.at[d * 4 + t],
                )
            )
    for copy in copies:
        copy.start()
    for copy in copies:
        copy.wait()


def exchange(array, groups):
    return lax.all_to_all(
        array, "seq", split_axis=0, concat_axis=0, axis_index_groups=groups, tiled=True
    )


def shift_owner(value, by):
    pairs = []
    for base in range(0, ZN * PLANE, RANGES):
        pairs += [(base + i, base + i + by) for i in range(RANGES) if 0 <= i + by < RANGES]
    return lax.ppermute(value, "seq", pairs)


def body(queries, keys, values, out_grad, cluster_ids):
    index = lax.axis_index("seq")
    place = jnp.stack([index // PLANE, index % RANGES]).astype(I32)
    hbm = pl.BlockSpec(memory_space=pltpu.HBM)
    anywhere = pl.BlockSpec(memory_space=pl.ANY)
    blocks = call(
        prep_kernel,
        [cluster_ids.T, queries, keys, values, out_grad],
        [out((4 * TOK + TILE, PAIR), BF)] * ZN,
        [pltpu.VMEM((TOK, ZN * PAIR), BF)] * 4 + [pltpu.SemaphoreType.DMA((4,))],
        specs={1: hbm, 2: hbm, 3: hbm, 4: hbm},
        limit=60,
    )
    moved = {0: blocks[0]}
    for d in ORDER:
        if d:
            moved[d] = lax.ppermute(blocks[d], "seq", z_pairs(d))
    codes, arrived, notes = [], [], []
    for i, chunk in enumerate(CHUNKS):
        n = len(chunk)
        rows = n * MOST
        extra = TILE if i == len(CHUNKS) - 1 else 0
        send, code, note = call(
            functools.partial(pack_kernel, i),
            [moved[d] for d in chunk] + notes,
            [
                out((PLANE, rows + extra, ALL), BF),
                out((HPZ * n, TOK), I32),
                out((PLANE, TILE, WIDTH), BF),
            ],
            [
                pltpu.VMEM((n * TOK, ALL), BF),
                pltpu.VMEM((PLANE, rows + extra, ALL), BF),
                pltpu.SemaphoreType.DMA((RANGES,)),
            ],
            flops=PACK_HINT[i],
            out_specs={0: hbm},
        )
        codes.append(code)
        notes.append(note)
        arrived.append(exchange(send, PLANES))
    rows_in, tail, head, rank = call(
        place_kernel,
        [place] + arrived,
        [
            out((SPANS, SPAN, ALL), BF),
            out((SPAN, PAIR), BF),
            out((SPAN, ALL), BF),
            out((1, SLOTS), I32),
        ],
        flops=2 * BLOCK * SLOTS * ALL,
        specs=SMEM,
    )
    tail = shift_owner(tail, 1)
    head = shift_owner(head, -1)
    main, part = call(
        main_kernel,
        [rows_in],
        [out((SPANS, SPAN, ALL), BF), out((2, SPAN, PAIR), F32)],
        flops=14 * SPANS * SPAN * 2 * SPAN * WIDTH,
    )
    sends = []
    for step, chunk in enumerate(RETURNS):
        rows = len(chunk) * MOST
        at = tuple(ORDER.index(d) for d in chunk)
        send_shape = out((PLANE, rows, ALL), BF)
        stage = [pltpu.VMEM((PLANE, rows, ALL), BF), pltpu.SemaphoreType.DMA((PICKS,))]
        if step == 0:
            o, send = call(
                functools.partial(edge_kernel, at),
                [place, rank, rows_in, tail, head, main, part],
                [out((BLOCK, ALL), BF), send_shape],
                [pltpu.VMEM((BLOCK, ALL), BF)] + stage + [pltpu.SemaphoreType.DMA((1,))],
                flops=2 * BLOCK * PLANE * rows * ALL,
                specs=SMEM,
                out_specs={0: hbm, 1: hbm},
            )
        else:
            (send,) = call(
                functools.partial(pick_kernel, at),
                [rank, o],
                [send_shape],
                stage,
                flops=PICK_HINT[step],
                out_specs={0: hbm},
            )
        sends.append(send)
    back = {}
    waits = {}
    for step, chunk in enumerate(RETURNS):
        got = exchange(sends[step], PLANES)
        places = tuple(
            (i, c.index(d)) for d in chunk for i, c in enumerate(CHUNKS) if d in c
        )
        wait = waits.get(step, [])
        pieces = call(
            functools.partial(unpack_kernel, places),
            codes + [got] + wait,
            [out((4 * TOK, PAIR), BF)] * len(chunk),
            flops=UNPACK_HINT[step],
            specs={len(codes) + 1 + j: anywhere for j in range(len(wait))},
        )
        for d, piece in zip(chunk, pieces):
            back[d] = lax.ppermute(piece, "seq", z_pairs(-d)) if d else piece
        if step == 0:
            waits[1] = [back[d] for d in chunk] + [sends[2]]
        if step == 1:
            waits[2] = list(
                call(
                    mark_kernel,
                    [place] + [back[d] for d in SOON],
                    [out((8, WIDTH), F32)],
                    specs={0: SMEM[0]} | {j + 1: anywhere for j in range(len(SOON))},
                    flops=10**11,
                )
            )
    return call(
        join_kernel,
        [place] + [back[d] for d in range(ZN)],
        [out((TOK, ZN * PAIR), BF)] * 4,
        [pltpu.SemaphoreType.DMA((4 * ZN,))],
        specs=SMEM,
        out_specs={i: hbm for i in range(4)},
    )


def solution(mesh):
    spec = P("seq", "head")
    return jax.shard_map(
        body,
        mesh=mesh,
        in_specs=(spec,) * 5,
        out_specs=(spec,) * 4,
        check_vma=False,
    )
```

```python
import functools
import math

import jax
import jax.numpy as jnp
from jax import lax
from jax.experimental import pallas as pl
from jax.experimental.pallas import tpu as pltpu
from jax.sharding import PartitionSpec as P

WIDTH = 128
SPAN = 256
CLUSTER_GROUP = 16
RANGES = 8
TOK = 128
MOST = 24
ZN = 8
PLANE = 16
HPZ = 2
ALL = 4 * WIDTH
PAIR = HPZ * WIDTH
STRIDE = 32
SLOTS = PLANE * ZN * MOST
BLOCK = 2048
SPANS = BLOCK // SPAN
TILE = 16
PICKS = 2
NONE = 4095
SCALING = 1.0 / math.sqrt(WIDTH)
BF = jnp.bfloat16
F32 = jnp.float32
I32 = jnp.int32

CHUNKS = ((0, 1, 7, 2), (6, 3, 5, 4))
PICK_HINT = (0, 10**9, 10**9)
UNPACK_HINT = (10**9, 10**11, 10**9)
RETURNS = ((3, 5), (4, 2, 6, 7), (0, 1))
ORDER = sum(CHUNKS, ())
SOON = (2, 6)
PACK_HINT = (10**6, 10**11)
PLANES = [[z * PLANE + i for i in range(PLANE)] for z in range(ZN)]


def z_pairs(step):
    return [
        (z * PLANE + i, ((z + step) % ZN) * PLANE + i)
        for z in range(ZN)
        for i in range(PLANE)
    ]


def whole():
    return pl.BlockSpec(memory_space=pltpu.VMEM)


def call(kernel, ins, outs, scratch=(), flops=0, specs=None, out_specs=None, out_spec=None, limit=28, aliases=None):
    size = sum(math.prod(o.shape) * o.dtype.itemsize for o in outs)
    size += sum(math.prod(a.shape) * a.dtype.itemsize for a in ins)
    specs = specs or {}
    return pl.pallas_call(
        kernel,
        out_shape=tuple(
            pltpu.HBM(o.shape, o.dtype) if i in (out_specs or {}) else o
            for i, o in enumerate(outs)
        ),
        in_specs=[specs.get(i) or whole() for i in range(len(ins))],
        out_specs=tuple((out_specs or {}).get(i) or out_spec or whole() for i in range(len(outs))),
        scratch_shapes=list(scratch),
        input_output_aliases=aliases or {},
        cost_estimate=pl.CostEstimate(flops=flops, bytes_accessed=size, transcendentals=0),
        compiler_params=pltpu.CompilerParams(vmem_limit_bytes=limit * 1024 * 1024),
    )(*ins)


SMEM = {0: pl.BlockSpec(memory_space=pltpu.SMEM)}


def out(shape, dtype):
    return jax.ShapeDtypeStruct(shape, dtype)


def iota(shape, dim):
    return lax.broadcasted_iota(I32, shape, dim)


def one_hot(mask):
    return mask.astype(F32).astype(BF)


def row_to_col(row):
    eye = iota((128, 128), 0) == iota((128, 128), 1)
    parts = []
    for i in range(row.shape[1] // 128):
        piece = row[:, i * 128 : (i + 1) * 128]
        parts.append(jnp.sum(jnp.where(eye, piece, 0.0), axis=1, keepdims=True))
    return jnp.concatenate(parts, axis=0)


def dot(a, b, dims=((1,), (0,))):
    return lax.dot_general(a, b, (dims, ((), ())), preferred_element_type=F32)


NT = ((1,), (1,))
TN = ((0,), (0,))


def prep_kernel(ids_ref, *refs):
    arrays, blocks, stages, sems = refs[:4], refs[4 : 4 + ZN], refs[4 + ZN : 8 + ZN], refs[8 + ZN]
    z = lax.axis_index("seq") // PLANE
    copies = [pltpu.make_async_copy(arrays[t], stages[t], sems.at[t]) for t in range(4)]
    for copy in copies:
        copy.start()
    for d in range(ZN):
        at = ((z + d) & (ZN - 1)) * HPZ
        rows = [ids_ref[pl.ds(at + hh, 1), :] for hh in range(HPZ)]
        tile = jnp.concatenate(rows + [jnp.zeros((TILE - HPZ, TOK), I32)], axis=0)
        blocks[d][4 * TOK :, 0:TOK] = tile.astype(F32).astype(BF)
        blocks[d][4 * TOK :, TOK:] = jnp.zeros((TILE, PAIR - TOK), BF)
    for t in range(4):
        copies[t].wait()
        for d in range(ZN):
            cols = pl.ds(pl.multiple_of(((z + d) & (ZN - 1)) * PAIR, PAIR), PAIR)
            blocks[d][t * TOK : (t + 1) * TOK, :] = stages[t][:, cols]


def leave(stage_ref, out_ref, sems, i, n):
    size = PLANE // n
    part = slice(i * size, (i + 1) * size)
    return pltpu.make_async_copy(stage_ref.at[part], out_ref.at[part], sems.at[i])


def pack_kernel(index, *refs):
    chunk = CHUNKS[index]
    n = len(chunk)
    blocks, notes = refs[:n], refs[n : n + index]
    out_ref, code_ref, note_ref, x_ref, send_ref, sems = refs[-6:]
    last = index == len(CHUNKS) - 1
    rows = n * MOST
    ids = [blocks[i][4 * TOK :, 0:TOK].astype(F32) for i in range(n)]
    ids = jnp.concatenate(
        [ids[i][hh : hh + 1] for hh in range(HPZ) for i in range(n)], axis=0
    ).astype(I32)
    group = lax.shift_right_logical(ids, 4)
    local = ((ids & (CLUSTER_GROUP - 1)) + 1).astype(F32).astype(BF)
    tri = one_hot(iota((TOK, TOK), 0) < iota((TOK, TOK), 1))
    slot = jnp.zeros(ids.shape, F32)
    for b in range(RANGES):
        hot = (group == b).astype(F32)
        slot = slot + hot * dot(hot.astype(BF), tri)
    code = group * STRIDE + slot.astype(I32)
    code_ref[...] = code
    zeros = jnp.zeros((TILE, WIDTH), BF)
    for hh in range(HPZ):
        for i in range(n):
            for t in range(4):
                x_ref[i * TOK : (i + 1) * TOK, t * WIDTH : (t + 1) * WIDTH] = blocks[i][
                    t * TOK : (t + 1) * TOK, hh * WIDTH : (hh + 1) * WIDTH
                ]
        pairs = []
        for p in range(0, n, 2):
            mine = [hh * n + p, hh * n + p + 1]
            position = jnp.concatenate(
                [(code[i : i + 1] & (STRIDE - 1)) + j * MOST for j, i in enumerate(mine)], axis=1
            )
            owner = jnp.concatenate([group[i : i + 1] for i in mine], axis=1)
            value = jnp.concatenate([local[i : i + 1] for i in mine], axis=1)
            pairs.append((position, owner, jnp.broadcast_to(value, (TILE, 2 * TOK))))
        for b in range(RANGES):
            to = hh * RANGES + b
            found = []
            for p, (position, owner, value) in enumerate(pairs):
                target = jnp.where(owner == b, position, -1)
                pick = one_hot(target == iota((2 * MOST, 2 * TOK), 0))
                x = x_ref[p * 2 * TOK : (p + 1) * 2 * TOK, :]
                send_ref[to, p * 2 * MOST : (p + 1) * 2 * MOST, :] = dot(pick, x).astype(BF)
                found.append(dot(value, pick, NT).astype(BF))
            note = jnp.concatenate(found + [zeros[:, n * MOST :]], axis=1)
            note_ref[to] = note
            if last:
                tile = [a[to] for a in notes] + [note]
                tile = tile + [zeros] * (4 - len(tile))
                send_ref[to, rows:, :] = jnp.concatenate(tile, axis=1)
            if b % 2:
                leave(send_ref, out_ref, sems, to // 2, RANGES).start()
    for i in range(RANGES):
        leave(send_ref, out_ref, sems, i, RANGES).wait()


def rank_rows(z, clusters):
    lanes = ZN * MOST

    def source(shape, dim):
        segment = iota(shape, dim) // MOST
        value = jnp.zeros(shape, I32)
        for i, d in enumerate(ORDER):
            value = jnp.where(segment == i, (z - d) & (ZN - 1), value)
        return value

    square = (lanes, lanes)
    from_z, to_z = source(square, 0), source(square, 1)
    same = from_z == to_z
    within = one_hot(same & (iota(square, 0) < iota(square, 1)))
    segment = one_hot(same)
    earlier = one_hot(from_z < to_z)
    hot = jnp.concatenate(
        [(clusters == float(c + 1)).astype(F32) for c in range(CLUSTER_GROUP)], axis=0
    )
    low = hot.astype(BF)
    side = CLUSTER_GROUP * PLANE
    row, col = iota((side, side), 0), iota((side, side), 1)
    row_c, col_c = lax.shift_right_logical(row, 4), lax.shift_right_logical(col, 4)
    before = one_hot((row_c == col_c) & (col < row))
    together = one_hot(row_c == col_c)
    lower = one_hot(col_c < row_c)
    total = dot(low, jnp.ones(square, BF))
    rank = (
        dot(low, within)
        + dot(before, dot(low, segment).astype(BF))
        + dot(together, dot(low, earlier).astype(BF))
        + dot(lower, total.astype(BF))
    )
    rank = jnp.sum((hot * rank).reshape(CLUSTER_GROUP, PLANE, lanes), axis=0)
    rank = jnp.where(clusters > 0.5, rank, float(NONE))
    return rank


def place_kernel(place_ref, *refs):
    n = len(CHUNKS)
    recvs, (sorted_ref, tail_ref, head_ref, rank_ref) = refs[:n], refs[n:]
    clusters = []
    end = len(CHUNKS[-1]) * MOST
    for i, chunk in enumerate(CHUNKS):
        rows = len(chunk) * MOST
        clusters.append(
            jnp.concatenate(
                [
                    recvs[-1][s, end:, i * WIDTH : i * WIDTH + rows].astype(F32)[0:1]
                    for s in range(PLANE)
                ],
                axis=0,
            )
        )
    rank = rank_rows(place_ref[0], jnp.concatenate(clusters, axis=1))
    rank_ref[...] = jnp.concatenate(
        [rank[s : s + 1, :] for s in range(PLANE)], axis=1
    ).astype(I32)
    parts = []
    at = 0
    for chunk, recv_ref in zip(CHUNKS, recvs):
        rows = len(chunk) * MOST
        row = jnp.concatenate([rank[s : s + 1, at : at + rows] for s in range(PLANE)], axis=1)
        parts.append((row.astype(I32), recv_ref[:, 0:rows, :].reshape(PLANE * rows, ALL)))
        at += rows
    step = 2
    for c in range(0, SPANS, step):
        got = jnp.zeros((step * SPAN, ALL), F32)
        for row, x in parts:
            pick = one_hot(row == iota((step * SPAN, row.shape[1]), 0) + c * SPAN)
            got = got + dot(pick, x)
        sorted_ref[c : c + step] = got.astype(BF).reshape(step, SPAN, ALL)
    tail_ref[...] = sorted_ref[SPANS - 1, :, WIDTH : 3 * WIDTH]
    head_ref[...] = sorted_ref[0]


def span_math(q, g, k0, k1, v0, v1, keep):
    s0 = dot(k0, q, NT)
    s1 = dot(k1, q, NT)
    if keep is not None:
        s0 = jnp.where(keep, s0, -1e30)
    peak = jnp.maximum(
        jnp.max(s0, axis=0, keepdims=True), jnp.max(s1, axis=0, keepdims=True)
    )
    factor = SCALING * math.log2(math.e)
    p0 = jnp.exp2((s0 - peak) * factor)
    p1 = jnp.exp2((s1 - peak) * factor)
    inverse = 1.0 / (
        jnp.sum(p0, axis=0, keepdims=True) + jnp.sum(p1, axis=0, keepdims=True)
    )
    w0 = p0 * inverse
    w1 = p1 * inverse
    l0 = w0.astype(BF)
    l1 = w1.astype(BF)
    attended = (dot(v0, l0, TN) + dot(v1, l1, TN)).T.astype(BF)
    e0 = dot(v0, g, NT)
    e1 = dot(v1, g, NT)
    inner = jnp.sum(w0 * e0, axis=0, keepdims=True) + jnp.sum(w1 * e1, axis=0, keepdims=True)
    h0 = (w0 * (e0 - inner) * SCALING).astype(BF)
    h1 = (w1 * (e1 - inner) * SCALING).astype(BF)
    dq = (dot(k0, h0, TN) + dot(k1, h1, TN)).T.astype(BF)
    return attended, dq, dot(h0, q), dot(h1, q), dot(l0, g), dot(l1, g)


Q, K, V, G = (slice(t * WIDTH, (t + 1) * WIDTH) for t in range(4))


def main_kernel(in_ref, o_ref, part_ref):
    held = (jnp.zeros((SPAN, WIDTH), F32),) * 2
    for c in range(1, SPANS):
        att, dq, dk0, dk1, dv0, dv1 = span_math(
            in_ref[c, :, Q], in_ref[c, :, G], in_ref[c - 1, :, K], in_ref[c, :, K],
            in_ref[c - 1, :, V], in_ref[c, :, V], None,
        )
        o_ref[c, :, Q] = att
        o_ref[c, :, K] = dq
        dk, dv = held[0] + dk0, held[1] + dv0
        if c == 1:
            part_ref[0, :, Q] = dk
            part_ref[0, :, K] = dv
        o_ref[c - 1, :, V] = dk.astype(BF)
        o_ref[c - 1, :, G] = dv.astype(BF)
        held = (dk1, dv1)
    part_ref[1, :, Q] = held[0]
    part_ref[1, :, K] = held[1]
    o_ref[0, :, 0 : 2 * WIDTH] = jnp.zeros((SPAN, 2 * WIDTH), BF)
    o_ref[SPANS - 1, :, 2 * WIDTH :] = jnp.zeros((SPAN, 2 * WIDTH), BF)


def pick_out(at, rank_ref, o, out_ref, send_ref, sems):
    col = row_to_col(rank_ref[...].astype(F32)).astype(I32)
    rows = send_ref.shape[1]
    step = PLANE // PICKS
    for p in range(PICKS):
        span = range(p * step, (p + 1) * step)
        part = jnp.concatenate(
            [
                col[i * ZN * MOST + j * MOST : i * ZN * MOST + (j + 1) * MOST, :]
                for i in span
                for j in at
            ],
            axis=0,
        )
        pick = one_hot(part == iota((step * rows, BLOCK), 1))
        send_ref[p * step : (p + 1) * step] = dot(pick, o).astype(BF).reshape(step, rows, ALL)
        leave(send_ref, out_ref, sems, p, PICKS).start()
    for p in range(PICKS):
        leave(send_ref, out_ref, sems, p, PICKS).wait()


def edge_kernel(
    at, place_ref, rank_ref, in_ref, tail_ref, head_ref, main_ref, part_ref,
    done_ref, out_ref, o_ref, send_ref, sems, done_sem,
):
    o_ref[SPAN:BLOCK, :] = main_ref[1:].reshape(BLOCK - SPAN, ALL)
    keep = jnp.broadcast_to(place_ref[1], (SPAN, SPAN)) > 0
    att, dq, _, dk1, _, dv1 = span_math(
        in_ref[0, :, Q], in_ref[0, :, G], tail_ref[:, Q], in_ref[0, :, K],
        tail_ref[:, K], in_ref[0, :, V], keep,
    )
    o_ref[0:SPAN, Q] = att
    o_ref[0:SPAN, K] = dq
    o_ref[0:SPAN, V] = (part_ref[0, :, Q] + dk1).astype(BF)
    o_ref[0:SPAN, G] = (part_ref[0, :, K] + dv1).astype(BF)
    end = SPANS - 1
    _, _, dk0, _, dv0, _ = span_math(
        head_ref[:, Q], head_ref[:, G], in_ref[end, :, K], head_ref[:, K],
        in_ref[end, :, V], head_ref[:, V], None,
    )
    o_ref[BLOCK - SPAN :, V] = (part_ref[1, :, Q] + dk0).astype(BF)
    o_ref[BLOCK - SPAN :, G] = (part_ref[1, :, K] + dv0).astype(BF)
    done = pltpu.make_async_copy(o_ref, done_ref, done_sem.at[0])
    done.start()
    pick_out(at, rank_ref, o_ref[...], out_ref, send_ref, sems)
    done.wait()


def pick_kernel(at, rank_ref, o_ref, *refs):
    pick_out(at, rank_ref, o_ref[...], *refs[-3:])


def unpack_kernel(places, *refs):
    codes, recv_ref, blocks = refs[: len(CHUNKS)], refs[len(CHUNKS)], refs[-len(places) :]
    for hh in range(HPZ):
        for p in range(0, len(places), 2):
            cols = []
            for j, (chunk, at) in enumerate(places[p : p + 2]):
                row = hh * len(CHUNKS[chunk]) + at
                mine = codes[chunk][row : row + 1, :]
                target = lax.shift_right_logical(mine, 5) * (2 * MOST) + (mine & (STRIDE - 1))
                cols.append(row_to_col((target + j * MOST).astype(F32)).astype(I32))
            col = jnp.concatenate(cols, axis=0)
            pick = one_hot(col == iota((2 * TOK, RANGES * 2 * MOST), 1))
            x = recv_ref[hh * RANGES : (hh + 1) * RANGES, p * MOST : (p + 2) * MOST, :]
            got = dot(pick, x.reshape(RANGES * 2 * MOST, ALL)).astype(BF)
            for j in range(2):
                for t in range(4):
                    blocks[p + j][t * TOK : (t + 1) * TOK, hh * WIDTH : (hh + 1) * WIDTH] = got[
                        j * TOK : (j + 1) * TOK, t * WIDTH : (t + 1) * WIDTH
                    ]


def join_kernel(dist, place_ref, *refs):
    blocks, outs, sems = refs[: len(dist)], refs[-5:-1], refs[-1]
    z = place_ref[0]
    copies = []
    for i, d in enumerate(dist):
        cols = pl.ds(pl.multiple_of(((z + d) & (ZN - 1)) * PAIR, PAIR), PAIR)
        for t in range(4):
            copies.append(
                pltpu.make_async_copy(
                    blocks[i].at[t * TOK : (t + 1) * TOK, :],
                    outs[t].at[:, cols],
                    sems.at[i * 4 + t],
                )
            )
    for copy in copies:
        copy.start()
    for copy in copies:
        copy.wait()


def exchange(array, groups):
    return lax.all_to_all(
        array, "seq", split_axis=0, concat_axis=0, axis_index_groups=groups, tiled=True
    )


def shift_owner(value, by):
    pairs = []
    for base in range(0, ZN * PLANE, RANGES):
        pairs += [(base + i, base + i + by) for i in range(RANGES) if 0 <= i + by < RANGES]
    return lax.ppermute(value, "seq", pairs)


def body(queries, keys, values, out_grad, cluster_ids):
    index = lax.axis_index("seq")
    place = jnp.stack([index // PLANE, index % RANGES]).astype(I32)
    hbm = pl.BlockSpec(memory_space=pltpu.HBM)
    anywhere = pl.BlockSpec(memory_space=pl.ANY)
    blocks = call(
        prep_kernel,
        [cluster_ids.T, queries, keys, values, out_grad],
        [out((4 * TOK + TILE, PAIR), BF)] * ZN,
        [pltpu.VMEM((TOK, ZN * PAIR), BF)] * 4 + [pltpu.SemaphoreType.DMA((4,))],
        specs={1: hbm, 2: hbm, 3: hbm, 4: hbm},
        limit=60,
    )
    moved = {0: blocks[0]}
    for d in ORDER:
        if d:
            moved[d] = lax.ppermute(blocks[d], "seq", z_pairs(d))
    codes, arrived, notes = [], [], []
    for i, chunk in enumerate(CHUNKS):
        n = len(chunk)
        rows = n * MOST
        extra = TILE if i == len(CHUNKS) - 1 else 0
        send, code, note = call(
            functools.partial(pack_kernel, i),
            [moved[d] for d in chunk] + notes,
            [
                out((PLANE, rows + extra, ALL), BF),
                out((HPZ * n, TOK), I32),
                out((PLANE, TILE, WIDTH), BF),
            ],
            [
                pltpu.VMEM((n * TOK, ALL), BF),
                pltpu.VMEM((PLANE, rows + extra, ALL), BF),
                pltpu.SemaphoreType.DMA((RANGES,)),
            ],
            flops=PACK_HINT[i],
            out_specs={0: hbm},
        )
        codes.append(code)
        notes.append(note)
        arrived.append(exchange(send, PLANES))
    rows_in, tail, head, rank = call(
        place_kernel,
        [place] + arrived,
        [
            out((SPANS, SPAN, ALL), BF),
            out((SPAN, PAIR), BF),
            out((SPAN, ALL), BF),
            out((1, SLOTS), I32),
        ],
        flops=2 * BLOCK * SLOTS * ALL,
        specs=SMEM,
    )
    tail = shift_owner(tail, 1)
    head = shift_owner(head, -1)
    main, part = call(
        main_kernel,
        [rows_in],
        [out((SPANS, SPAN, ALL), BF), out((2, SPAN, PAIR), F32)],
        flops=14 * SPANS * SPAN * 2 * SPAN * WIDTH,
    )
    sends = []
    for step, chunk in enumerate(RETURNS):
        rows = len(chunk) * MOST
        at = tuple(ORDER.index(d) for d in chunk)
        send_shape = out((PLANE, rows, ALL), BF)
        stage = [pltpu.VMEM((PLANE, rows, ALL), BF), pltpu.SemaphoreType.DMA((PICKS,))]
        if step == 0:
            o, send = call(
                functools.partial(edge_kernel, at),
                [place, rank, rows_in, tail, head, main, part],
                [out((BLOCK, ALL), BF), send_shape],
                [pltpu.VMEM((BLOCK, ALL), BF)] + stage + [pltpu.SemaphoreType.DMA((1,))],
                flops=2 * BLOCK * PLANE * rows * ALL,
                specs=SMEM,
                out_specs={0: hbm, 1: hbm},
            )
        else:
            (send,) = call(
                functools.partial(pick_kernel, at),
                [rank, o],
                [send_shape],
                stage,
                flops=PICK_HINT[step],
                out_specs={0: hbm},
            )
        sends.append(send)
    back = {}
    waits = {}

    def join(dist, outs, flops):
        n = 1 + len(dist)
        return call(
            functools.partial(join_kernel, dist),
            [place] + [back[d] for d in dist] + outs,
            [out((TOK, ZN * PAIR), BF)] * 4,
            [pltpu.SemaphoreType.DMA((4 * len(dist),))],
            flops=flops,
            specs={0: SMEM[0]} | {n + i: hbm for i in range(len(outs))},
            out_specs={i: hbm for i in range(4)},
            aliases={n + i: i for i in range(len(outs))},
        )

    for step, chunk in enumerate(RETURNS):
        got = exchange(sends[step], PLANES)
        places = tuple(
            (i, c.index(d)) for d in chunk for i, c in enumerate(CHUNKS) if d in c
        )
        wait = waits.get(step, [])
        pieces = call(
            functools.partial(unpack_kernel, places),
            codes + [got] + wait,
            [out((4 * TOK, PAIR), BF)] * len(chunk),
            flops=UNPACK_HINT[step],
            specs={len(codes) + 1 + j: anywhere for j in range(len(wait))},
        )
        for d, piece in zip(chunk, pieces):
            back[d] = lax.ppermute(piece, "seq", z_pairs(-d)) if d else piece
        if step == 0:
            waits[1] = [back[d] for d in chunk] + [sends[2]]
        if step == 1:
            joined = join(RETURNS[0] + SOON, [], 10**11)
            waits[2] = list(joined[:1])
    return join(tuple(d for d in back if d not in RETURNS[0] + SOON), list(joined), 0)


def solution(mesh):
    spec = P("seq", "head")
    return jax.shard_map(
        body,
        mesh=mesh,
        in_specs=(spec,) * 5,
        out_specs=(spec,) * 4,
        check_vma=False,
    )
```

```python
import functools
import math

import jax
import jax.numpy as jnp
from jax import lax
from jax.experimental import pallas as pl
from jax.experimental.pallas import tpu as pltpu
from jax.sharding import PartitionSpec as P

WIDTH = 128
SPAN = 256
CLUSTER_GROUP = 16
RANGES = 8
TOK = 128
MOST = 24
ZN = 8
PLANE = 16
HPZ = 2
ALL = 4 * WIDTH
PAIR = HPZ * WIDTH
STRIDE = 32
SLOTS = PLANE * ZN * MOST
BLOCK = 2048
SPANS = BLOCK // SPAN
TILE = 16
PICKS = 2
NONE = 4095
SCALING = 1.0 / math.sqrt(WIDTH)
BF = jnp.bfloat16
F32 = jnp.float32
I32 = jnp.int32

CHUNKS = ((0, 1, 7, 2), (6, 3, 5, 4))
PICK_HINT = (0, 10**9, 10**9)
UNPACK_HINT = (10**9, 10**11, 10**9)
RETURNS = ((3, 5), (4, 2, 6, 7), (0, 1))
ORDER = sum(CHUNKS, ())
SOON = (2, 6)
EARLY = (1, 7)
PACK_HINT = (10**6, 10**11)
PLANES = [[z * PLANE + i for i in range(PLANE)] for z in range(ZN)]


def z_pairs(step):
    return [
        (z * PLANE + i, ((z + step) % ZN) * PLANE + i)
        for z in range(ZN)
        for i in range(PLANE)
    ]


def whole():
    return pl.BlockSpec(memory_space=pltpu.VMEM)


def call(kernel, ins, outs, scratch=(), flops=0, specs=None, out_specs=None, out_spec=None, limit=28, aliases=None):
    size = sum(math.prod(o.shape) * o.dtype.itemsize for o in outs)
    size += sum(math.prod(a.shape) * a.dtype.itemsize for a in ins)
    specs = specs or {}
    return pl.pallas_call(
        kernel,
        out_shape=tuple(
            pltpu.HBM(o.shape, o.dtype) if i in (out_specs or {}) else o
            for i, o in enumerate(outs)
        ),
        in_specs=[specs.get(i) or whole() for i in range(len(ins))],
        out_specs=tuple((out_specs or {}).get(i) or out_spec or whole() for i in range(len(outs))),
        scratch_shapes=list(scratch),
        input_output_aliases=aliases or {},
        cost_estimate=pl.CostEstimate(flops=flops, bytes_accessed=size, transcendentals=0),
        compiler_params=pltpu.CompilerParams(vmem_limit_bytes=limit * 1024 * 1024),
    )(*ins)


SMEM = {0: pl.BlockSpec(memory_space=pltpu.SMEM)}


def out(shape, dtype):
    return jax.ShapeDtypeStruct(shape, dtype)


def iota(shape, dim):
    return lax.broadcasted_iota(I32, shape, dim)


def one_hot(mask):
    return mask.astype(F32).astype(BF)


def row_to_col(row):
    eye = iota((128, 128), 0) == iota((128, 128), 1)
    parts = []
    for i in range(row.shape[1] // 128):
        piece = row[:, i * 128 : (i + 1) * 128]
        parts.append(jnp.sum(jnp.where(eye, piece, 0.0), axis=1, keepdims=True))
    return jnp.concatenate(parts, axis=0)


def dot(a, b, dims=((1,), (0,))):
    return lax.dot_general(a, b, (dims, ((), ())), preferred_element_type=F32)


NT = ((1,), (1,))
TN = ((0,), (0,))


def prep_kernel(dist, ids_ref, *refs):
    arrays, (blocks, sems) = refs[:4], (refs[-1 - len(dist) : -1], refs[-1])
    z = lax.axis_index("seq") // PLANE
    copies = []
    for i, d in enumerate(dist):
        cols = pl.ds(pl.multiple_of(((z + d) & (ZN - 1)) * PAIR, PAIR), PAIR)
        for t in range(4):
            copies.append(
                pltpu.make_async_copy(
                    arrays[t].at[:, cols],
                    blocks[i].at[t * TOK : (t + 1) * TOK, :],
                    sems.at[i * 4 + t],
                )
            )
    for copy in copies:
        copy.start()
    for i, d in enumerate(dist):
        at = ((z + d) & (ZN - 1)) * HPZ
        rows = [ids_ref[pl.ds(at + hh, 1), :] for hh in range(HPZ)]
        tile = jnp.concatenate(rows + [jnp.zeros((TILE - HPZ, TOK), I32)], axis=0)
        blocks[i][4 * TOK :, 0:TOK] = tile.astype(F32).astype(BF)
        blocks[i][4 * TOK :, TOK:] = jnp.zeros((TILE, PAIR - TOK), BF)
    for copy in copies:
        copy.wait()


def leave(stage_ref, out_ref, sems, i, n):
    size = PLANE // n
    part = slice(i * size, (i + 1) * size)
    return pltpu.make_async_copy(stage_ref.at[part], out_ref.at[part], sems.at[i])


def pack_kernel(index, *refs):
    chunk = CHUNKS[index]
    n = len(chunk)
    blocks, notes = refs[:n], refs[n : n + index]
    out_ref, code_ref, note_ref, x_ref, send_ref, sems = refs[-6:]
    last = index == len(CHUNKS) - 1
    rows = n * MOST
    ids = [blocks[i][4 * TOK :, 0:TOK].astype(F32) for i in range(n)]
    ids = jnp.concatenate(
        [ids[i][hh : hh + 1] for hh in range(HPZ) for i in range(n)], axis=0
    ).astype(I32)
    group = lax.shift_right_logical(ids, 4)
    local = ((ids & (CLUSTER_GROUP - 1)) + 1).astype(F32).astype(BF)
    tri = one_hot(iota((TOK, TOK), 0) < iota((TOK, TOK), 1))
    slot = jnp.zeros(ids.shape, F32)
    for b in range(RANGES):
        hot = (group == b).astype(F32)
        slot = slot + hot * dot(hot.astype(BF), tri)
    code = group * STRIDE + slot.astype(I32)
    code_ref[...] = code
    zeros = jnp.zeros((TILE, WIDTH), BF)
    for hh in range(HPZ):
        for i in range(n):
            for t in range(4):
                x_ref[i * TOK : (i + 1) * TOK, t * WIDTH : (t + 1) * WIDTH] = blocks[i][
                    t * TOK : (t + 1) * TOK, hh * WIDTH : (hh + 1) * WIDTH
                ]
        pairs = []
        for p in range(0, n, 2):
            mine = [hh * n + p, hh * n + p + 1]
            position = jnp.concatenate(
                [(code[i : i + 1] & (STRIDE - 1)) + j * MOST for j, i in enumerate(mine)], axis=1
            )
            owner = jnp.concatenate([group[i : i + 1] for i in mine], axis=1)
            value = jnp.concatenate([local[i : i + 1] for i in mine], axis=1)
            pairs.append((position, owner, jnp.broadcast_to(value, (TILE, 2 * TOK))))
        for b in range(RANGES):
            to = hh * RANGES + b
            found = []
            for p, (position, owner, value) in enumerate(pairs):
                target = jnp.where(owner == b, position, -1)
                pick = one_hot(target == iota((2 * MOST, 2 * TOK), 0))
                x = x_ref[p * 2 * TOK : (p + 1) * 2 * TOK, :]
                send_ref[to, p * 2 * MOST : (p + 1) * 2 * MOST, :] = dot(pick, x).astype(BF)
                found.append(dot(value, pick, NT).astype(BF))
            note = jnp.concatenate(found + [zeros[:, n * MOST :]], axis=1)
            note_ref[to] = note
            if last:
                tile = [a[to] for a in notes] + [note]
                tile = tile + [zeros] * (4 - len(tile))
                send_ref[to, rows:, :] = jnp.concatenate(tile, axis=1)
            if b % 2:
                leave(send_ref, out_ref, sems, to // 2, RANGES).start()
    for i in range(RANGES):
        leave(send_ref, out_ref, sems, i, RANGES).wait()


def rank_rows(z, clusters):
    lanes = ZN * MOST

    def source(shape, dim):
        segment = iota(shape, dim) // MOST
        value = jnp.zeros(shape, I32)
        for i, d in enumerate(ORDER):
            value = jnp.where(segment == i, (z - d) & (ZN - 1), value)
        return value

    square = (lanes, lanes)
    from_z, to_z = source(square, 0), source(square, 1)
    same = from_z == to_z
    within = one_hot(same & (iota(square, 0) < iota(square, 1)))
    segment = one_hot(same)
    earlier = one_hot(from_z < to_z)
    hot = jnp.concatenate(
        [(clusters == float(c + 1)).astype(F32) for c in range(CLUSTER_GROUP)], axis=0
    )
    low = hot.astype(BF)
    side = CLUSTER_GROUP * PLANE
    row, col = iota((side, side), 0), iota((side, side), 1)
    row_c, col_c = lax.shift_right_logical(row, 4), lax.shift_right_logical(col, 4)
    before = one_hot((row_c == col_c) & (col < row))
    together = one_hot(row_c == col_c)
    lower = one_hot(col_c < row_c)
    total = dot(low, jnp.ones(square, BF))
    rank = (
        dot(low, within)
        + dot(before, dot(low, segment).astype(BF))
        + dot(together, dot(low, earlier).astype(BF))
        + dot(lower, total.astype(BF))
    )
    rank = jnp.sum((hot * rank).reshape(CLUSTER_GROUP, PLANE, lanes), axis=0)
    rank = jnp.where(clusters > 0.5, rank, float(NONE))
    return rank


def place_kernel(place_ref, *refs):
    n = len(CHUNKS)
    recvs, (sorted_ref, tail_ref, head_ref, rank_ref) = refs[:n], refs[n:]
    clusters = []
    end = len(CHUNKS[-1]) * MOST
    for i, chunk in enumerate(CHUNKS):
        rows = len(chunk) * MOST
        clusters.append(
            jnp.concatenate(
                [
                    recvs[-1][s, end:, i * WIDTH : i * WIDTH + rows].astype(F32)[0:1]
                    for s in range(PLANE)
                ],
                axis=0,
            )
        )
    rank = rank_rows(place_ref[0], jnp.concatenate(clusters, axis=1))
    rank_ref[...] = jnp.concatenate(
        [rank[s : s + 1, :] for s in range(PLANE)], axis=1
    ).astype(I32)
    parts = []
    at = 0
    for chunk, recv_ref in zip(CHUNKS, recvs):
        rows = len(chunk) * MOST
        row = jnp.concatenate([rank[s : s + 1, at : at + rows] for s in range(PLANE)], axis=1)
        parts.append((row.astype(I32), recv_ref[:, 0:rows, :].reshape(PLANE * rows, ALL)))
        at += rows
    step = 2
    for c in range(0, SPANS, step):
        got = jnp.zeros((step * SPAN, ALL), F32)
        for row, x in parts:
            pick = one_hot(row == iota((step * SPAN, row.shape[1]), 0) + c * SPAN)
            got = got + dot(pick, x)
        sorted_ref[c : c + step] = got.astype(BF).reshape(step, SPAN, ALL)
    tail_ref[...] = sorted_ref[SPANS - 1, :, WIDTH : 3 * WIDTH]
    head_ref[...] = sorted_ref[0]


def span_math(q, g, k0, k1, v0, v1, keep):
    s0 = dot(k0, q, NT)
    s1 = dot(k1, q, NT)
    if keep is not None:
        s0 = jnp.where(keep, s0, -1e30)
    peak = jnp.maximum(
        jnp.max(s0, axis=0, keepdims=True), jnp.max(s1, axis=0, keepdims=True)
    )
    factor = SCALING * math.log2(math.e)
    p0 = jnp.exp2((s0 - peak) * factor)
    p1 = jnp.exp2((s1 - peak) * factor)
    inverse = 1.0 / (
        jnp.sum(p0, axis=0, keepdims=True) + jnp.sum(p1, axis=0, keepdims=True)
    )
    w0 = p0 * inverse
    w1 = p1 * inverse
    l0 = w0.astype(BF)
    l1 = w1.astype(BF)
    attended = (dot(v0, l0, TN) + dot(v1, l1, TN)).T.astype(BF)
    e0 = dot(v0, g, NT)
    e1 = dot(v1, g, NT)
    inner = jnp.sum(w0 * e0, axis=0, keepdims=True) + jnp.sum(w1 * e1, axis=0, keepdims=True)
    h0 = (w0 * (e0 - inner) * SCALING).astype(BF)
    h1 = (w1 * (e1 - inner) * SCALING).astype(BF)
    dq = (dot(k0, h0, TN) + dot(k1, h1, TN)).T.astype(BF)
    return attended, dq, dot(h0, q), dot(h1, q), dot(l0, g), dot(l1, g)


Q, K, V, G = (slice(t * WIDTH, (t + 1) * WIDTH) for t in range(4))


def main_kernel(in_ref, o_ref, part_ref):
    held = (jnp.zeros((SPAN, WIDTH), F32),) * 2
    for c in range(1, SPANS):
        att, dq, dk0, dk1, dv0, dv1 = span_math(
            in_ref[c, :, Q], in_ref[c, :, G], in_ref[c - 1, :, K], in_ref[c, :, K],
            in_ref[c - 1, :, V], in_ref[c, :, V], None,
        )
        o_ref[c, :, Q] = att
        o_ref[c, :, K] = dq
        dk, dv = held[0] + dk0, held[1] + dv0
        if c == 1:
            part_ref[0, :, Q] = dk
            part_ref[0, :, K] = dv
        o_ref[c - 1, :, V] = dk.astype(BF)
        o_ref[c - 1, :, G] = dv.astype(BF)
        held = (dk1, dv1)
    part_ref[1, :, Q] = held[0]
    part_ref[1, :, K] = held[1]
    o_ref[0, :, 0 : 2 * WIDTH] = jnp.zeros((SPAN, 2 * WIDTH), BF)
    o_ref[SPANS - 1, :, 2 * WIDTH :] = jnp.zeros((SPAN, 2 * WIDTH), BF)


def pick_out(at, rank_ref, o, out_ref, send_ref, sems):
    col = row_to_col(rank_ref[...].astype(F32)).astype(I32)
    rows = send_ref.shape[1]
    step = PLANE // PICKS
    for p in range(PICKS):
        span = range(p * step, (p + 1) * step)
        part = jnp.concatenate(
            [
                col[i * ZN * MOST + j * MOST : i * ZN * MOST + (j + 1) * MOST, :]
                for i in span
                for j in at
            ],
            axis=0,
        )
        pick = one_hot(part == iota((step * rows, BLOCK), 1))
        send_ref[p * step : (p + 1) * step] = dot(pick, o).astype(BF).reshape(step, rows, ALL)
        leave(send_ref, out_ref, sems, p, PICKS).start()
    for p in range(PICKS):
        leave(send_ref, out_ref, sems, p, PICKS).wait()


def edge_kernel(
    at, place_ref, rank_ref, in_ref, tail_ref, head_ref, main_ref, part_ref,
    done_ref, out_ref, o_ref, send_ref, sems, done_sem,
):
    o_ref[SPAN:BLOCK, :] = main_ref[1:].reshape(BLOCK - SPAN, ALL)
    keep = jnp.broadcast_to(place_ref[1], (SPAN, SPAN)) > 0
    att, dq, _, dk1, _, dv1 = span_math(
        in_ref[0, :, Q], in_ref[0, :, G], tail_ref[:, Q], in_ref[0, :, K],
        tail_ref[:, K], in_ref[0, :, V], keep,
    )
    o_ref[0:SPAN, Q] = att
    o_ref[0:SPAN, K] = dq
    o_ref[0:SPAN, V] = (part_ref[0, :, Q] + dk1).astype(BF)
    o_ref[0:SPAN, G] = (part_ref[0, :, K] + dv1).astype(BF)
    end = SPANS - 1
    _, _, dk0, _, dv0, _ = span_math(
        head_ref[:, Q], head_ref[:, G], in_ref[end, :, K], head_ref[:, K],
        in_ref[end, :, V], head_ref[:, V], None,
    )
    o_ref[BLOCK - SPAN :, V] = (part_ref[1, :, Q] + dk0).astype(BF)
    o_ref[BLOCK - SPAN :, G] = (part_ref[1, :, K] + dv0).astype(BF)
    done = pltpu.make_async_copy(o_ref, done_ref, done_sem.at[0])
    done.start()
    pick_out(at, rank_ref, o_ref[...], out_ref, send_ref, sems)
    done.wait()


def pick_kernel(at, rank_ref, o_ref, *refs):
    pick_out(at, rank_ref, o_ref[...], *refs[-3:])


def unpack_kernel(places, *refs):
    codes, recv_ref, blocks = refs[: len(CHUNKS)], refs[len(CHUNKS)], refs[-len(places) :]
    for hh in range(HPZ):
        for p in range(0, len(places), 2):
            cols = []
            for j, (chunk, at) in enumerate(places[p : p + 2]):
                row = hh * len(CHUNKS[chunk]) + at
                mine = codes[chunk][row : row + 1, :]
                target = lax.shift_right_logical(mine, 5) * (2 * MOST) + (mine & (STRIDE - 1))
                cols.append(row_to_col((target + j * MOST).astype(F32)).astype(I32))
            col = jnp.concatenate(cols, axis=0)
            pick = one_hot(col == iota((2 * TOK, RANGES * 2 * MOST), 1))
            x = recv_ref[hh * RANGES : (hh + 1) * RANGES, p * MOST : (p + 2) * MOST, :]
            got = dot(pick, x.reshape(RANGES * 2 * MOST, ALL)).astype(BF)
            for j in range(2):
                for t in range(4):
                    blocks[p + j][t * TOK : (t + 1) * TOK, hh * WIDTH : (hh + 1) * WIDTH] = got[
                        j * TOK : (j + 1) * TOK, t * WIDTH : (t + 1) * WIDTH
                    ]


def join_kernel(dist, place_ref, *refs):
    blocks, outs, sems = refs[: len(dist)], refs[-5:-1], refs[-1]
    z = place_ref[0]
    copies = []
    for i, d in enumerate(dist):
        cols = pl.ds(pl.multiple_of(((z + d) & (ZN - 1)) * PAIR, PAIR), PAIR)
        for t in range(4):
            copies.append(
                pltpu.make_async_copy(
                    blocks[i].at[t * TOK : (t + 1) * TOK, :],
                    outs[t].at[:, cols],
                    sems.at[i * 4 + t],
                )
            )
    for copy in copies:
        copy.start()
    for copy in copies:
        copy.wait()


def exchange(array, groups):
    return lax.all_to_all(
        array, "seq", split_axis=0, concat_axis=0, axis_index_groups=groups, tiled=True
    )


def shift_owner(value, by):
    pairs = []
    for base in range(0, ZN * PLANE, RANGES):
        pairs += [(base + i, base + i + by) for i in range(RANGES) if 0 <= i + by < RANGES]
    return lax.ppermute(value, "seq", pairs)


def body(queries, keys, values, out_grad, cluster_ids):
    index = lax.axis_index("seq")
    place = jnp.stack([index // PLANE, index % RANGES]).astype(I32)
    hbm = pl.BlockSpec(memory_space=pltpu.HBM)
    anywhere = pl.BlockSpec(memory_space=pl.ANY)
    blocks = {}
    for dist in EARLY, tuple(d for d in ORDER if d not in EARLY):
        earlier = [blocks[EARLY[0]]] if blocks else []
        made = call(
            functools.partial(prep_kernel, dist),
            [cluster_ids.T, queries, keys, values, out_grad] + earlier,
            [out((4 * TOK + TILE, PAIR), BF)] * len(dist),
            [pltpu.SemaphoreType.DMA((4 * len(dist),))],
            specs={1: hbm, 2: hbm, 3: hbm, 4: hbm, 5: anywhere},
            limit=60,
        )
        blocks.update(zip(dist, made))
    moved = {0: blocks[0]}
    for d in ORDER:
        if d:
            moved[d] = lax.ppermute(blocks[d], "seq", z_pairs(d))
    codes, arrived, notes = [], [], []
    for i, chunk in enumerate(CHUNKS):
        n = len(chunk)
        rows = n * MOST
        extra = TILE if i == len(CHUNKS) - 1 else 0
        send, code, note = call(
            functools.partial(pack_kernel, i),
            [moved[d] for d in chunk] + notes,
            [
                out((PLANE, rows + extra, ALL), BF),
                out((HPZ * n, TOK), I32),
                out((PLANE, TILE, WIDTH), BF),
            ],
            [
                pltpu.VMEM((n * TOK, ALL), BF),
                pltpu.VMEM((PLANE, rows + extra, ALL), BF),
                pltpu.SemaphoreType.DMA((RANGES,)),
            ],
            flops=PACK_HINT[i],
            out_specs={0: hbm},
        )
        codes.append(code)
        notes.append(note)
        arrived.append(exchange(send, PLANES))
    rows_in, tail, head, rank = call(
        place_kernel,
        [place] + arrived,
        [
            out((SPANS, SPAN, ALL), BF),
            out((SPAN, PAIR), BF),
            out((SPAN, ALL), BF),
            out((1, SLOTS), I32),
        ],
        flops=2 * BLOCK * SLOTS * ALL,
        specs=SMEM,
    )
    tail = shift_owner(tail, 1)
    head = shift_owner(head, -1)
    main, part = call(
        main_kernel,
        [rows_in],
        [out((SPANS, SPAN, ALL), BF), out((2, SPAN, PAIR), F32)],
        flops=14 * SPANS * SPAN * 2 * SPAN * WIDTH,
    )
    sends = []
    for step, chunk in enumerate(RETURNS):
        rows = len(chunk) * MOST
        at = tuple(ORDER.index(d) for d in chunk)
        send_shape = out((PLANE, rows, ALL), BF)
        stage = [pltpu.VMEM((PLANE, rows, ALL), BF), pltpu.SemaphoreType.DMA((PICKS,))]
        if step == 0:
            o, send = call(
                functools.partial(edge_kernel, at),
                [place, rank, rows_in, tail, head, main, part],
                [out((BLOCK, ALL), BF), send_shape],
                [pltpu.VMEM((BLOCK, ALL), BF)] + stage + [pltpu.SemaphoreType.DMA((1,))],
                flops=2 * BLOCK * PLANE * rows * ALL,
                specs=SMEM,
                out_specs={0: hbm, 1: hbm},
            )
        else:
            (send,) = call(
                functools.partial(pick_kernel, at),
                [rank, o],
                [send_shape],
                stage,
                flops=PICK_HINT[step],
                out_specs={0: hbm},
            )
        sends.append(send)
    back = {}
    waits = {}

    def join(dist, outs, flops):
        n = 1 + len(dist)
        return call(
            functools.partial(join_kernel, dist),
            [place] + [back[d] for d in dist] + outs,
            [out((TOK, ZN * PAIR), BF)] * 4,
            [pltpu.SemaphoreType.DMA((4 * len(dist),))],
            flops=flops,
            specs={0: SMEM[0]} | {n + i: hbm for i in range(len(outs))},
            out_specs={i: hbm for i in range(4)},
            aliases={n + i: i for i in range(len(outs))},
        )

    for step, chunk in enumerate(RETURNS):
        got = exchange(sends[step], PLANES)
        places = tuple(
            (i, c.index(d)) for d in chunk for i, c in enumerate(CHUNKS) if d in c
        )
        wait = waits.get(step, [])
        pieces = call(
            functools.partial(unpack_kernel, places),
            codes + [got] + wait,
            [out((4 * TOK, PAIR), BF)] * len(chunk),
            flops=UNPACK_HINT[step],
            specs={len(codes) + 1 + j: anywhere for j in range(len(wait))},
        )
        for d, piece in zip(chunk, pieces):
            back[d] = lax.ppermute(piece, "seq", z_pairs(-d)) if d else piece
        if step == 0:
            waits[1] = [back[d] for d in chunk] + [sends[2]]
        if step == 1:
            joined = join(RETURNS[0] + SOON, [], 10**11)
            waits[2] = list(joined[:1])
    return join(tuple(d for d in back if d not in RETURNS[0] + SOON), list(joined), 0)


def solution(mesh):
    spec = P("seq", "head")
    return jax.shard_map(
        body,
        mesh=mesh,
        in_specs=(spec,) * 5,
        out_specs=(spec,) * 4,
        check_vma=False,
    )
```
